32 devices in a mesh: seq: 8 (over z, y), tp: 4 (over x, core).
Axes of the slice: x: 2, y: 2, z: 4, core: 2. Of those that a mesh axis runs over, the one named last changes fastest.
Arguments:
- head_input: bfloat16 [4096, 5120], P('seq', 'tp'), may hold values from -5 to 5
- gate_input: bfloat16 [4096, 5120], P('seq', 'tp'), may hold values from -1000 to 1000
- write_vecs: bfloat16 [4096, 128], P('seq'), may hold values from -2.09375 to 2.09375
- read_vecs: bfloat16 [4096, 128], P('seq'), may hold values from -2.09375 to 2.09375
- step_raw: bfloat16 [80, 4096], P('tp', 'seq'), may hold values from -4 to 12
- segment_ids: int32 [4096], P('seq'), may hold values from 0 to 3, never falling along the last dimension, each value on 1 to 2048 neighbouring positions
- decay_log: float32 [80], P('tp'), may hold values from -8 to 0
- step_bias: float32 [80], P('tp'), may hold values from -8 to -1
- skip_gain: float32 [80], P('tp'), may hold values from 0.5 to 1.5
- norm_gain: float32 [5120], P('tp'), may hold values from 0.1 to 1.9
- out_weight: bfloat16 [5120, 2560], P('tp'), may hold values from -0.078125 to 0.078125
Outputs:
- mixed_out: bfloat16 [2560, 4096], P('tp', 'seq')
The draws below stay inside these ranges and needn't reach their ends.
Inputs may be any that keep to these rules, and one draw needn't show every extreme that they name: `segment_ids`: never falls along the tokens; each id covers 1 to 2048 consecutive tokens, and one covers exactly 2048.
All inputs are finite; a program needn't handle non-finite values.
Results may differ from the reference program's by a relative error of at most 0.0054.
Values may be sent and summed in bfloat16 or wider, within the bound.
No kernel may reach another device: no remote copies, remote signals or barrier semaphores. Data moves between devices by JAX's collectives and lax.ppermute only.
A program may use at most 128 MiB of HBM per device.

```python
import math
import jax
import jax.numpy as jnp
import numpy as np
from jax import lax

D_MODEL = 2560
HEADS = 80
HEAD_DIM = 64
STATE = 128
GROUP = 256
TOK_DEV = 512
TOKENS = 4096
SEGMENT_TOKEN_CAP = 2048
SEGS = 4


def spike_rows(key):
    return jax.random.randint(jax.random.fold_in(key, 31), (3,), 0, TOKENS)


def head_log_rates(key):
    kind_draw = jax.random.uniform(jax.random.fold_in(key, 51), (HEADS,), jnp.float32)
    pick_draw = jax.random.uniform(jax.random.fold_in(key, 52), (HEADS,), jnp.float32)
    fast_share = 0.4
    middle_share = 0.6
    span_log = jnp.log(jnp.float32(SEGMENT_TOKEN_CAP))
    fast_log = jnp.log(1.0 / 50.0) + pick_draw * (jnp.log(1.0 / 30.0) - jnp.log(1.0 / 50.0))
    middle_log = -span_log + pick_draw * (jnp.log(1.0 / 40.0) + span_log)
    slow_log = jnp.log(0.3) - span_log + pick_draw * -jnp.log(0.3)
    return jnp.where(kind_draw < fast_share, fast_log, jnp.where(kind_draw < middle_share, middle_log, slow_log))


def draw_decay_log(key, part):
    jitter = jax.random.uniform(jax.random.fold_in(key, 41), (HEADS,), jnp.float32, -0.15, 0.15)
    return (0.5 * head_log_rates(key) + jitter).astype(jnp.float32)


def draw_step_bias(key, part):
    jitter = jax.random.uniform(jax.random.fold_in(key, 43), (HEADS,), jnp.float32, -0.15, 0.15)
    target = jnp.exp(0.5 * head_log_rates(key) + jitter)
    return jnp.log(jnp.expm1(target)).astype(jnp.float32)


def draw_head_input(key, part):
    width = HEADS * HEAD_DIM
    value_entries = jnp.clip(jax.random.normal(jax.random.fold_in(key, 1), (TOKENS, width), jnp.float32), -5.0, 5.0)
    row_position_index = jnp.arange(TOKENS)
    spiking_flag = jnp.any(row_position_index[:, None] == spike_rows(key)[None, :], axis=1)
    row_scale = jnp.where(spiking_flag, 0.04, 1.0)
    return (value_entries * row_scale[:, None]).astype(jnp.bfloat16)


def draw_step_raw(key, part):
    random_noise = jnp.clip(0.5 * jax.random.normal(jax.random.fold_in(key, 2), (HEADS, TOKENS), jnp.float32), -2.5, 2.5)
    segment_offsets = jax.random.uniform(jax.random.fold_in(key, 3), (TOKENS // TOK_DEV,), jnp.float32, -0.7, 0.7)
    segment_offsets = jnp.repeat(segment_offsets, TOK_DEV)
    column_index = jnp.arange(TOKENS)
    spiking_flag = jnp.any(column_index[:, None] == spike_rows(key)[None, :], axis=1)
    spike_value = jnp.log(0.35 * jnp.float32(SEGMENT_TOKEN_CAP))
    value_entries = jnp.where(spiking_flag[None, :], spike_value, random_noise + segment_offsets[None, :])
    return value_entries.astype(jnp.bfloat16)


def draw_gate_input(key, part):
    width = HEADS * HEAD_DIM
    col_pos = (jnp.arange(width).astype(jnp.float32) + 0.5) / width
    row_scale = jnp.exp(jax.random.uniform(jax.random.fold_in(key, 61), (TOKENS,), jnp.float32, 0.0, jnp.log(10.0)))
    base = jnp.clip(jax.random.normal(jax.random.fold_in(key, 62), (TOKENS, width), jnp.float32), -5.0, 5.0)
    col_scale = 10.0 ** col_pos
    return (base * col_scale[None, :] * row_scale[:, None]).astype(jnp.bfloat16)


def levels(stream_key, extent, shards, smallest, top_value):
    loudness, own = 1.0, jax.random.fold_in(stream_key, 6)
    for axis_at, parts in shards:
        heights = jnp.exp(jax.random.uniform(jax.random.fold_in(own, axis_at), (parts,), jnp.float32, smallest / len(shards), top_value / len(shards)))
        loudness = loudness * jnp.repeat(heights, extent[axis_at] // parts).reshape([-1 if axis == axis_at else 1 for axis in range(len(extent))])
    return loudness


def profile(amount, total, most, skew):
    loads = [(1 << 20) // math.isqrt(standing ** skew) + 1 for standing in range(2, amount + 1)]
    spare, holding = total - most - (amount - 1), [1] * (amount - 1)
    while spare > 0:
        candidates = [i for i in range(amount - 1) if holding[i] < most]
        whole, budget = sum([loads[i] for i in candidates]), spare
        for i in candidates:
            more = min(most - holding[i], max(1, budget * loads[i] // whole), spare)
            holding[i] = holding[i] + more
            spare = spare - more
    return np.array([most] + holding)


def ragged(stream_key, amount, total, most, skew):
    if amount == 2:
        one = jax.random.randint(stream_key, (), max(1, total - most), min(most, total - 1) + 1)
        return jnp.stack([one, total - one])
    tallies = jnp.asarray(profile(amount, total, most, skew), jnp.int32)
    pairs = (amount - 1) // 2
    giver, receiver = tallies[1:1 + 2 * pairs:2], tallies[2:2 + 2 * pairs:2]
    margin = jnp.minimum(giver - 1, most - receiver)
    shifted = jax.random.randint(jax.random.fold_in(stream_key, 1), (pairs,), 0, 1 << 20) % (margin + 1)
    tallies = tallies.at[1:1 + 2 * pairs:2].set(giver - shifted).at[2:2 + 2 * pairs:2].set(receiver + shifted)
    return tallies[jax.random.permutation(jax.random.fold_in(stream_key, 2), amount)]


def bell_draw(key, extent, scale, reach, cuts=(), dtype=jnp.bfloat16):
    drawn = scale * jax.random.normal(key, extent, jnp.float32)
    if cuts:
        drawn = drawn * levels(key, extent, cuts, -0.22, 0.18)
    return jnp.clip(drawn, -reach, reach).astype(dtype)


def setup_inputs(seed: int = 0) -> dict:
    key_of = jax.random.split(jax.random.key(seed), 12)
    return {
        "head_input": draw_head_input(jax.random.fold_in(key_of[11], 71), 0),
        "gate_input": draw_gate_input(jax.random.fold_in(key_of[11], 71), 0),
        "write_vecs": bell_draw(key_of[2], (TOKENS, STATE), 0.35, 2.09375, ((0, 8),)),
        "read_vecs": bell_draw(key_of[3], (TOKENS, STATE), 0.35, 2.09375, ((0, 8),)),
        "step_raw": draw_step_raw(jax.random.fold_in(key_of[11], 71), 0),
        "segment_ids": jnp.searchsorted(jnp.cumsum(ragged(key_of[5], SEGS, TOKENS, SEGMENT_TOKEN_CAP, 2)), jnp.arange(TOKENS), side="right").astype(jnp.int32),
        "decay_log": draw_decay_log(jax.random.fold_in(key_of[11], 71), 0),
        "step_bias": draw_step_bias(jax.random.fold_in(key_of[11], 71), 0),
        "skip_gain": jnp.clip(0.5 + 1.0 * jax.random.uniform(key_of[8], (HEADS,), jnp.float32) ** levels(key_of[8], (HEADS,), ((0, 4),), -0.2, 0.2), 0.5, 1.5),
        "norm_gain": jnp.clip(1.0 + 0.18 * jax.random.normal(key_of[9], (HEADS * HEAD_DIM,), jnp.float32), 0.1, 1.9),
        "out_weight": bell_draw(key_of[10], (HEADS * HEAD_DIM, D_MODEL), (HEADS * HEAD_DIM) ** -0.5, 0.078125, ((0, 4),)),
    }


def reference(head_input, gate_input, write_vecs, read_vecs, step_raw, segment_ids, decay_log, step_bias, skip_gain, norm_gain, out_weight):
    heads_all = decay_log.shape[0]
    width = head_input.shape[1]
    head_width = width // heads_all
    num_blocks = TOKENS // GROUP
    step_size = jax.nn.softplus(step_raw.astype(jnp.float32) + step_bias[:, None])
    decay_rate = -jnp.exp(decay_log)[:, None] * step_size
    inputs_b = head_input.reshape(num_blocks, GROUP, heads_all, head_width)
    write_b = write_vecs.reshape(num_blocks, GROUP, STATE)
    read_b = read_vecs.reshape(num_blocks, GROUP, STATE)
    steps_b = step_size.reshape(heads_all, num_blocks, GROUP).transpose(1, 0, 2)
    rates_b = decay_rate.reshape(heads_all, num_blocks, GROUP).transpose(1, 0, 2)
    seg_b = segment_ids.reshape(num_blocks, GROUP).astype(jnp.int32)
    before = jnp.concatenate([jnp.full((1,), -1, jnp.int32), seg_b[:-1, -1].astype(jnp.int32)])
    row_iota = lax.broadcasted_iota(jnp.int32, (GROUP, GROUP), 0)
    col_iota = lax.broadcasted_iota(jnp.int32, (GROUP, GROUP), 1)
    causal = row_iota >= col_iota

    def advance(carry_state, inputs):
        x_block, write_block, read_block, step_block, rate_block, seg_block, prev_id = inputs
        cum_block = jnp.cumsum(rate_block, axis=1)
        same_seg = (seg_block[:, None] == seg_block[None, :]) & causal
        scores = jnp.dot(read_block, write_block.T, preferred_element_type=jnp.float32)
        gap_rate = jnp.where(same_seg[None], cum_block[:, :, None] - cum_block[:, None, :], 0.0)
        mix_weights = jnp.where(same_seg[None], scores[None] * jnp.exp(gap_rate) * step_block[:, None, :], 0.0).astype(jnp.bfloat16)
        inner_out = jnp.einsum('htu,uhp->thp', mix_weights.astype(jnp.float32), x_block.astype(jnp.float32))
        entry_mask = (seg_block == prev_id).astype(jnp.float32)
        carried = jnp.einsum('tn,hpn->thp', read_block.astype(jnp.float32), carry_state, precision=lax.Precision.HIGHEST)
        carried = carried * jnp.exp(cum_block).T[:, :, None] * entry_mask[:, None, None]
        last_id = seg_block[-1]
        tail_scale = jnp.where((seg_block == last_id)[None, :], jnp.exp(cum_block[:, -1:] - cum_block) * step_block, 0.0)
        written = (write_block[None].astype(jnp.float32) * tail_scale[:, :, None]).astype(jnp.bfloat16)
        block_state = jnp.einsum('uhp,hun->hpn', x_block.astype(jnp.float32), written.astype(jnp.float32))
        keep_rate = jnp.exp(cum_block[:, -1]) * (last_id == prev_id).astype(jnp.float32)
        new_state = keep_rate[:, None, None] * carry_state + block_state
        ssm_out = inner_out + carried + skip_gain[None, :, None] * x_block.astype(jnp.float32)
        return (new_state, ssm_out)
    start_state = jnp.zeros((heads_all, head_width, STATE), jnp.float32)
    _, outputs = lax.scan(advance, start_state, (inputs_b, write_b, read_b, steps_b, rates_b, seg_b, before))
    ssm_all = outputs.reshape(TOKENS, width)
    gated = ssm_all * jax.nn.silu(gate_input.astype(jnp.float32))
    inv_rms = lax.rsqrt(lax.optimization_barrier(jnp.mean(gated * gated, axis=1)) + 1e-05)
    normed = (gated * inv_rms[:, None] * norm_gain[None, :]).astype(jnp.bfloat16)
    mixed = lax.dot_general(out_weight, normed, (((0,), (1,)), ((), ())), preferred_element_type=jnp.float32)
    return mixed.astype(jnp.bfloat16)
```

```python
import functools

import jax
import jax.numpy as jnp
from jax import lax
from jax.experimental import pallas as pl
from jax.experimental.pallas import tpu as pltpu
from jax.sharding import PartitionSpec as P

GROUP = 256
LANES = 128
EPS = 1e-05
LOG2E = 1.4426950408889634
SEG_LANE = 32
VMEM = 48 * 1024 * 1024
F32 = jnp.float32
BF16 = jnp.bfloat16


def dot(a, b, dims=((1,), (0,))):
    return lax.dot_general(a, b, (dims, ((), ())), preferred_element_type=F32)


def lane_iota(rows):
    return lax.broadcasted_iota(jnp.int32, (rows, LANES), 1)


def spread(cols, first, width):
    rows = cols.shape[0]
    per = LANES // width
    lane = lane_iota(rows)
    out = jnp.broadcast_to(cols[:, first : first + 1], (rows, LANES))
    for k in range(1, per):
        nxt = jnp.broadcast_to(cols[:, first + k : first + k + 1], (rows, LANES))
        out = jnp.where(lane < k * width, out, nxt)
    return out


def call(body, n_in, grid, in_specs, out_specs, out_shape, scratch=(), flops=0, nbytes=0):
    del n_in
    return pl.pallas_call(
        body,
        grid_spec=pltpu.PrefetchScalarGridSpec(
            num_scalar_prefetch=1,
            grid=grid,
            in_specs=in_specs,
            out_specs=out_specs,
            scratch_shapes=list(scratch),
        ),
        out_shape=out_shape,
        compiler_params=pltpu.CompilerParams(vmem_limit_bytes=VMEM),
        cost_estimate=pl.CostEstimate(flops=flops, bytes_accessed=nbytes, transcendentals=0),
    )


def whole(shape):
    return pl.BlockSpec(shape, lambda i, sc: (0,) * len(shape))


def prepare(heads, width, sc, raw, seg, decay_log, bias, skip, x, write):
    toks = raw.shape[1]
    half_w = x.shape[1] // 2
    half_h = heads // 2
    blocks = toks // GROUP

    def body(
        sc_ref, raw_ref, seg_ref, dl_ref, sb_ref, sk_ref, x_ref, wr_ref,
        send_ref, ccol_ref, arow_ref, tail_ref, meta_ref, pad, rows,
    ):
        pad[...] = jnp.zeros_like(pad)
        pad[0:heads] = raw_ref[...].astype(F32)
        pad[SEG_LANE : SEG_LANE + 1] = seg_ref[...].astype(F32)
        rows[...] = jnp.zeros_like(rows)
        rows[0:1, 0:heads] = dl_ref[...]
        rows[1:2, 0:heads] = sb_ref[...]
        rows[2:3, 0:heads] = sk_ref[...]
        cols = jnp.transpose(pad[...])
        lane = lane_iota(toks)
        z = cols + rows[1:2]
        step = jnp.maximum(z, 0.0) + jnp.log1p(jnp.exp(-jnp.abs(z)))
        rate = -jnp.exp(rows[0:1]) * step
        tri = (
            lax.broadcasted_iota(jnp.int32, (GROUP, GROUP), 0)
            >= lax.broadcasted_iota(jnp.int32, (GROUP, GROUP), 1)
        ).astype(BF16)
        cum, full = [], []
        base = jnp.zeros((1, LANES), F32)
        for b in range(blocks):
            r = rate[b * GROUP : (b + 1) * GROUP]
            r1 = r.astype(BF16)
            d1 = r - r1.astype(F32)
            r2 = d1.astype(BF16)
            r3 = (d1 - r2.astype(F32)).astype(BF16)
            c = dot(tri, r1) + (dot(tri, r2) + dot(tri, r3))
            cum.append(c)
            full.append(c + base)
            base = base + c[GROUP - 1 : GROUP]
        total = base
        seg_col = cols[:, SEG_LANE : SEG_LANE + 1]
        last = cols[toks - 1 : toks, SEG_LANE : SEG_LANE + 1]
        cum_all = jnp.concatenate(cum, axis=0)
        tail = jnp.exp(total - jnp.concatenate(full, axis=0)) * step
        tail = jnp.where(seg_col == last, tail, 0.0)
        last0 = cols[GROUP - 1 : GROUP, SEG_LANE : SEG_LANE + 1]
        tail0 = jnp.exp(cum[0][GROUP - 1 : GROUP] - cum[0]) * step[0:GROUP]
        tail0 = jnp.where(seg_col[0:GROUP] == last0, tail0, 0.0)
        cc = cum_all * LOG2E
        a = jnp.where(lane == SEG_LANE, cols, cc - jnp.log(step) * LOG2E)
        arow_ref[...] = jnp.transpose(a)[0:64]
        seg_b = jnp.broadcast_to(seg_col, (toks, LANES))
        ccol_ref[0] = jnp.where(lane == SEG_LANE, seg_b, cc)
        ccol_ref[1] = jnp.where(lane == SEG_LANE, seg_b, pltpu.roll(cc, LANES - half_h, 1))
        tail_r = pltpu.roll(tail, LANES - half_h, 1)
        tail_ref[0, 0:toks] = tail
        tail_ref[1, 0:toks] = tail_r
        tail_ref[0, toks : toks + GROUP] = tail0
        tail_ref[1, toks : toks + GROUP] = pltpu.roll(tail0, LANES - half_h, 1)
        keep = jnp.exp(total)
        per = LANES // width
        for j in range(2):
            for i in range(half_w // LANES):
                at = j * half_h + i * per
                tile = slice(i * LANES, (i + 1) * LANES)
                meta_ref[j, 0:1, tile] = spread(keep, at, width)
                meta_ref[j, 1:2, tile] = jnp.broadcast_to(last, (1, LANES))
                meta_ref[j, 2:3, tile] = spread(rows[2:3], at, width)
                meta_ref[j, 3:8, tile] = jnp.zeros((5, LANES), F32)
        mine = jnp.where(sc_ref[1] == 0, tail, tail_r)
        parts = []
        for i in range(half_w // LANES):
            xt = x_ref[:, i * LANES : (i + 1) * LANES].astype(F32)
            parts.append((xt * spread(mine, i * per, width)).astype(BF16))
        xs = jnp.concatenate(parts, axis=1)
        send_ref[...] = dot(wr_ref[...], xs, ((0,), (0,))).astype(BF16)

    state = write.shape[1]
    return call(
        body, 7, (1,),
        [
            whole(raw.shape), whole(seg.shape), whole(decay_log.shape), whole(bias.shape), whole(skip.shape),
            pl.BlockSpec((toks, half_w), lambda i, sc: (0, sc[1])),
            whole(write.shape),
        ],
        [
            whole((state, half_w)), whole((2, toks, LANES)), whole((64, toks)),
            whole((2, toks + GROUP, LANES)), whole((2, 8, half_w)),
        ],
        [
            jax.ShapeDtypeStruct((state, half_w), BF16),
            jax.ShapeDtypeStruct((2, toks, LANES), F32),
            jax.ShapeDtypeStruct((64, toks), F32),
            jax.ShapeDtypeStruct((2, toks + GROUP, LANES), F32),
            jax.ShapeDtypeStruct((2, 8, half_w), F32),
        ],
        [pltpu.VMEM((LANES, toks), F32), pltpu.VMEM((8, LANES), F32)],
        flops=2 * toks * state * half_w, nbytes=4_000_000,
    )(sc, raw, seg, decay_log, bias, skip, x, write)


def kept_state(width, sc, tail, x, write):
    toks, state = write.shape
    half_w = x.shape[1] // 2
    per = LANES // width

    def body(sc_ref, tail_ref, x_ref, wr_ref, out_ref):
        mine = tail_ref[0]
        parts = []
        for i in range(half_w // LANES):
            xt = x_ref[:, i * LANES : (i + 1) * LANES].astype(F32)
            parts.append((xt * spread(mine, i * per, width)).astype(BF16))
        out_ref[...] = dot(wr_ref[...], jnp.concatenate(parts, axis=1), ((0,), (0,)))

    return call(
        body, 3, (1,),
        [
            pl.BlockSpec((1, toks, LANES), lambda i, sc: (sc[0], 0, 0)),
            pl.BlockSpec((toks, half_w), lambda i, sc: (0, sc[0])),
            whole(write.shape),
        ],
        whole((state, half_w)),
        jax.ShapeDtypeStruct((state, half_w), F32),
        flops=2 * toks * state * half_w, nbytes=2_000_000,
    )(sc, tail, x, write)


def local_part(which, heads, width, sc, x, gate, read, write, ccol, arow, tail, meta):
    toks, state = write.shape
    half_w = x.shape[1] // 2
    half_h = heads // 2
    per = LANES // width
    tiles = half_w // LANES
    blocks = toks // GROUP
    sub = GROUP // 2

    def body(
        sc_ref, x_ref, gate_ref, rd_ref, wr_ref, ccol_ref, arow_ref, tail0_ref, meta_ref,
        a_ref, b_ref, scores,
    ):
        i = pl.program_id(0)
        seg_col = ccol_ref[0, :, SEG_LANE : SEG_LANE + 1]

        @pl.when(i == 0)
        def _():
            for b in range(blocks):
                rows = slice(b * GROUP, (b + 1) * GROUP)
                s = dot(rd_ref[rows], wr_ref[rows], ((1,), (1,)))
                causal = lax.broadcasted_iota(jnp.int32, (GROUP, GROUP), 0) >= lax.broadcasted_iota(
                    jnp.int32, (GROUP, GROUP), 1
                )
                same = seg_col[rows] == arow_ref[SEG_LANE : SEG_LANE + 1, rows]
                scores[b] = jnp.where(causal & same, s, 0.0)

        turn = lax.rem(LANES - per * i, LANES)
        cr = pltpu.roll(ccol_ref[0], turn, 1)
        tr = pltpu.roll(tail0_ref[0], turn, 1)
        skip = meta_ref[0, 2:3, :]
        lane = lane_iota(GROUP)
        head0 = sc_ref[which] * half_h + per * i
        carry = None
        start = jnp.ones((1, LANES), F32)
        for b in range(blocks):
            rows = slice(b * GROUP, (b + 1) * GROUP)
            xb = x_ref[rows]
            inner = None
            dec_log = None
            for k in range(per):
                cb = jnp.broadcast_to(cr[rows, k : k + 1], (GROUP, LANES))
                ar = arow_ref[pl.ds(head0 + k, 1), rows]
                sb = scores[b]
                lo = jnp.exp2(jnp.minimum(cb - ar[:, 0:sub], 60.0)) * sb[:, 0:sub]
                hi = jnp.exp2(jnp.minimum(cb[sub:] - ar[:, sub:], 60.0)) * sb[sub:, sub:]
                lo = lo.astype(BF16)
                top = dot(lo[0:sub], xb[0:sub])
                bottom = dot(jnp.concatenate([lo[sub:], hi.astype(BF16)], axis=1), xb)
                o = jnp.concatenate([top, bottom], axis=0)
                inner = o if inner is None else jnp.where(lane < k * width, inner, o)
                dec_log = cb if dec_log is None else jnp.where(lane < k * width, dec_log, cb)
            dec = jnp.exp2(dec_log)
            xf = xb.astype(F32)
            y = inner + skip * xf
            if b == 1:
                linked = seg_col[rows] == seg_col[GROUP - 1 : GROUP]
                rm = jnp.where(linked, rd_ref[rows].astype(F32), 0.0).astype(BF16)
                y = y + (dot(rm, carry[0]) + dot(rm, carry[1])) * dec
            else:
                xs = (xf * spread(tr, 0, width)).astype(BF16)
                s0 = dot(wr_ref[rows], xs, ((0,), (0,)))
                s0h = s0.astype(BF16)
                carry = (s0h, (s0 - s0h.astype(F32)).astype(BF16))
            v = gate_ref[rows].astype(F32)
            sg = v / (1.0 + jnp.exp(-v))
            a_ref[rows] = sg * y
            b_ref[rows] = sg * (dec * start)
            start = start * dec[GROUP - 1 : GROUP]

    tile = pl.BlockSpec((toks, LANES), lambda i, sc: (0, sc[which] * tiles + i))
    out = pl.BlockSpec((toks, LANES), lambda i, sc: (0, i))
    return call(
        body, 8, (tiles,),
        [
            tile, tile, whole(read.shape), whole(write.shape),
            pl.BlockSpec((1, toks, LANES), lambda i, sc: (sc[which], 0, 0)),
            whole(arow.shape),
            pl.BlockSpec((1, GROUP, LANES), lambda i, sc: (sc[which], toks // GROUP, 0)),
            pl.BlockSpec((1, 8, LANES), lambda i, sc: (sc[which], 0, i)),
        ],
        [out, out],
        [jax.ShapeDtypeStruct((toks, half_w), F32), jax.ShapeDtypeStruct((toks, half_w), F32)],
        [pltpu.VMEM((blocks, GROUP, GROUP), F32)],
        flops=4_000_000_000, nbytes=8_000_000,
    )(sc, x, gate, read, write, ccol, arow, tail, meta)


def gated_tile(prev_ref, rd_ref, seg_ref, a_ref, b_ref, e_ref, gain_ref):
    linked = seg_ref[0, :, SEG_LANE : SEG_LANE + 1] == prev_ref[0:1, 0:1]
    rm = jnp.where(linked, rd_ref[...].astype(F32), 0.0).astype(BF16)
    gated = a_ref[...] + b_ref[...] * dot(rm, e_ref[...])
    sq = gated * gated
    part = sq[:, 0:LANES]
    for i in range(1, sq.shape[1] // LANES):
        part = part + sq[:, i * LANES : (i + 1) * LANES]
    squares = jnp.sum(jnp.transpose(part), axis=0, keepdims=True)
    return (gated * gain_ref[...]).astype(BF16), squares


def gate_specs(which, toks, half_w, state):
    return [
        whole((8, LANES)), whole((toks, state)),
        pl.BlockSpec((1, toks, LANES), lambda i, sc: (0, 0, 0)),
        whole((toks, half_w)), whole((toks, half_w)), whole((state, half_w)),
        pl.BlockSpec((1, half_w), lambda i, sc: (0, sc[which])),
    ]


def gated_half(which, sc, prev, read, ccol, a, b, e, gain):
    toks, half_w = a.shape

    def body(sc_ref, prev_ref, rd_ref, seg_ref, a_ref, b_ref, e_ref, gain_ref, g_ref, s_ref):
        g_ref[...], s_ref[...] = gated_tile(prev_ref, rd_ref, seg_ref, a_ref, b_ref, e_ref, gain_ref)

    return call(
        body, 7, (1,),
        gate_specs(which, toks, half_w, read.shape[1]),
        [whole((toks, half_w)), whole((1, toks))],
        [jax.ShapeDtypeStruct((toks, half_w), BF16), jax.ShapeDtypeStruct((1, toks), F32)],
        flops=2 * toks * half_w * read.shape[1], nbytes=4_000_000,
    )(sc, prev, read, ccol, a, b, e, gain)


def gate_and_project(which, quarter, sc, prev, read, ccol, a, b, e, gain, g_keep, weight):
    toks, half_w = a.shape
    cols = weight.shape[1] // 4

    def body(
        sc_ref, prev_ref, rd_ref, seg_ref, a_ref, b_ref, e_ref, gain_ref, gk_ref, w_ref,
        g_ref, s_ref, y_ref,
    ):
        g, s_ref[...] = gated_tile(prev_ref, rd_ref, seg_ref, a_ref, b_ref, e_ref, gain_ref)
        g_ref[...] = g
        y = dot(gk_ref[...], w_ref[pl.ds(sc_ref[0] * half_w, half_w)])
        y = y + dot(g, w_ref[pl.ds(sc_ref[1] * half_w, half_w)])
        y_ref[...] = y.astype(BF16)

    return call(
        body, 9, (1,),
        gate_specs(which, toks, half_w, read.shape[1])
        + [whole((toks, half_w)), pl.BlockSpec((2 * half_w, cols), lambda i, sc: (0, sc[quarter]))],
        [whole((toks, half_w)), whole((1, toks)), whole((toks, cols))],
        [
            jax.ShapeDtypeStruct((toks, half_w), BF16),
            jax.ShapeDtypeStruct((1, toks), F32),
            jax.ShapeDtypeStruct((toks, cols), BF16),
        ],
        flops=4 * toks * half_w * cols, nbytes=6_000_000,
    )(sc, prev, read, ccol, a, b, e, gain, g_keep, weight)


def project(quarter, dtype, sc, g_keep, g_other, weight):
    toks, half_w = g_keep.shape
    cols = weight.shape[1] // 4

    def body(sc_ref, gk_ref, go_ref, w_ref, y_ref):
        y = dot(gk_ref[...], w_ref[pl.ds(sc_ref[0] * half_w, half_w)])
        y = y + dot(go_ref[...], w_ref[pl.ds(sc_ref[1] * half_w, half_w)])
        y_ref[...] = y.astype(dtype)

    return call(
        body, 3, (1,),
        [
            whole((toks, half_w)), whole((toks, half_w)),
            pl.BlockSpec((2 * half_w, cols), lambda i, sc: (0, sc[quarter])),
        ],
        whole((toks, cols)),
        jax.ShapeDtypeStruct((toks, cols), dtype),
        flops=4 * toks * half_w * cols, nbytes=4_000_000,
    )(sc, g_keep, g_other, weight)


def finish(features, sc, own, from_core, from_far, squares):
    toks, cols = own.shape

    def body(sc_ref, own_ref, core_ref, far_ref, sq_ref, out_ref):
        y = (own_ref[...] + core_ref[...].astype(F32)) + far_ref[...].astype(F32)
        inv = lax.rsqrt(sq_ref[...] / features + EPS)
        out_ref[...] = (jnp.transpose(y) * inv).astype(BF16)

    return call(
        body, 4, (1,),
        [whole((toks, cols))] * 3 + [whole((1, toks))],
        whole((cols, toks)),
        jax.ShapeDtypeStruct((cols, toks), BF16),
        flops=4 * toks * cols, nbytes=3_000_000,
    )(sc, own, from_core, from_far, squares)


def on_device(
    n_seq, n_tp, head_input, gate_input, write_vecs, read_vecs, step_raw, segment_ids,
    decay_log, step_bias, skip_gain, norm_gain, out_weight,
):
    heads = decay_log.shape[0]
    toks, feats = head_input.shape
    width = feats // heads
    half_w = feats // 2
    place = lax.axis_index("seq")
    rank = lax.axis_index("tp")
    odd = lax.rem(place, 2)
    even = odd == 0
    near, far = rank ^ 1, rank ^ 2
    sc = jnp.stack([odd, 1 - odd, far ^ 1, far, near, rank]).astype(jnp.int32)

    def pair(a):
        return lax.ppermute(a, "seq", [(i, i ^ 1) for i in range(n_seq)])

    def shift(a, by):
        return lax.ppermute(a, "seq", [(i, i + by) for i in range(n_seq - by)])

    def across(a, bit):
        return lax.ppermute(a, "tp", [(i, i ^ bit) for i in range(n_tp)])

    send, ccol, arow, tail, meta = prepare(
        heads, width, sc, step_raw, segment_ids.reshape(1, toks), decay_log.reshape(1, heads),
        step_bias.reshape(1, heads), skip_gain.reshape(1, heads), head_input, write_vecs,
    )
    got_state = pair(send)
    got_meta = pair(lax.dynamic_index_in_dim(meta, 1 - odd, 0, False))
    own_meta = lax.dynamic_index_in_dim(meta, odd, 0, False)
    own_state = kept_state(width, sc, tail, head_input, write_vecs)
    a_keep, b_keep = local_part(
        0, heads, width, sc, head_input, gate_input, read_vecs, write_vecs, ccol, arow, tail, meta
    )
    keep_first = jnp.where(even, own_meta[0:1], got_meta[0:1])
    keep_second = jnp.where(even, got_meta[0:1], own_meta[0:1])
    last_first = jnp.where(even, own_meta[1:2, 0:1], got_meta[1:2, 0:1])
    last_second = jnp.where(even, got_meta[1:2, 0:1], own_meta[1:2, 0:1])
    got_f = got_state.astype(F32)
    first = jnp.where(even, own_state, got_f)
    second = jnp.where(even, got_f, own_state)
    joined = second + keep_second * (last_first == last_second).astype(F32) * first
    through = keep_first * keep_second
    last_tile = jnp.broadcast_to(last_second, (8, LANES))
    prev_last = shift(last_tile, 2)
    reach = 1
    pairs = n_seq // 2
    while reach < pairs // 2:
        before = shift(joined.astype(BF16), 2 * reach)
        last_before = prev_last if reach == 1 else shift(last_tile, 2 * reach)
        link = through * (last_before[0:1, 0:1] == last_second).astype(F32)
        joined = joined + link * before.astype(F32)
        if 2 * reach < pairs // 2:
            through = link * shift(through, 2 * reach)
        reach *= 2
    entry = shift(joined.astype(BF16), 2)
    a_other, b_other = local_part(
        1, heads, width, sc, head_input, gate_input, read_vecs, write_vecs, ccol, arow, tail, meta
    )
    prev_id = prev_last[0:1, 0:1]
    after_first = (
        first + keep_first * (last_first == prev_id).astype(F32) * entry.astype(F32)
    ).astype(BF16)
    e_other = pair(jnp.where(even, after_first, entry))
    e_keep = jnp.where(even, entry, after_first)
    prev = jnp.where(even, prev_last, jnp.broadcast_to(last_first, (8, LANES)))
    gain = norm_gain.reshape(1, feats)
    g_keep, s_keep = gated_half(0, sc, prev, read_vecs, ccol, a_keep, b_keep, e_keep, gain)
    g_other, s_other, y_far_near = gate_and_project(
        1, 2, sc, prev, read_vecs, ccol, a_other, b_other, e_other, gain, g_keep, out_weight
    )
    got_far = across(y_far_near, 1)
    y_far = project(3, F32, sc, g_keep, g_other, out_weight)
    got_x = across((y_far + got_far.astype(F32)).astype(BF16), 2)
    squares = s_keep + s_other
    squares = squares + across(squares, 1)
    squares = squares + across(squares, 2)
    got_near = across(project(4, BF16, sc, g_keep, g_other, out_weight), 1)
    y_own = project(5, F32, sc, g_keep, g_other, out_weight)
    return finish(feats * n_tp, sc, y_own, got_near, got_x, squares)


def solution(mesh):
    in_specs = (
        P("seq", "tp"),
        P("seq", "tp"),
        P("seq", None),
        P("seq", None),
        P("tp", "seq"),
        P("seq"),
        P("tp"),
        P("tp"),
        P("tp"),
        P("tp"),
        P("tp", None),
    )
    out_specs = P("tp", "seq")
    return jax.shard_map(
        functools.partial(on_device, mesh.shape["seq"], mesh.shape["tp"]),
        mesh=mesh, in_specs=in_specs, out_specs=out_specs, check_vma=False,
    )
```

```python
import functools

import jax
import jax.numpy as jnp
from jax import lax
from jax.experimental import pallas as pl
from jax.experimental.pallas import tpu as pltpu
from jax.sharding import PartitionSpec as P

GROUP = 256
LANES = 128
EPS = 1e-05
LOG2E = 1.4426950408889634
SEG_LANE = 32
EXTRA = 16
VMEM = 20 * 1024 * 1024
VMEM_ALL = 63 * 1024 * 1024
F32 = jnp.float32
BF16 = jnp.bfloat16


def dot(a, b, dims=((1,), (0,))):
    return lax.dot_general(a, b, (dims, ((), ())), preferred_element_type=F32)


def lane_iota(rows):
    return lax.broadcasted_iota(jnp.int32, (rows, LANES), 1)


def spread(cols, first, width):
    rows = cols.shape[0]
    per = LANES // width
    lane = lane_iota(rows)
    out = jnp.broadcast_to(cols[:, first : first + 1], (rows, LANES))
    for k in range(1, per):
        nxt = jnp.broadcast_to(cols[:, first + k : first + k + 1], (rows, LANES))
        out = jnp.where(lane < k * width, out, nxt)
    return out


def call(body, n_in, grid, in_specs, out_specs, out_shape, scratch=(), flops=0, nbytes=0, limit=VMEM):
    del n_in
    return pl.pallas_call(
        body,
        grid_spec=pltpu.PrefetchScalarGridSpec(
            num_scalar_prefetch=1,
            grid=grid,
            in_specs=in_specs,
            out_specs=out_specs,
            scratch_shapes=list(scratch),
        ),
        out_shape=out_shape,
        compiler_params=pltpu.CompilerParams(vmem_limit_bytes=limit),
        cost_estimate=pl.CostEstimate(flops=flops, bytes_accessed=nbytes, transcendentals=0),
    )


def whole(shape):
    return pl.BlockSpec(shape, lambda i, sc: (0,) * len(shape))


def pack_rows(out_ref, state, meta):
    keep = meta[0:1]
    high = keep.astype(BF16)
    low = (keep - high.astype(F32)).astype(BF16)
    row = lax.broadcasted_iota(jnp.int32, (EXTRA, meta.shape[1]), 0)
    rows = jnp.where(row == 0, high.astype(F32), jnp.where(row == 1, low.astype(F32), meta[1:2]))
    out_ref[state : state + EXTRA] = rows.astype(BF16)


def prepare(heads, width, sc, raw, seg, decay_log, bias, skip, x, write):
    toks = raw.shape[1]
    state = write.shape[1]
    half_w = x.shape[1] // 2
    half_h = heads // 2
    blocks = toks // GROUP

    def body(
        sc_ref, raw_ref, seg_ref, dl_ref, sb_ref, sk_ref, x_ref, wr_ref,
        send_ref, ccol_ref, arow_ref, tail_ref, meta_ref, pad, rows,
    ):
        pad[...] = jnp.zeros_like(pad)
        pad[0:heads] = raw_ref[...].astype(F32)
        pad[SEG_LANE : SEG_LANE + 1] = seg_ref[...].astype(F32)
        rows[...] = jnp.zeros_like(rows)
        rows[0:1, 0:heads] = dl_ref[...]
        rows[1:2, 0:heads] = sb_ref[...]
        rows[2:3, 0:heads] = sk_ref[...]
        cols = jnp.transpose(pad[...])
        lane = lane_iota(toks)
        z = cols + rows[1:2]
        step = jnp.maximum(z, 0.0) + jnp.log1p(jnp.exp(-jnp.abs(z)))
        rate = -jnp.exp(rows[0:1]) * step
        tri = (
            lax.broadcasted_iota(jnp.int32, (GROUP, GROUP), 0)
            >= lax.broadcasted_iota(jnp.int32, (GROUP, GROUP), 1)
        ).astype(BF16)
        cum, full = [], []
        base = jnp.zeros((1, LANES), F32)
        for b in range(blocks):
            r = rate[b * GROUP : (b + 1) * GROUP]
            r1 = r.astype(BF16)
            d1 = r - r1.astype(F32)
            r2 = d1.astype(BF16)
            r3 = (d1 - r2.astype(F32)).astype(BF16)
            c = dot(tri, r1) + (dot(tri, r2) + dot(tri, r3))
            cum.append(c)
            full.append(c + base)
            base = base + c[GROUP - 1 : GROUP]
        total = base
        seg_col = cols[:, SEG_LANE : SEG_LANE + 1]
        last = cols[toks - 1 : toks, SEG_LANE : SEG_LANE + 1]
        cum_all = jnp.concatenate(cum, axis=0)
        tail = jnp.exp(total - jnp.concatenate(full, axis=0)) * step
        tail = jnp.where(seg_col == last, tail, 0.0)
        last0 = cols[GROUP - 1 : GROUP, SEG_LANE : SEG_LANE + 1]
        tail0 = jnp.exp(cum[0][GROUP - 1 : GROUP] - cum[0]) * step[0:GROUP]
        tail0 = jnp.where(seg_col[0:GROUP] == last0, tail0, 0.0)
        cc = cum_all * LOG2E
        a = jnp.where(lane == SEG_LANE, cols, cc - jnp.log(step) * LOG2E)
        arow_ref[...] = jnp.transpose(a)[0:64]
        seg_b = jnp.broadcast_to(seg_col, (toks, LANES))
        ccol_ref[0] = jnp.where(lane == SEG_LANE, seg_b, cc)
        ccol_ref[1] = jnp.where(lane == SEG_LANE, seg_b, pltpu.roll(cc, LANES - half_h, 1))
        tail_r = pltpu.roll(tail, LANES - half_h, 1)
        tail_ref[0, 0:toks] = tail
        tail_ref[1, 0:toks] = tail_r
        tail_ref[0, toks : toks + GROUP] = tail0
        tail_ref[1, toks : toks + GROUP] = pltpu.roll(tail0, LANES - half_h, 1)
        keep = jnp.exp(total)
        per = LANES // width
        for j in range(2):
            for i in range(half_w // LANES):
                at = j * half_h + i * per
                tile = slice(i * LANES, (i + 1) * LANES)
                meta_ref[j, 0:1, tile] = spread(keep, at, width)
                meta_ref[j, 1:2, tile] = jnp.broadcast_to(last, (1, LANES))
                meta_ref[j, 2:3, tile] = spread(rows[2:3], at, width)
                meta_ref[j, 3:8, tile] = jnp.zeros((5, LANES), F32)
        mine = jnp.where(sc_ref[1] == 0, tail, tail_r)
        parts = []
        for i in range(half_w // LANES):
            xt = x_ref[:, i * LANES : (i + 1) * LANES].astype(F32)
            parts.append((xt * spread(mine, i * per, width)).astype(BF16))
        xs = jnp.concatenate(parts, axis=1)
        send_ref[0:state] = dot(wr_ref[...], xs, ((0,), (0,))).astype(BF16)
        pack_rows(send_ref, state, meta_ref[sc_ref[1]])

    return call(
        body, 7, (1,),
        [
            whole(raw.shape), whole(seg.shape), whole(decay_log.shape), whole(bias.shape), whole(skip.shape),
            pl.BlockSpec((toks, half_w), lambda i, sc: (0, sc[1])),
            whole(write.shape),
        ],
        [
            whole((state + EXTRA, half_w)), whole((2, toks, LANES)), whole((64, toks)),
            whole((2, toks + GROUP, LANES)), whole((2, 8, half_w)),
        ],
        [
            jax.ShapeDtypeStruct((state + EXTRA, half_w), BF16),
            jax.ShapeDtypeStruct((2, toks, LANES), F32),
            jax.ShapeDtypeStruct((64, toks), F32),
            jax.ShapeDtypeStruct((2, toks + GROUP, LANES), F32),
            jax.ShapeDtypeStruct((2, 8, half_w), F32),
        ],
        [pltpu.VMEM((LANES, toks), F32), pltpu.VMEM((8, LANES), F32)],
        flops=2 * toks * state * half_w, nbytes=4_000_000, limit=VMEM_ALL,
    )(sc, raw, seg, decay_log, bias, skip, x, write)


def kept_state(width, sc, tail, meta, x, write):
    toks, state = write.shape
    half_w = x.shape[1] // 2
    per = LANES // width

    def body(sc_ref, tail_ref, meta_ref, x_ref, wr_ref, out_ref, send_ref):
        mine = tail_ref[0]
        parts = []
        for i in range(half_w // LANES):
            xt = x_ref[:, i * LANES : (i + 1) * LANES].astype(F32)
            parts.append((xt * spread(mine, i * per, width)).astype(BF16))
        own = dot(wr_ref[...], jnp.concatenate(parts, axis=1), ((0,), (0,)))
        out_ref[...] = own
        send_ref[0:state] = own.astype(BF16)
        pack_rows(send_ref, state, meta_ref[0])

    return call(
        body, 3, (1,),
        [
            pl.BlockSpec((1, toks, LANES), lambda i, sc: (sc[0], 0, 0)),
            pl.BlockSpec((1, 8, half_w), lambda i, sc: (sc[0], 0, 0)),
            pl.BlockSpec((toks, half_w), lambda i, sc: (0, sc[0])),
            whole(write.shape),
        ],
        [whole((state, half_w)), whole((state + EXTRA, half_w))],
        [
            jax.ShapeDtypeStruct((state, half_w), F32),
            jax.ShapeDtypeStruct((state + EXTRA, half_w), BF16),
        ],
        flops=2 * toks * state * half_w, nbytes=2_000_000,
    )(sc, tail, meta, x, write)


def local_part(which, heads, width, sc, x, gate, read, write, ccol, arow, tail, meta, after):
    toks, state = write.shape
    half_w = x.shape[1] // 2
    half_h = heads // 2
    per = LANES // width
    tiles = half_w // LANES
    blocks = toks // GROUP
    sub = GROUP // 2

    def body(
        sc_ref, x_ref, gate_ref, rd_ref, wr_ref, ccol_ref, arow_ref, tail0_ref, meta_ref, after_ref,
        a_ref, b_ref, scores,
    ):
        i = pl.program_id(0)
        seg_col = ccol_ref[0, :, SEG_LANE : SEG_LANE + 1]

        @pl.when(i == 0)
        def _():
            for b in range(blocks):
                rows = slice(b * GROUP, (b + 1) * GROUP)
                s = dot(rd_ref[rows], wr_ref[rows], ((1,), (1,)))
                causal = lax.broadcasted_iota(jnp.int32, (GROUP, GROUP), 0) >= lax.broadcasted_iota(
                    jnp.int32, (GROUP, GROUP), 1
                )
                same = seg_col[rows] == arow_ref[SEG_LANE : SEG_LANE + 1, rows]
                scores[b] = jnp.where(causal & same, s, 0.0)

        turn = lax.rem(LANES - per * i, LANES)
        cr = pltpu.roll(ccol_ref[0], turn, 1)
        tr = pltpu.roll(tail0_ref[0], turn, 1)
        skip = meta_ref[0, 2:3, :]
        lane = lane_iota(GROUP)
        head0 = sc_ref[which] * half_h + per * i
        carry = None
        start = jnp.ones((1, LANES), F32)
        for b in range(blocks):
            rows = slice(b * GROUP, (b + 1) * GROUP)
            xb = x_ref[rows]
            inner = None
            dec_log = None
            for k in range(per):
                cb = jnp.broadcast_to(cr[rows, k : k + 1], (GROUP, LANES))
                ar = arow_ref[pl.ds(head0 + k, 1), rows]
                sb = scores[b]
                lo = jnp.exp2(jnp.minimum(cb - ar[:, 0:sub], 60.0)) * sb[:, 0:sub]
                hi = jnp.exp2(jnp.minimum(cb[sub:] - ar[:, sub:], 60.0)) * sb[sub:, sub:]
                lo = lo.astype(BF16)
                top = dot(lo[0:sub], xb[0:sub])
                bottom = dot(jnp.concatenate([lo[sub:], hi.astype(BF16)], axis=1), xb)
                o = jnp.concatenate([top, bottom], axis=0)
                inner = o if inner is None else jnp.where(lane < k * width, inner, o)
                dec_log = cb if dec_log is None else jnp.where(lane < k * width, dec_log, cb)
            dec = jnp.exp2(dec_log)
            xf = xb.astype(F32)
            y = inner + skip * xf
            if b == 1:
                linked = seg_col[rows] == seg_col[GROUP - 1 : GROUP]
                rm = jnp.where(linked, rd_ref[rows].astype(F32), 0.0).astype(BF16)
                y = y + (dot(rm, carry[0]) + dot(rm, carry[1])) * dec
            else:
                xs = (xf * spread(tr, 0, width)).astype(BF16)
                s0 = dot(wr_ref[rows], xs, ((0,), (0,)))
                s0h = s0.astype(BF16)
                carry = (s0h, (s0 - s0h.astype(F32)).astype(BF16))
            v = gate_ref[rows].astype(F32)
            sg = v / (1.0 + jnp.exp(-v))
            a_ref[rows] = sg * y
            b_ref[rows] = sg * (dec * start)
            start = start * dec[GROUP - 1 : GROUP]

    tile = pl.BlockSpec((toks, LANES), lambda i, sc: (0, sc[which] * tiles + i))
    out = pl.BlockSpec((toks, LANES), lambda i, sc: (0, i))
    return call(
        body, 8, (tiles,),
        [
            tile, tile, whole(read.shape), whole(write.shape),
            pl.BlockSpec((1, toks, LANES), lambda i, sc: (sc[which], 0, 0)),
            whole(arow.shape),
            pl.BlockSpec((1, GROUP, LANES), lambda i, sc: (sc[which], toks // GROUP, 0)),
            pl.BlockSpec((1, 8, LANES), lambda i, sc: (sc[which], 0, i)),
            pl.BlockSpec(memory_space=pl.ANY),
        ],
        [out, out],
        [jax.ShapeDtypeStruct((toks, half_w), F32), jax.ShapeDtypeStruct((toks, half_w), F32)],
        [pltpu.VMEM((blocks, GROUP, GROUP), F32)],
        flops=4_000_000_000, nbytes=8_000_000,
    )(sc, x, gate, read, write, ccol, arow, tail, meta, after)


def gated_tile(prev_ref, rd_ref, seg_ref, a_ref, b_ref, e_ref, gain_ref):
    linked = seg_ref[0, :, SEG_LANE : SEG_LANE + 1] == prev_ref[0:1, 0:1]
    rm = jnp.where(linked, rd_ref[...].astype(F32), 0.0).astype(BF16)
    gated = a_ref[...] + b_ref[...] * dot(rm, e_ref[...])
    sq = gated * gated
    part = sq[:, 0:LANES]
    for i in range(1, sq.shape[1] // LANES):
        part = part + sq[:, i * LANES : (i + 1) * LANES]
    squares = jnp.sum(jnp.transpose(part), axis=0, keepdims=True)
    return (gated * gain_ref[...]).astype(BF16), squares


def gate_specs(which, toks, half_w, state):
    return [
        whole((8, LANES)), whole((toks, state)),
        pl.BlockSpec((1, toks, LANES), lambda i, sc: (0, 0, 0)),
        whole((toks, half_w)), whole((toks, half_w)), whole((state, half_w)),
        pl.BlockSpec((1, half_w), lambda i, sc: (0, sc[which])),
    ]


def gated_half(which, sc, prev, read, ccol, a, b, e, gain):
    toks, half_w = a.shape

    def body(sc_ref, prev_ref, rd_ref, seg_ref, a_ref, b_ref, e_ref, gain_ref, g_ref, s_ref):
        g_ref[...], s_ref[...] = gated_tile(prev_ref, rd_ref, seg_ref, a_ref, b_ref, e_ref, gain_ref)

    return call(
        body, 7, (1,),
        gate_specs(which, toks, half_w, read.shape[1]),
        [whole((toks, half_w)), whole((1, toks))],
        [jax.ShapeDtypeStruct((toks, half_w), BF16), jax.ShapeDtypeStruct((1, toks), F32)],
        flops=2 * toks * half_w * read.shape[1], nbytes=4_000_000,
    )(sc, prev, read, ccol, a, b, e, gain)


def gate_and_project(which, quarter, sc, prev, read, ccol, a, b, e, gain, g_keep, weight):
    toks, half_w = a.shape
    cols = weight.shape[1] // 4

    def body(
        sc_ref, prev_ref, rd_ref, seg_ref, a_ref, b_ref, e_ref, gain_ref, gk_ref, w_ref,
        g_ref, s_ref, y_ref,
    ):
        g, s_ref[...] = gated_tile(prev_ref, rd_ref, seg_ref, a_ref, b_ref, e_ref, gain_ref)
        g_ref[...] = g
        y = dot(gk_ref[...], w_ref[pl.ds(sc_ref[0] * half_w, half_w)])
        y = y + dot(g, w_ref[pl.ds(sc_ref[1] * half_w, half_w)])
        y_ref[...] = jnp.transpose(y).astype(BF16)

    return call(
        body, 9, (1,),
        gate_specs(which, toks, half_w, read.shape[1])
        + [whole((toks, half_w)), pl.BlockSpec((2 * half_w, cols), lambda i, sc: (0, sc[quarter]))],
        [whole((toks, half_w)), whole((1, toks)), whole((cols, toks))],
        [
            jax.ShapeDtypeStruct((toks, half_w), BF16),
            jax.ShapeDtypeStruct((1, toks), F32),
            jax.ShapeDtypeStruct((cols, toks), BF16),
        ],
        flops=4 * toks * half_w * cols, nbytes=6_000_000,
    )(sc, prev, read, ccol, a, b, e, gain, g_keep, weight)


def project(quarter, dtype, sc, g_keep, g_other, weight, after):
    toks, half_w = g_keep.shape
    cols = weight.shape[1] // 4

    def body(sc_ref, gk_ref, go_ref, w_ref, after_ref, y_ref):
        y = dot(gk_ref[...], w_ref[pl.ds(sc_ref[0] * half_w, half_w)])
        y = y + dot(go_ref[...], w_ref[pl.ds(sc_ref[1] * half_w, half_w)])
        y_ref[...] = jnp.transpose(y).astype(dtype)

    return call(
        body, 4, (1,),
        [
            whole((toks, half_w)), whole((toks, half_w)),
            pl.BlockSpec((2 * half_w, cols), lambda i, sc: (0, sc[quarter])),
            pl.BlockSpec(memory_space=pl.ANY),
        ],
        whole((cols, toks)),
        jax.ShapeDtypeStruct((cols, toks), dtype),
        flops=4 * toks * half_w * cols, nbytes=4_000_000,
    )(sc, g_keep, g_other, weight, after)


def on_device(
    n_seq, n_tp, head_input, gate_input, write_vecs, read_vecs, step_raw, segment_ids,
    decay_log, step_bias, skip_gain, norm_gain, out_weight,
):
    heads = decay_log.shape[0]
    toks, feats = head_input.shape
    width = feats // heads
    state = write_vecs.shape[1]
    place = lax.axis_index("seq")
    rank = lax.axis_index("tp")
    odd = lax.rem(place, 2)
    even = odd == 0
    near, far = rank ^ 1, rank ^ 2
    sc = jnp.stack([odd, 1 - odd, far ^ 1, far, near, rank]).astype(jnp.int32)

    def swap(a, bit):
        return lax.ppermute(a, "seq", [(i, i ^ bit) for i in range(n_seq)])

    def across(a, bit):
        return lax.ppermute(a, "tp", [(i, i ^ bit) for i in range(n_tp)])

    def member(payload):
        f = payload.astype(F32)
        return f[0:state], f[state : state + 1] + f[state + 1 : state + 2], f[state + 2 : state + 3, 0:1]

    def joined(first, second):
        link = second[1] * (first[2] == second[2]).astype(F32)
        return second[0] + link * first[0], second[1] * first[1], second[2]

    def ordered(swapped, one, two):
        firsts = tuple(jnp.where(swapped, t, o) for o, t in zip(one, two))
        seconds = tuple(jnp.where(swapped, o, t) for o, t in zip(one, two))
        return firsts, seconds

    send_other, ccol, arow, tail, meta = prepare(
        heads, width, sc, step_raw, segment_ids.reshape(1, toks), decay_log.reshape(1, heads),
        step_bias.reshape(1, heads), skip_gain.reshape(1, heads), head_input, write_vecs,
    )
    mate_raw = swap(send_other, 1)
    cross_raw = swap(send_other, 3) if n_seq > 2 else None
    own_state, send_keep = kept_state(width, sc, tail, meta, head_input, write_vecs)
    side_raw = swap(send_keep, 2) if n_seq > 2 else None
    a_keep, b_keep = local_part(
        0, heads, width, sc, head_input, gate_input, read_vecs, write_vecs, ccol, arow, tail, meta, send_keep
    )
    own = (own_state,) + member(send_keep)[1:]
    first, second = ordered(odd == 1, own, member(mate_raw))
    total = joined(first, second)
    entry = jnp.zeros_like(own_state)
    entry_through = jnp.ones_like(total[1])
    entry_id = jnp.full((1, 1), -1.0, F32)
    after = send_keep
    bit = 2
    while bit < n_seq:
        upper = (place & bit) != 0
        if bit == 2:
            other = joined(*ordered(odd == 1, member(side_raw), member(cross_raw)))
        else:
            sent = total[0].astype(BF16)
            after = sent
            other_state = swap(sent, bit).astype(F32)
            rows = swap(jnp.concatenate([total[1], jnp.broadcast_to(total[2], total[1].shape)], axis=0), bit)
            other = (other_state, rows[0:1], rows[1:2, 0:1])
        link = entry_through * ((entry_id < 0) | (other[2] == entry_id)).astype(F32)
        link = jnp.where(upper, link, 0.0)
        entry = entry + link * other[0]
        entry_id = jnp.where(upper & (entry_id < 0), other[2], entry_id)
        entry_through = entry_through * jnp.where(upper, other[1], 1.0)
        if 2 * bit < n_seq:
            total = joined(*ordered(upper, total, other))
        bit *= 2
    a_other, b_other = local_part(
        1, heads, width, sc, head_input, gate_input, read_vecs, write_vecs, ccol, arow, tail, meta, after
    )
    reached = first[0] + first[1] * (first[2] == entry_id).astype(F32) * entry
    entry, reached = entry.astype(BF16), reached.astype(BF16)
    e_other = swap(jnp.where(even, reached, entry), 1)
    e_keep = jnp.where(even, entry, reached)
    prev = jnp.broadcast_to(jnp.where(even, entry_id, first[2]), (8, LANES))
    gain = norm_gain.reshape(1, feats)
    g_keep, s_keep = gated_half(0, sc, prev, read_vecs, ccol, a_keep, b_keep, e_keep, gain)
    g_other, s_other, y_far_near = gate_and_project(
        1, 2, sc, prev, read_vecs, ccol, a_other, b_other, e_other, gain, g_keep, out_weight
    )
    got_far = across(y_far_near, 1)
    squares = s_keep + s_other
    squares = squares + across(squares, 1)
    y_far = project(3, F32, sc, g_keep, g_other, out_weight, y_far_near)
    to_far = (y_far + got_far.astype(F32)).astype(BF16)
    got_x = across(to_far, 2)
    squares = squares + across(squares, 2)
    got_near = across(project(4, BF16, sc, g_keep, g_other, out_weight, to_far), 1)
    y_own = project(5, F32, sc, g_keep, g_other, out_weight, to_far)
    inv = lax.rsqrt(squares / (feats * n_tp) + EPS)
    out = (y_own + got_near.astype(F32)) + got_x.astype(F32)
    return (out * inv).astype(BF16)


def solution(mesh):
    in_specs = (
        P("seq", "tp"),
        P("seq", "tp"),
        P("seq", None),
        P("seq", None),
        P("tp", "seq"),
        P("seq"),
        P("tp"),
        P("tp"),
        P("tp"),
        P("tp"),
        P("tp", None),
    )
    out_specs = P("tp", "seq")
    return jax.shard_map(
        functools.partial(on_device, mesh.shape["seq"], mesh.shape["tp"]),
        mesh=mesh, in_specs=in_specs, out_specs=out_specs, check_vma=False,
    )
```

```python
import functools

import jax
import jax.numpy as jnp
from jax import lax
from jax.experimental import pallas as pl
from jax.experimental.pallas import tpu as pltpu
from jax.sharding import PartitionSpec as P

GROUP = 256
LANES = 128
EPS = 1e-05
LOG2E = 1.4426950408889634
SEG_LANE = 32
EXTRA = 16
VMEM = 48 * 1024 * 1024
VMEM_ALL = 63 * 1024 * 1024
F32 = jnp.float32
BF16 = jnp.bfloat16


def dot(a, b, dims=((1,), (0,))):
    return lax.dot_general(a, b, (dims, ((), ())), preferred_element_type=F32)


def lane_iota(rows):
    return lax.broadcasted_iota(jnp.int32, (rows, LANES), 1)


def spread(cols, first, width):
    rows = cols.shape[0]
    per = LANES // width
    lane = lane_iota(rows)
    out = jnp.broadcast_to(cols[:, first : first + 1], (rows, LANES))
    for k in range(1, per):
        nxt = jnp.broadcast_to(cols[:, first + k : first + k + 1], (rows, LANES))
        out = jnp.where(lane < k * width, out, nxt)
    return out


def call(body, grid, in_specs, out_specs, out_shape, scratch=(), cost=0, limit=VMEM):
    return pl.pallas_call(
        body,
        grid_spec=pltpu.PrefetchScalarGridSpec(
            num_scalar_prefetch=1,
            grid=grid,
            in_specs=in_specs,
            out_specs=out_specs,
            scratch_shapes=list(scratch),
        ),
        out_shape=out_shape,
        compiler_params=pltpu.CompilerParams(vmem_limit_bytes=limit),
        cost_estimate=pl.CostEstimate(flops=cost, bytes_accessed=1000, transcendentals=0),
    )


def anywhere():
    return pl.BlockSpec(memory_space=pl.ANY)


def whole(shape):
    return pl.BlockSpec(shape, lambda i, sc: (0,) * len(shape))


def pack(out_ref, total):
    state, through, last = total
    size, lanes = state.shape
    high = through.astype(BF16).astype(F32)
    row = lax.broadcasted_iota(jnp.int32, (EXTRA, lanes), 0)
    rows = jnp.where(row == 0, high, jnp.where(row == 1, through - high, last))
    out_ref[0:size] = state.astype(BF16)
    out_ref[size : size + EXTRA] = rows.astype(BF16)


def unpack(ref):
    size = ref.shape[0] - EXTRA
    rows = ref[size : size + EXTRA].astype(F32)
    return ref[0:size].astype(F32), rows[0:1] + rows[1:2], rows[2:3, 0:1]


def joined(first, second):
    link = second[1] * (first[2] == second[2]).astype(F32)
    return second[0] + link * first[0], second[1] * first[1], second[2]


def ordered(swapped, one, two):
    firsts = tuple(jnp.where(swapped, t, o) for o, t in zip(one, two))
    seconds = tuple(jnp.where(swapped, o, t) for o, t in zip(one, two))
    return firsts, seconds


def prepare(heads, width, raw, seg, decay_log, bias, skip, x, write):
    toks = raw.shape[1]
    state = write.shape[1]
    half_w = x.shape[1] // 2
    half_h = heads // 2
    blocks = toks // GROUP

    def body(
        raw_ref, seg_ref, dl_ref, sb_ref, sk_ref, x_hbm, wr_ref,
        other_ref, keep_ref, own_ref, ccol_ref, arow_ref, tail_ref, skip_ref,
        pad, rows, x_ref, sem,
    ):
        copy = pltpu.make_async_copy(x_hbm, x_ref, sem)
        copy.start()
        pad[...] = jnp.zeros_like(pad)
        pad[0:heads] = raw_ref[...].astype(F32)
        pad[SEG_LANE : SEG_LANE + 1] = seg_ref[...].astype(F32)
        rows[...] = jnp.zeros_like(rows)
        rows[0:1, 0:heads] = dl_ref[...]
        rows[1:2, 0:heads] = sb_ref[...]
        rows[2:3, 0:heads] = sk_ref[...]
        cols = jnp.transpose(pad[...])
        lane = lane_iota(toks)
        z = cols + rows[1:2]
        step = jnp.maximum(z, 0.0) + jnp.log1p(jnp.exp(-jnp.abs(z)))
        rate = -jnp.exp(rows[0:1]) * step
        tri = (
            lax.broadcasted_iota(jnp.int32, (GROUP, GROUP), 0)
            >= lax.broadcasted_iota(jnp.int32, (GROUP, GROUP), 1)
        ).astype(BF16)
        cum, full = [], []
        base = jnp.zeros((1, LANES), F32)
        for b in range(blocks):
            r = rate[b * GROUP : (b + 1) * GROUP]
            r1 = r.astype(BF16)
            d1 = r - r1.astype(F32)
            r2 = d1.astype(BF16)
            r3 = (d1 - r2.astype(F32)).astype(BF16)
            c = dot(tri, r1) + (dot(tri, r2) + dot(tri, r3))
            cum.append(c)
            full.append(c + base)
            base = base + c[GROUP - 1 : GROUP]
        total = base
        seg_col = cols[:, SEG_LANE : SEG_LANE + 1]
        last = cols[toks - 1 : toks, SEG_LANE : SEG_LANE + 1]
        tail = jnp.exp(total - jnp.concatenate(full, axis=0)) * step
        tail = jnp.where(seg_col == last, tail, 0.0)
        per = LANES // width
        keep = jnp.exp(total)
        copy.wait()
        halves = []
        for j in range(2):
            parts, through = [], []
            for i in range(half_w // LANES):
                at = j * half_h + i * per
                xt = x_ref[:, j * half_w + i * LANES : j * half_w + (i + 1) * LANES].astype(F32)
                parts.append((xt * spread(tail, at, width)).astype(BF16))
                through.append(spread(keep, at, width))
            own = dot(wr_ref[...], jnp.concatenate(parts, axis=1), ((0,), (0,)))
            halves.append((own, jnp.concatenate(through, axis=1), last))
        odd = lax.rem(lax.axis_index("seq"), 2) == 1
        mine, other = ordered(odd, *halves)
        own_ref[...] = mine[0]
        pack(keep_ref, mine)
        pack(other_ref, other)
        cum_all = jnp.concatenate(cum, axis=0)
        last0 = cols[GROUP - 1 : GROUP, SEG_LANE : SEG_LANE + 1]
        tail0 = jnp.exp(cum[0][GROUP - 1 : GROUP] - cum[0]) * step[0:GROUP]
        tail0 = jnp.where(seg_col[0:GROUP] == last0, tail0, 0.0)
        cc = cum_all * LOG2E
        a = jnp.where(lane == SEG_LANE, cols, cc - jnp.log(step) * LOG2E)
        arow_ref[...] = jnp.transpose(a)[0:64]
        seg_b = jnp.broadcast_to(seg_col, (toks, LANES))
        ccol_ref[0] = jnp.where(lane == SEG_LANE, seg_b, cc)
        ccol_ref[1] = jnp.where(lane == SEG_LANE, seg_b, pltpu.roll(cc, LANES - half_h, 1))
        tail_ref[0] = tail0
        tail_ref[1] = pltpu.roll(tail0, LANES - half_h, 1)
        for j in range(2):
            for i in range(half_w // LANES):
                tile = slice(i * LANES, (i + 1) * LANES)
                gains = spread(rows[2:3], j * half_h + i * per, width)
                skip_ref[j, :, tile] = jnp.broadcast_to(gains, (8, LANES))

    vm = pl.BlockSpec(memory_space=pltpu.VMEM)
    return pl.pallas_call(
        body,
        in_specs=[vm, vm, vm, vm, vm, anywhere(), vm],
        out_specs=[vm] * 7,
        out_shape=[
            jax.ShapeDtypeStruct((state + EXTRA, half_w), BF16),
            jax.ShapeDtypeStruct((state + EXTRA, half_w), BF16),
            jax.ShapeDtypeStruct((state, half_w), F32),
            jax.ShapeDtypeStruct((2, toks, LANES), F32),
            jax.ShapeDtypeStruct((64, toks), F32),
            jax.ShapeDtypeStruct((2, GROUP, LANES), F32),
            jax.ShapeDtypeStruct((2, 8, half_w), F32),
        ],
        scratch_shapes=[
            pltpu.VMEM((LANES, toks), F32), pltpu.VMEM((8, LANES), F32),
            pltpu.VMEM(x.shape, BF16), pltpu.SemaphoreType.DMA(()),
        ],
        compiler_params=pltpu.CompilerParams(vmem_limit_bytes=VMEM_ALL),
        cost_estimate=pl.CostEstimate(flops=4_000_000_000, bytes_accessed=1000, transcendentals=0),
    )(raw, seg, decay_log, bias, skip, x, write)


def gather_level(upper, entry, other):
    state, through, last_id = entry
    link = through * ((last_id < 0) | (other[2] == last_id)).astype(F32)
    state = state + jnp.where(upper, link, 0.0) * other[0]
    last_id = jnp.where(upper & (last_id < 0), other[2], last_id)
    return state, through * jnp.where(upper, other[1], 1.0), last_id


def put_rows(rows_ref, rows):
    lanes = rows_ref.shape[1]
    for at, row in enumerate(rows):
        rows_ref[at : at + 1] = jnp.broadcast_to(row, (1, lanes))


def pair_step(sc, own, keep, mate, side, cross, after):
    size, lanes = own.shape

    def body(
        sc_ref, own_ref, keep_ref, mate_ref, side_ref, cross_ref, after_ref,
        send_ref, entry_ref, first_ref, total_ref, rows_ref,
    ):
        odd = sc_ref[0] == 1
        upper = (sc_ref[6] & 2) != 0
        mine = (own_ref[...],) + unpack(keep_ref)[1:]
        first, second = ordered(odd, mine, unpack(mate_ref))
        total = joined(first, second)
        other = joined(*ordered(odd, unpack(side_ref), unpack(cross_ref)))
        nothing = (jnp.zeros_like(own_ref), jnp.ones_like(total[1]), jnp.full((1, 1), -1.0, F32))
        entry = gather_level(upper, nothing, other)
        total = joined(*ordered(upper, total, other))
        pack(send_ref, total)
        entry_ref[...], first_ref[...], total_ref[...] = entry[0], first[0], total[0]
        put_rows(rows_ref, entry[1:] + first[1:] + total[1:])

    return call(
        body, (1,),
        [whole((size, lanes))] + [whole(mate.shape)] * 4 + [anywhere()],
        [whole(mate.shape)] + [whole((size, lanes))] * 3 + [whole((8, lanes))],
        [jax.ShapeDtypeStruct(mate.shape, BF16)]
        + [jax.ShapeDtypeStruct((size, lanes), F32)] * 3
        + [jax.ShapeDtypeStruct((8, lanes), F32)],
    )(sc, own, keep, mate, side, cross, after)


def level_step(bit, final, sc, got, entry, first, total, rows, after):
    size, lanes = entry.shape

    def body(
        sc_ref, got_ref, entry_ref, first_ref, total_ref, rows_ref, after_ref,
        send_ref, one_ref, two_ref, three_ref,
    ):
        upper = (sc_ref[6] & bit) != 0
        other = unpack(got_ref)
        old = (entry_ref[...], rows_ref[0:1], rows_ref[1:2, 0:1])
        new = gather_level(upper, old, other)
        if final:
            even = sc_ref[0] == 0
            last_first = rows_ref[3:4, 0:1]
            link = rows_ref[2:3] * (last_first == new[2]).astype(F32)
            reached = first_ref[...] + link * new[0]
            send_ref[...] = jnp.where(even, reached, new[0]).astype(BF16)
            one_ref[...] = jnp.where(even, new[0], reached).astype(BF16)
            two_ref[...] = jnp.broadcast_to(jnp.where(even, new[2], last_first), (8, LANES))
            three_ref[...] = jnp.zeros_like(three_ref)
        else:
            held = (total_ref[...], rows_ref[4:5], rows_ref[5:6, 0:1])
            held = joined(*ordered(upper, held, other))
            pack(send_ref, held)
            one_ref[...] = new[0]
            two_ref[...] = held[0]
            put_rows(three_ref, new[1:] + (rows_ref[2:3], rows_ref[3:4]) + held[1:])

    state = [jax.ShapeDtypeStruct((size, lanes), F32)]
    if final:
        out = [jax.ShapeDtypeStruct((size, lanes), BF16)] * 2 + [jax.ShapeDtypeStruct((8, LANES), F32)] * 2
    else:
        out = [jax.ShapeDtypeStruct(got.shape, BF16)] + state * 2 + [jax.ShapeDtypeStruct((8, lanes), F32)]
    return call(
        body, (1,),
        [whole(got.shape)] + [whole((size, lanes))] * 3 + [whole((8, lanes)), anywhere()],
        [whole(o.shape) for o in out],
        out,
    )(sc, got, entry, first, total, rows, after)


def local_part(which, heads, width, sc, x, gate, read, write, ccol, arow, tail, skip, after):
    toks = write.shape[0]
    half_w = x.shape[1] // 2
    half_h = heads // 2
    per = LANES // width
    tiles = half_w // LANES
    blocks = toks // GROUP
    strip = 64

    def body(
        sc_ref, x_ref, gate_ref, rd_ref, wr_ref, ccol_ref, arow_ref, tail0_ref, skip_ref, after_ref,
        a_ref, b_ref, scores, mix,
    ):
        i = pl.program_id(0)
        seg_col = ccol_ref[0, :, SEG_LANE : SEG_LANE + 1]

        @pl.when(i == 0)
        def _():
            mix[...] = jnp.zeros_like(mix)
            for b in range(blocks):
                rows = slice(b * GROUP, (b + 1) * GROUP)
                s = dot(rd_ref[rows], wr_ref[rows], ((1,), (1,)))
                causal = lax.broadcasted_iota(jnp.int32, (GROUP, GROUP), 0) >= lax.broadcasted_iota(
                    jnp.int32, (GROUP, GROUP), 1
                )
                same = seg_col[rows] == arow_ref[SEG_LANE : SEG_LANE + 1, rows]
                scores[b] = jnp.where(causal & same, s, 0.0)

        turn = lax.rem(LANES - per * i, LANES)
        cr = pltpu.roll(ccol_ref[0], turn, 1)
        tr = pltpu.roll(tail0_ref[0], turn, 1)
        gains = skip_ref[0, 0:1, :]
        lane = lane_iota(GROUP)
        head0 = sc_ref[which] * half_h + per * i
        carry = None
        start = jnp.ones((1, LANES), F32)
        for b in range(blocks):
            rows = slice(b * GROUP, (b + 1) * GROUP)
            xb = x_ref[rows]
            logs = []
            for k in range(per):
                cb = jnp.broadcast_to(cr[rows, k : k + 1], (GROUP, LANES))
                logs.append(cb)
                ar = arow_ref[pl.ds(head0 + k, 1), rows]
                for low in range(0, GROUP, strip):
                    for left in range(0, min(low + strip, GROUP), LANES):
                        part = jnp.exp2(jnp.minimum(cb[low : low + strip] - ar[:, left : left + LANES], 60.0))
                        part = part * scores[b, low : low + strip, left : left + LANES]
                        mix[b, k * GROUP + low : k * GROUP + low + strip, left : left + LANES] = part.astype(BF16)
            both = dot(mix[b], xb)
            inner, dec_log = both[0:GROUP], logs[0]
            for k in range(1, per):
                inner = jnp.where(lane < k * width, inner, both[k * GROUP : (k + 1) * GROUP])
                dec_log = jnp.where(lane < k * width, dec_log, logs[k])
            dec = jnp.exp2(dec_log)
            xf = xb.astype(F32)
            y = inner + gains * xf
            if b == 1:
                linked = seg_col[rows] == seg_col[GROUP - 1 : GROUP]
                rm = jnp.where(linked, rd_ref[rows].astype(F32), 0.0).astype(BF16)
                y = y + (dot(rm, carry[0]) + dot(rm, carry[1])) * dec
            else:
                xs = (xf * spread(tr, 0, width)).astype(BF16)
                s0 = dot(wr_ref[rows], xs, ((0,), (0,)))
                s0h = s0.astype(BF16)
                carry = (s0h, (s0 - s0h.astype(F32)).astype(BF16))
            v = gate_ref[rows].astype(F32)
            sg = v / (1.0 + jnp.exp(-v))
            a_ref[rows] = sg * y
            b_ref[rows] = sg * (dec * start)
            start = start * dec[GROUP - 1 : GROUP]

    tile = pl.BlockSpec((toks, LANES), lambda i, sc: (0, sc[which] * tiles + i))
    out = pl.BlockSpec((toks, LANES), lambda i, sc: (0, i))
    return call(
        body, (tiles,),
        [
            tile, tile, whole(read.shape), whole(write.shape),
            pl.BlockSpec((1, toks, LANES), lambda i, sc: (sc[which], 0, 0)),
            whole(arow.shape),
            pl.BlockSpec((1, GROUP, LANES), lambda i, sc: (sc[which], 0, 0)),
            pl.BlockSpec((1, 8, LANES), lambda i, sc: (sc[which], 0, i)),
            anywhere(),
        ],
        [out, out],
        [jax.ShapeDtypeStruct((toks, half_w), F32), jax.ShapeDtypeStruct((toks, half_w), F32)],
        [pltpu.VMEM((blocks, GROUP, GROUP), F32), pltpu.VMEM((blocks, per * GROUP, GROUP), BF16)],
        cost=4_000_000_000,
    )(sc, x, gate, read, write, ccol, arow, tail, skip, after)


def gated_tile(prev_ref, rd_ref, seg_ref, a_ref, b_ref, e_ref, gain_ref):
    linked = seg_ref[0, :, SEG_LANE : SEG_LANE + 1] == prev_ref[0:1, 0:1]
    rm = jnp.where(linked, rd_ref[...].astype(F32), 0.0).astype(BF16)
    gated = a_ref[...] + b_ref[...] * dot(rm, e_ref[...])
    sq = gated * gated
    part = sq[:, 0:LANES]
    for i in range(1, sq.shape[1] // LANES):
        part = part + sq[:, i * LANES : (i + 1) * LANES]
    squares = jnp.sum(jnp.transpose(part), axis=0, keepdims=True)
    return (gated * gain_ref[...]).astype(BF16), squares


def gate_specs(which, toks, half_w, state):
    return [
        whole((8, LANES)), whole((toks, state)),
        pl.BlockSpec((1, toks, LANES), lambda i, sc: (0, 0, 0)),
        whole((toks, half_w)), whole((toks, half_w)), whole((state, half_w)),
        pl.BlockSpec((1, half_w), lambda i, sc: (0, sc[which])),
    ]


def gated_half(which, sc, prev, read, ccol, a, b, e, gain):
    toks, half_w = a.shape

    def body(sc_ref, prev_ref, rd_ref, seg_ref, a_ref, b_ref, e_ref, gain_ref, g_ref, s_ref):
        g_ref[...], s_ref[...] = gated_tile(prev_ref, rd_ref, seg_ref, a_ref, b_ref, e_ref, gain_ref)

    return call(
        body, (1,),
        gate_specs(which, toks, half_w, read.shape[1]),
        [whole((toks, half_w)), whole((1, toks))],
        [jax.ShapeDtypeStruct((toks, half_w), BF16), jax.ShapeDtypeStruct((1, toks), F32)],
        cost=1_000_000_000,
    )(sc, prev, read, ccol, a, b, e, gain)


def weight_block(sc_ref, quarter, w_hbm, w_ref, sems):
    half_w, cols = w_ref.shape[1:]
    copies = []
    for at in range(2):
        rows = pl.ds(pl.multiple_of(sc_ref[at] * half_w, LANES), half_w)
        columns = pl.ds(pl.multiple_of(sc_ref[quarter] * cols, LANES), cols)
        copies.append(pltpu.make_async_copy(w_hbm.at[rows, columns], w_ref.at[at], sems.at[at]))
        copies[-1].start()
    return copies


def gate_and_project(which, quarter, sc, prev, read, ccol, a, b, e, gain, g_keep, weight):
    toks, half_w = a.shape
    cols = weight.shape[1] // 4

    def body(
        sc_ref, prev_ref, rd_ref, seg_ref, a_ref, b_ref, e_ref, gain_ref, gk_ref, w_hbm,
        g_ref, s_ref, y_ref, w_ref, sems,
    ):
        copies = weight_block(sc_ref, quarter, w_hbm, w_ref, sems)
        g, s_ref[...] = gated_tile(prev_ref, rd_ref, seg_ref, a_ref, b_ref, e_ref, gain_ref)
        g_ref[...] = g
        copies[0].wait()
        y = dot(gk_ref[...], w_ref[0])
        copies[1].wait()
        y = y + dot(g, w_ref[1])
        y_ref[...] = jnp.transpose(y).astype(BF16)

    return call(
        body, (1,),
        gate_specs(which, toks, half_w, read.shape[1]) + [whole((toks, half_w)), anywhere()],
        [whole((toks, half_w)), whole((1, toks)), whole((cols, toks))],
        [
            jax.ShapeDtypeStruct((toks, half_w), BF16),
            jax.ShapeDtypeStruct((1, toks), F32),
            jax.ShapeDtypeStruct((cols, toks), BF16),
        ],
        [pltpu.VMEM((2, half_w, cols), BF16), pltpu.SemaphoreType.DMA((2,))],
        cost=1_000_000_000,
    )(sc, prev, read, ccol, a, b, e, gain, g_keep, weight)


def project(quarter, dtype, sc, g_keep, g_other, weight, after):
    toks, half_w = g_keep.shape
    cols = weight.shape[1] // 4

    def body(sc_ref, gk_ref, go_ref, w_hbm, after_ref, y_ref, w_ref, sems):
        copies = weight_block(sc_ref, quarter, w_hbm, w_ref, sems)
        copies[0].wait()
        y = dot(gk_ref[...], w_ref[0])
        copies[1].wait()
        y = y + dot(go_ref[...], w_ref[1])
        y_ref[...] = jnp.transpose(y).astype(dtype)

    return call(
        body, (1,),
        [whole((toks, half_w)), whole((toks, half_w)), anywhere(), anywhere()],
        whole((cols, toks)),
        jax.ShapeDtypeStruct((cols, toks), dtype),
        [pltpu.VMEM((2, half_w, cols), BF16), pltpu.SemaphoreType.DMA((2,))],
        cost=1_000_000,
    )(sc, g_keep, g_other, weight, after)


def on_device(
    n_seq, n_tp, head_input, gate_input, write_vecs, read_vecs, step_raw, segment_ids,
    decay_log, step_bias, skip_gain, norm_gain, out_weight,
):
    heads = decay_log.shape[0]
    toks, feats = head_input.shape
    width = feats // heads
    place = lax.axis_index("seq")
    rank = lax.axis_index("tp")
    odd = lax.rem(place, 2)
    near, far = rank ^ 1, rank ^ 2
    sc = jnp.stack([odd, 1 - odd, far ^ 1, far, near, rank, place]).astype(jnp.int32)

    def swap(a, bit):
        return lax.ppermute(a, "seq", [(i, i ^ bit) for i in range(n_seq)])

    def across(a, bit):
        return lax.ppermute(a, "tp", [(i, i ^ bit) for i in range(n_tp)])

    send_other, send_keep, own, ccol, arow, tail, skip = prepare(
        heads, width, step_raw, segment_ids.reshape(1, toks), decay_log.reshape(1, heads),
        step_bias.reshape(1, heads), skip_gain.reshape(1, heads), head_input, write_vecs,
    )
    mate = swap(send_other, 1)
    cross = swap(send_other, 3)
    side = swap(send_keep, 2)
    shared = (head_input, gate_input, read_vecs, write_vecs, ccol, arow, tail, skip)
    a_keep, b_keep = local_part(0, heads, width, sc, *shared, send_keep)
    sent, entry, first, total, rows = pair_step(sc, own, send_keep, mate, side, cross, a_keep)
    a_other, b_other = local_part(1, heads, width, sc, *shared, sent)
    bit = 4
    while 2 * bit < n_seq:
        sent, entry, total, rows = level_step(
            bit, False, sc, swap(sent, bit), entry, first, total, rows, a_other
        )
        bit *= 2
    sent, e_keep, prev, _ = level_step(bit, True, sc, swap(sent, bit), entry, first, total, rows, a_other)
    e_other = swap(sent, 1)
    gain = norm_gain.reshape(1, feats)
    g_keep, s_keep = gated_half(0, sc, prev, read_vecs, ccol, a_keep, b_keep, e_keep, gain)
    g_other, s_other, y_far_near = gate_and_project(
        1, 2, sc, prev, read_vecs, ccol, a_other, b_other, e_other, gain, g_keep, out_weight
    )
    got_far = across(y_far_near, 1)
    squares = s_keep + s_other
    squares = squares + across(squares, 1)
    y_far = project(3, F32, sc, g_keep, g_other, out_weight, y_far_near)
    to_far = (y_far + got_far.astype(F32)).astype(BF16)
    got_x = across(to_far, 2)
    squares = squares + across(squares, 2)
    got_near = across(project(4, BF16, sc, g_keep, g_other, out_weight, to_far), 1)
    y_own = project(5, F32, sc, g_keep, g_other, out_weight, to_far)
    inv = lax.rsqrt(squares / (feats * n_tp) + EPS)
    out = (y_own + got_near.astype(F32)) + got_x.astype(F32)
    return (out * inv).astype(BF16)


def solution(mesh):
    in_specs = (
        P("seq", "tp"),
        P("seq", "tp"),
        P("seq", None),
        P("seq", None),
        P("tp", "seq"),
        P("seq"),
        P("tp"),
        P("tp"),
        P("tp"),
        P("tp"),
        P("tp", None),
    )
    out_specs = P("tp", "seq")
    return jax.shard_map(
        functools.partial(on_device, mesh.shape["seq"], mesh.shape["tp"]),
        mesh=mesh, in_specs=in_specs, out_specs=out_specs, check_vma=False,
    )
```

```python
import functools

import jax
import jax.numpy as jnp
from jax import lax
from jax.experimental import pallas as pl
from jax.experimental.pallas import tpu as pltpu
from jax.sharding import PartitionSpec as P

GROUP = 256
LANES = 128
EPS = 1e-05
LOG2E = 1.4426950408889634
SEG_LANE = 24
EXTRA = 16
VMEM = 16 * 1024 * 1024
VMEM_ALL = 56 * 1024 * 1024
F32 = jnp.float32
BF16 = jnp.bfloat16


def dot(a, b, dims=((1,), (0,))):
    return lax.dot_general(a, b, (dims, ((), ())), preferred_element_type=F32)


def lane_iota(rows):
    return lax.broadcasted_iota(jnp.int32, (rows, LANES), 1)


def spread(cols, first, width):
    rows = cols.shape[0]
    per = LANES // width
    lane = lane_iota(rows)
    out = jnp.broadcast_to(cols[:, first : first + 1], (rows, LANES))
    for k in range(1, per):
        nxt = jnp.broadcast_to(cols[:, first + k : first + k + 1], (rows, LANES))
        out = jnp.where(lane < k * width, out, nxt)
    return out


def call(body, sc, args, out_shape, scratch=(), cost=0, after=None):
    vm = pl.BlockSpec(memory_space=pltpu.VMEM)
    specs = [pl.BlockSpec(memory_space=pltpu.SMEM)] + [vm] * len(args)
    operands = [sc, *args]
    kernel = body
    if after is not None:
        specs.append(pl.BlockSpec(memory_space=pl.ANY))
        operands.append(after)
        at = len(operands) - 1

        def kernel(*refs):
            body(*refs[:at], *refs[at + 1 :])

    return pl.pallas_call(
        kernel,
        in_specs=specs,
        out_specs=jax.tree.map(lambda _: vm, out_shape),
        out_shape=out_shape,
        scratch_shapes=list(scratch),
        compiler_params=pltpu.CompilerParams(vmem_limit_bytes=VMEM),
        cost_estimate=pl.CostEstimate(flops=cost, bytes_accessed=1000, transcendentals=0),
    )(*operands)


def shaped(*shapes):
    return [jax.ShapeDtypeStruct(shape, dtype) for shape, dtype in shapes]


def pack(out_ref, total):
    state, through, last = total
    size, lanes = state.shape
    high = through.astype(BF16).astype(F32)
    row = lax.broadcasted_iota(jnp.int32, (EXTRA, lanes), 0)
    rows = jnp.where(row == 0, high, jnp.where(row == 1, through - high, last))
    out_ref[0:size] = state.astype(BF16)
    out_ref[size : size + EXTRA] = rows.astype(BF16)


def unpack(ref):
    size = ref.shape[0] - EXTRA
    rows = ref[size : size + EXTRA].astype(F32)
    return ref[0:size].astype(F32), rows[0:1] + rows[1:2], rows[2:3, 0:1]


def merged(swapped, one, two):
    later = jnp.where(swapped, one[1], two[1])
    link = later * (one[2] == two[2]).astype(F32)
    state = jnp.where(swapped, 1.0, link) * one[0] + jnp.where(swapped, link, 1.0) * two[0]
    return state, one[1] * two[1], jnp.where(swapped, one[2], two[2])


def ordered(swapped, one, two):
    firsts = tuple(jnp.where(swapped, t, o) for o, t in zip(one, two))
    seconds = tuple(jnp.where(swapped, o, t) for o, t in zip(one, two))
    return firsts, seconds


def stash_rows(state):
    return slice(0, state), slice(state + 8, state + 40), slice(state + 40, state + 72)


def put_rows(rows_ref, rows):
    lanes = rows_ref.shape[1]
    for at, row in enumerate(rows):
        rows_ref[at : at + 1] = jnp.broadcast_to(row, (1, lanes))


def prepare(heads, width, raw, seg, decay_log, bias, x, write):
    toks, state = write.shape
    half_w = x.shape[1] // 2
    half_h = heads // 2
    blocks = toks // GROUP
    arrays = (raw, seg, decay_log, bias, write, x)

    def body(*refs):
        hbm, (other_ref, keep_ref, stash_ref) = refs[: len(arrays)], refs[len(arrays) : -10]
        raw_ref, seg_ref, dl_ref, sb_ref, wr_ref, x_ref, rows, pad, cols, sems = refs[-10:]
        copies = [
            pltpu.make_async_copy(src, dst, sems.at[k])
            for k, (src, dst) in enumerate(zip(hbm, (raw_ref, seg_ref, dl_ref, sb_ref, wr_ref, x_ref)))
        ]
        for copy in copies:
            copy.start()
        rows[...] = jnp.zeros_like(rows)
        pad[...] = jnp.zeros_like(pad)
        tri = (
            lax.broadcasted_iota(jnp.int32, (GROUP, GROUP), 0)
            <= lax.broadcasted_iota(jnp.int32, (GROUP, GROUP), 1)
        ).astype(BF16)
        for copy in copies[:4]:
            copy.wait()
        rows[0:1, 0:heads] = dl_ref[...]
        rows[1:2, 0:heads] = sb_ref[...]
        pad[0:heads] = raw_ref[...].astype(F32)
        params = jnp.transpose(rows[...])[0:32]
        z = pad[0:32] + params[:, 1:2]
        step = jnp.maximum(z, 0.0) + jnp.log1p(jnp.exp(-jnp.abs(z)))
        rate = -jnp.exp(params[:, 0:1]) * step
        cum, full = [], []
        base = jnp.zeros((32, 1), F32)
        for b in range(blocks):
            r = rate[:, b * GROUP : (b + 1) * GROUP]
            r1 = r.astype(BF16)
            d1 = r - r1.astype(F32)
            r2 = d1.astype(BF16)
            r3 = (d1 - r2.astype(F32)).astype(BF16)
            c = dot(r1, tri) + (dot(r2, tri) + dot(r3, tri))
            cum.append(c)
            full.append(c + base)
            base = base + c[:, GROUP - 1 : GROUP]
        seg_row = seg_ref[...].astype(F32)
        last = seg_row[:, toks - 1 : toks]
        tail = jnp.exp(base - jnp.concatenate(full, axis=1)) * step
        pad[0:32] = jnp.where(seg_row == last, tail, 0.0)
        own_rows, cum_rows, step_rows = stash_rows(state)
        stash_ref[cum_rows, 0:toks] = jnp.concatenate(cum, axis=1)
        stash_ref[cum_rows.start + SEG_LANE : cum_rows.start + SEG_LANE + 1, 0:toks] = seg_row
        stash_ref[step_rows, 0:toks] = step
        cols[...] = jnp.transpose(pad[...])
        rows[...] = jnp.zeros_like(rows)
        rows[0:32] = jnp.broadcast_to(jnp.exp(base), (32, LANES))
        keep = jnp.transpose(rows[...])[0:1]
        per = LANES // width
        odd = lax.rem(lax.axis_index("seq"), 2) == 1
        for copy in copies[4:]:
            copy.wait()
        halves = []
        for j in range(2):
            parts, through = [], []
            for i in range(half_w // LANES):
                at = j * half_h + i * per
                xt = x_ref[:, j * half_w + i * LANES : j * half_w + (i + 1) * LANES].astype(F32)
                parts.append((xt * spread(cols[...], at, width)).astype(BF16))
                through.append(spread(keep, at, width))
            own = dot(wr_ref[...], jnp.concatenate(parts, axis=1), ((0,), (0,)))
            halves.append((own, jnp.concatenate(through, axis=1), last))
        mine, other = ordered(odd, *halves)
        stash_ref[own_rows] = mine[0]
        put_rows(stash_ref.at[state : state + 8], mine[1:])
        pack(keep_ref, mine)
        pack(other_ref, other)

    vm = pl.BlockSpec(memory_space=pltpu.VMEM)
    out_shape = shaped(
        ((state + EXTRA, half_w), BF16), ((state + EXTRA, half_w), BF16),
        ((stash_rows(state)[2].stop, max(half_w, toks)), F32),
    )
    return pl.pallas_call(
        body,
        in_specs=[pl.BlockSpec(memory_space=pltpu.HBM)] * len(arrays),
        out_specs=[vm] * len(out_shape),
        out_shape=out_shape,
        scratch_shapes=[
            *[pltpu.VMEM(a.shape, a.dtype) for a in arrays],
            pltpu.VMEM((LANES, LANES), F32), pltpu.VMEM((LANES, toks), F32), pltpu.VMEM((toks, LANES), F32),
            pltpu.SemaphoreType.DMA((len(arrays),)),
        ],
        compiler_params=pltpu.CompilerParams(vmem_limit_bytes=VMEM_ALL),
        cost_estimate=pl.CostEstimate(flops=4_000_000_000, bytes_accessed=1000, transcendentals=0),
    )(*arrays)


def gather_level(upper, entry, other):
    state, through, last_id = entry
    link = through * ((last_id < 0) | (other[2] == last_id)).astype(F32)
    state = state + jnp.where(upper, link, 0.0) * other[0]
    last_id = jnp.where(upper & (last_id < 0), other[2], last_id)
    return state, through * jnp.where(upper, other[1], 1.0), last_id


def pair_step(sc, stash, mate, side, cross, after):
    size, lanes = mate.shape[0] - EXTRA, mate.shape[1]

    def body(
        sc_ref, stash_ref, mate_ref, side_ref, cross_ref, send_ref, entry_ref, first_ref, total_ref, rows_ref
    ):
        odd = sc_ref[0] == 1
        upper = (sc_ref[6] & 2) != 0
        mine = (
            stash_ref[0:size, 0:lanes], stash_ref[size : size + 1, 0:lanes], stash_ref[size + 1 : size + 2, 0:1]
        )
        mate = unpack(mate_ref)
        total = merged(odd, mine, mate)
        other = merged(odd, unpack(side_ref), unpack(cross_ref))
        nothing = (0.0, jnp.ones_like(total[1]), jnp.full((1, 1), -1.0, F32))
        entry = gather_level(upper, nothing, other)
        total = merged(upper, total, other)
        pack(send_ref, total)
        entry_ref[...], total_ref[...] = entry[0], total[0]
        first_ref[...] = jnp.where(odd, mate[0], mine[0])
        rows = tuple(jnp.where(odd, m, o) for o, m in zip(mine[1:], mate[1:]))
        put_rows(rows_ref, entry[1:] + rows + total[1:])

    state = ((size, lanes), F32)
    return call(
        body, sc, (stash, mate, side, cross),
        shaped((mate.shape, BF16), state, state, state, ((8, lanes), F32)), after=after,
    )


def level_step(bit, final, sc, got, entry, first, total, rows, after):
    size, lanes = entry.shape

    def body(
        sc_ref, got_ref, entry_ref, first_ref, total_ref, rows_ref,
        send_ref, one_ref, two_ref, three_ref,
    ):
        upper = (sc_ref[6] & bit) != 0
        other = unpack(got_ref)
        old = (entry_ref[...], rows_ref[0:1], rows_ref[1:2, 0:1])
        new = gather_level(upper, old, other)
        if final:
            even = sc_ref[0] == 0
            last_first = rows_ref[3:4, 0:1]
            link = rows_ref[2:3] * (last_first == new[2]).astype(F32)
            reached = first_ref[...] + link * new[0]
            send_ref[...] = jnp.where(even, reached, new[0]).astype(BF16)
            one_ref[...] = jnp.where(even, new[0], reached).astype(BF16)
            two_ref[...] = jnp.broadcast_to(jnp.where(even, new[2], last_first), (8, LANES))
            three_ref[...] = jnp.zeros_like(three_ref)
        else:
            held = (total_ref[...], rows_ref[4:5], rows_ref[5:6, 0:1])
            held = merged(upper, held, other)
            pack(send_ref, held)
            one_ref[...] = new[0]
            two_ref[...] = held[0]
            put_rows(three_ref, new[1:] + (rows_ref[2:3], rows_ref[3:4]) + held[1:])

    if final:
        out = shaped(((size, lanes), BF16), ((size, lanes), BF16), ((8, LANES), F32), ((8, LANES), F32))
    else:
        out = shaped((got.shape, BF16), ((size, lanes), F32), ((size, lanes), F32), ((8, lanes), F32))
    return call(body, sc, (got, entry, first, total, rows), out, after=after)


def local_part(heads, width, sc, x, gate, read, write, stash, skip, after):
    toks = write.shape[0]
    feats = x.shape[1]
    per = LANES // width
    blocks = toks // GROUP
    strip = 64

    def body(
        sc_ref, x_ref, gate_ref, rd_ref, wr_ref, stash_ref, skip_ref,
        a_ref, b_ref, log_cum, scores, mix, pad, tails, rows_ref,
    ):
        _, cum_rows, step_rows = stash_rows(write.shape[1])
        cum_ref = stash_ref.at[cum_rows, 0:toks]
        step_ref = stash_ref.at[step_rows, 0:toks]
        lane = lane_iota(GROUP)
        mix[...] = jnp.zeros_like(mix)
        pad[...] = jnp.zeros_like(pad)
        rows_ref[...] = jnp.zeros_like(rows_ref)
        rows_ref[0:1, 0:heads] = skip_ref[...]
        skips = rows_ref[0:1]
        seg_row = cum_ref[SEG_LANE : SEG_LANE + 1]
        log_row = cum_ref[...] * LOG2E - jnp.log(step_ref[...]) * LOG2E
        pad[0:32] = cum_ref[...] * LOG2E
        pad[SEG_LANE : SEG_LANE + 1] = seg_row
        log_cum[...] = jnp.transpose(pad[...])
        seg_col = log_cum[:, SEG_LANE : SEG_LANE + 1]
        tail0 = jnp.exp(cum_ref[:, GROUP - 1 : GROUP] - cum_ref[:, 0:GROUP]) * step_ref[:, 0:GROUP]
        same = seg_row[:, 0:GROUP] == seg_row[:, GROUP - 1 : GROUP]
        pad[0:32, 0:GROUP] = jnp.where(same, tail0, 0.0)
        tails[...] = jnp.transpose(pad[:, 0:GROUP])
        masked = []
        for b in range(blocks):
            rows = slice(b * GROUP, (b + 1) * GROUP)
            s = dot(rd_ref[rows], wr_ref[rows], ((1,), (1,)))
            causal = lax.broadcasted_iota(jnp.int32, (GROUP, GROUP), 0) >= lax.broadcasted_iota(
                jnp.int32, (GROUP, GROUP), 1
            )
            scores[b] = jnp.where(causal & (seg_col[rows] == seg_row[:, rows]), s, 0.0)
            linked = seg_col[rows] == seg_col[b * GROUP - 1 : b * GROUP] if b else None
            masked.append(jnp.where(linked, rd_ref[rows].astype(F32), 0.0).astype(BF16) if b else None)
        for i in range(feats // LANES):
            tile = slice(i * LANES, (i + 1) * LANES)
            gains = spread(skips, i * per, width)
            carry = None
            start = jnp.ones((1, LANES), F32)
            for b in range(blocks):
                rows = slice(b * GROUP, (b + 1) * GROUP)
                slot = (i * blocks + b) % mix.shape[0]
                xb = x_ref[rows, tile]
                logs = []
                for k in range(per):
                    head = i * per + k
                    cb = jnp.broadcast_to(log_cum[rows, head : head + 1], (GROUP, LANES))
                    logs.append(cb)
                    ar = log_row[head : head + 1, rows]
                    for low in range(0, GROUP, strip):
                        for left in range(0, min(low + strip, GROUP), LANES):
                            gap = cb[low : low + strip] - ar[:, left : left + LANES]
                            part = jnp.exp2(jnp.minimum(gap, 60.0))
                            part = part * scores[b, low : low + strip, left : left + LANES]
                            at = k * GROUP + low
                            mix[slot, at : at + strip, left : left + LANES] = part.astype(BF16)
                both = dot(mix[slot], xb)
                inner, dec_log = both[0:GROUP], logs[0]
                for k in range(1, per):
                    inner = jnp.where(lane < k * width, inner, both[k * GROUP : (k + 1) * GROUP])
                    dec_log = jnp.where(lane < k * width, dec_log, logs[k])
                dec = jnp.exp2(dec_log)
                xf = xb.astype(F32)
                y = inner + gains * xf
                if b == 1:
                    y = y + (dot(masked[b], carry[0]) + dot(masked[b], carry[1])) * dec
                else:
                    xs = (xf * spread(tails[...], i * per, width)).astype(BF16)
                    s0 = dot(wr_ref[rows], xs, ((0,), (0,)))
                    s0h = s0.astype(BF16)
                    carry = (s0h, (s0 - s0h.astype(F32)).astype(BF16))
                v = gate_ref[rows, tile].astype(F32)
                sg = v / (1.0 + jnp.exp(-v))
                a_ref[rows, tile] = sg * y
                b_ref[rows, tile] = sg * (dec * start)
                start = start * dec[GROUP - 1 : GROUP]

    return call(
        body, sc, (x, gate, read, write, stash, skip),
        shaped(((toks, feats), F32), ((toks, feats), F32), ((toks, LANES), F32)),
        [
            pltpu.VMEM((blocks, GROUP, GROUP), F32), pltpu.VMEM((4, per * GROUP, GROUP), BF16),
            pltpu.VMEM((LANES, toks), F32), pltpu.VMEM((GROUP, LANES), F32), pltpu.VMEM((8, LANES), F32),
        ],
        cost=8_000_000_000, after=after,
    )


def gated_tile(which, sc_ref, prev_ref, rd_ref, cum_ref, a_ref, b_ref, e_ref, gain_ref):
    half_w = e_ref.shape[1]
    here = pl.ds(pl.multiple_of(sc_ref[which] * half_w, LANES), half_w)
    linked = cum_ref[:, SEG_LANE : SEG_LANE + 1] == prev_ref[0:1, 0:1]
    rm = jnp.where(linked, rd_ref[...].astype(F32), 0.0).astype(BF16)
    gated = a_ref[:, here] + b_ref[:, here] * dot(rm, e_ref[...])
    sq = gated * gated
    part = sq[:, 0:LANES]
    for i in range(1, half_w // LANES):
        part = part + sq[:, i * LANES : (i + 1) * LANES]
    squares = jnp.sum(jnp.transpose(part), axis=0, keepdims=True)
    return (gated * gain_ref[:, here]).astype(BF16), squares


def projected(which, quarter, sc_ref, w_ref, g):
    half_w = g.shape[1]
    cols = w_ref.shape[1] // 4
    rows = pl.ds(pl.multiple_of(sc_ref[which] * half_w, LANES), half_w)
    columns = pl.ds(pl.multiple_of(sc_ref[quarter] * cols, LANES), cols)
    return dot(w_ref[rows, columns], g, ((0,), (1,)))


def put_squares(out_ref, size, squares):
    high = squares.astype(BF16).astype(F32)
    middle = (squares - high).astype(BF16).astype(F32)
    row = lax.broadcasted_iota(jnp.int32, (EXTRA, squares.shape[1]), 0)
    rows = jnp.where(row == 0, high, jnp.where(row == 1, middle, squares - high - middle))
    out_ref[size : size + EXTRA] = rows.astype(BF16)


def get_squares(ref):
    rows = ref[ref.shape[0] - EXTRA :].astype(F32)
    return rows[0:1] + (rows[1:2] + rows[2:3])


def gated_first(sc, prev, read, cum, a, b, e, gain, weight):
    toks = a.shape[0]
    half_w = e.shape[1]
    feats = weight.shape[1]

    def body(
        sc_ref, prev_ref, rd_ref, cum_ref, a_ref, b_ref, e_ref, gain_ref, w_ref, g_ref, s_ref, y_ref
    ):
        g, s_ref[...] = gated_tile(0, sc_ref, prev_ref, rd_ref, cum_ref, a_ref, b_ref, e_ref, gain_ref)
        g_ref[...] = g
        for quarter in range(4):
            y_ref[quarter] = projected(0, 2 + quarter, sc_ref, w_ref, g)

    return call(
        body, sc, (prev, read, cum, a, b, e, gain, weight),
        shaped(((toks, half_w), BF16), ((1, toks), F32), ((4, feats // 4, toks), F32)),
        cost=2_000_000_000,
    )


def gated_second(sc, prev, read, cum, a, b, e, gain, partial, s_first, weight):
    toks = a.shape[0]
    half_w = e.shape[1]
    cols = weight.shape[1] // 4

    def body(
        sc_ref, prev_ref, rd_ref, cum_ref, a_ref, b_ref, e_ref, gain_ref, p_ref, sf_ref, w_ref, g_ref, y_ref
    ):
        g, squares = gated_tile(1, sc_ref, prev_ref, rd_ref, cum_ref, a_ref, b_ref, e_ref, gain_ref)
        g_ref[...] = g
        y_ref[0:cols] = (p_ref[0] + projected(1, 2, sc_ref, w_ref, g)).astype(BF16)
        put_squares(y_ref, cols, sf_ref[...] + squares)

    return call(
        body, sc, (prev, read, cum, a, b, e, gain, partial, s_first, weight),
        shaped(((toks, half_w), BF16), ((cols + EXTRA, toks), BF16)), cost=1_000_000_000,
    )


def project_rest(quarter, dtype, cost, sc, g, partial, weight, after, add=None):
    toks = g.shape[0]
    block = (weight.shape[1] // 4, toks)

    def body(sc_ref, g_ref, p_ref, w_ref, *refs):
        y = p_ref[quarter] + projected(1, 2 + quarter, sc_ref, w_ref, g_ref[...])
        if add is not None:
            y = y + refs[0][...].astype(F32)
        refs[-1][...] = y.astype(dtype)

    more = () if add is None else (add,)
    return call(
        body, sc, (g, partial, weight, *more), jax.ShapeDtypeStruct(block, dtype), cost=cost, after=after
    )


def add_far(sc, y_far, to_near, got_near):
    size = y_far.shape[0]

    def body(sc_ref, y_ref, mine_ref, got_ref, out_ref):
        out_ref[0:size] = (y_ref[...] + got_ref[0:size].astype(F32)).astype(BF16)
        put_squares(out_ref, size, get_squares(mine_ref) + get_squares(got_ref))

    return call(body, sc, (y_far, to_near, got_near), jax.ShapeDtypeStruct(got_near.shape, BF16))


def finish(features, sc, y_own, to_far, got_far):
    size = y_own.shape[0]

    def body(sc_ref, own_ref, mine_ref, far_ref, out_ref):
        inv = lax.rsqrt((get_squares(mine_ref) + get_squares(far_ref)) / features + EPS)
        out_ref[...] = ((own_ref[...] + far_ref[0:size].astype(F32)) * inv).astype(BF16)

    return call(body, sc, (y_own, to_far, got_far), jax.ShapeDtypeStruct(y_own.shape, BF16))


def on_device(
    n_seq, n_tp, head_input, gate_input, write_vecs, read_vecs, step_raw, segment_ids,
    decay_log, step_bias, skip_gain, norm_gain, out_weight,
):
    heads = decay_log.shape[0]
    toks, feats = head_input.shape
    width = feats // heads
    place = lax.axis_index("seq")
    rank = lax.axis_index("tp")
    odd = lax.rem(place, 2)
    near, far = rank ^ 1, rank ^ 2
    sc = jnp.stack([odd, 1 - odd, far ^ 1, far, near, rank, place]).astype(jnp.int32)

    def swap(a, bit):
        return lax.ppermute(a, "seq", [(i, i ^ bit) for i in range(n_seq)])

    def across(a, bit):
        return lax.ppermute(a, "tp", [(i, i ^ bit) for i in range(n_tp)])

    send_other, send_keep, stash = prepare(
        heads, width, step_raw, segment_ids.reshape(1, toks), decay_log.reshape(1, heads),
        step_bias.reshape(1, heads), head_input, write_vecs,
    )
    side = swap(send_keep, 2)
    cross = swap(send_other, 3)
    mate = swap(send_other, 1)
    a, b, log_cum = local_part(
        heads, width, sc, head_input, gate_input, read_vecs, write_vecs, stash,
        skip_gain.reshape(1, heads), None,
    )
    sent, entry, first, total, rows = pair_step(sc, stash, mate, side, cross, a)
    bit = 4
    while 2 * bit < n_seq:
        sent, entry, total, rows = level_step(bit, False, sc, swap(sent, bit), entry, first, total, rows, None)
        bit *= 2
    sent, e_keep, prev, _ = level_step(bit, True, sc, swap(sent, bit), entry, first, total, rows, None)
    e_other = swap(sent, 1)
    gain = norm_gain.reshape(1, feats)
    shared = (prev, read_vecs, log_cum, a, b)
    g_keep, s_keep, partial = gated_first(sc, *shared, e_keep, gain, out_weight)
    g_other, to_near = gated_second(sc, *shared, e_other, gain, partial, s_keep, out_weight)
    got_near = across(to_near, 1)
    y_near = project_rest(2, BF16, 500_000_000, sc, g_other, partial, out_weight, to_near)
    got_own = across(y_near, 1)
    y_far = project_rest(1, F32, 500_000_000, sc, g_other, partial, out_weight, y_near)
    to_far = add_far(sc, y_far, to_near, got_near)
    got_far = across(to_far, 2)
    y_own = project_rest(3, F32, 10_000_000_000, sc, g_other, partial, out_weight, to_far, got_own)
    return finish(feats * n_tp, sc, y_own, to_far, got_far)


def solution(mesh):
    in_specs = (
        P("seq", "tp"),
        P("seq", "tp"),
        P("seq", None),
        P("seq", None),
        P("tp", "seq"),
        P("seq"),
        P("tp"),
        P("tp"),
        P("tp"),
        P("tp"),
        P("tp", None),
    )
    out_specs = P("tp", "seq")
    return jax.shard_map(
        functools.partial(on_device, mesh.shape["seq"], mesh.shape["tp"]),
        mesh=mesh, in_specs=in_specs, out_specs=out_specs, check_vma=False,
    )
```

```python
import functools

import jax
import jax.numpy as jnp
from jax import lax
from jax.experimental import pallas as pl
from jax.experimental.pallas import tpu as pltpu
from jax.sharding import PartitionSpec as P

GROUP = 256
LANES = 128
EPS = 1e-05
LOG2E = 1.4426950408889634
SEG_LANE = 24
EXTRA = 8
VMEM = 16 * 1024 * 1024
VMEM_ALL = 56 * 1024 * 1024
F32 = jnp.float32
BF16 = jnp.bfloat16


def dot(a, b, dims=((1,), (0,))):
    return lax.dot_general(a, b, (dims, ((), ())), preferred_element_type=F32)


def lane_iota(rows):
    return lax.broadcasted_iota(jnp.int32, (rows, LANES), 1)


def spread(cols, first, width):
    rows = cols.shape[0]
    per = LANES // width
    lane = lane_iota(rows)
    out = jnp.broadcast_to(cols[:, first : first + 1], (rows, LANES))
    for k in range(1, per):
        nxt = jnp.broadcast_to(cols[:, first + k : first + k + 1], (rows, LANES))
        out = jnp.where(lane < k * width, out, nxt)
    return out


def position():
    place, rank = lax.axis_index("seq"), lax.axis_index("tp")
    odd = place & 1
    far = rank ^ 2
    return odd, 1 - odd, far ^ 1, far, rank ^ 1, rank, place


def call(body, args, out_shape, scratch=(), cost=0, after=None):
    vm = pl.BlockSpec(memory_space=pltpu.VMEM)
    specs = [vm] * len(args)
    operands = list(args)
    kernel = body
    if after is not None:
        specs.append(pl.BlockSpec(memory_space=pl.ANY))
        operands.append(after)
        at = len(operands) - 1

        def kernel(*refs):
            body(*refs[:at], *refs[at + 1 :])

    return pl.pallas_call(
        kernel,
        in_specs=specs,
        out_specs=jax.tree.map(lambda _: vm, out_shape),
        out_shape=out_shape,
        scratch_shapes=list(scratch),
        compiler_params=pltpu.CompilerParams(vmem_limit_bytes=VMEM),
        cost_estimate=pl.CostEstimate(flops=cost, bytes_accessed=1000, transcendentals=0),
    )(*operands)


def shaped(*shapes):
    return [jax.ShapeDtypeStruct(shape, dtype) for shape, dtype in shapes]


def pack(out_ref, total):
    state, through, last = total
    high = through.astype(BF16).astype(F32)
    row = lax.broadcasted_iota(jnp.int32, (EXTRA, state.shape[1]), 0)
    rows = jnp.where(row == 0, high, jnp.where(row == 1, through - high, last))
    out_ref[...] = jnp.concatenate([state, rows], axis=0).astype(BF16)


def unpack(ref):
    size = ref.shape[0] - EXTRA
    whole = ref[...].astype(F32)
    return whole[0:size], whole[size : size + 1] + whole[size + 1 : size + 2], whole[size + 2 : size + 3]


def merged(swapped, one, two):
    later = jnp.where(swapped, one[1], two[1])
    link = later * (one[2] == two[2]).astype(F32)
    state = jnp.where(swapped, 1.0, link) * one[0] + jnp.where(swapped, link, 1.0) * two[0]
    return state, one[1] * two[1], jnp.where(swapped, one[2], two[2])


def ordered(swapped, one, two):
    firsts = tuple(jnp.where(swapped, t, o) for o, t in zip(one, two))
    seconds = tuple(jnp.where(swapped, o, t) for o, t in zip(one, two))
    return firsts, seconds


def stash_rows():
    return slice(0, 32), slice(32, 64)


def put_rows(rows_ref, rows):
    lanes = rows_ref.shape[1]
    for at, row in enumerate(rows):
        rows_ref[at : at + 1] = jnp.broadcast_to(row, (1, lanes))


def prepare(heads, width, raw, seg, decay_log, bias, x, write):
    toks, state = write.shape
    half_w = x.shape[1] // 2
    half_h = heads // 2
    blocks = toks // GROUP
    arrays = (raw, seg, decay_log, bias, write, x)

    def body(*refs):
        hbm, (other_ref, keep_ref, stash_ref) = refs[: len(arrays)], refs[len(arrays) : -9]
        raw_ref, seg_ref, dl_ref, sb_ref, wr_ref, x_ref, rows, pad, sems = refs[-9:]
        copies = [
            pltpu.make_async_copy(src, dst, sems.at[k])
            for k, (src, dst) in enumerate(zip(hbm, (raw_ref, seg_ref, dl_ref, sb_ref, wr_ref, x_ref)))
        ]
        for copy in copies:
            copy.start()
        rows[...] = jnp.zeros_like(rows)
        pad[...] = jnp.zeros_like(pad)
        tri = (
            lax.broadcasted_iota(jnp.int32, (GROUP, GROUP), 0)
            <= lax.broadcasted_iota(jnp.int32, (GROUP, GROUP), 1)
        ).astype(BF16)
        for copy in copies[:5]:
            copy.wait()
        vecs = jnp.transpose(wr_ref[...].astype(F32))
        rows[0:1, 0:heads] = dl_ref[...]
        rows[1:2, 0:heads] = sb_ref[...]
        pad[0:heads] = raw_ref[...].astype(F32)
        params = jnp.transpose(rows[...])[0:32]
        z = pad[0:32] + params[:, 1:2]
        step = jnp.maximum(z, 0.0) + jnp.log1p(jnp.exp(-jnp.abs(z)))
        rate = -jnp.exp(params[:, 0:1]) * step
        cum, full = [], []
        base = jnp.zeros((32, 1), F32)
        for b in range(blocks):
            r = rate[:, b * GROUP : (b + 1) * GROUP]
            r1 = r.astype(BF16)
            d1 = r - r1.astype(F32)
            r2 = d1.astype(BF16)
            r3 = (d1 - r2.astype(F32)).astype(BF16)
            c = dot(r1, tri) + (dot(r2, tri) + dot(r3, tri))
            cum.append(c)
            full.append(c + base)
            base = base + c[:, GROUP - 1 : GROUP]
        seg_row = seg_ref[...].astype(F32)
        last = seg_row[:, toks - 1 : toks]
        tail = jnp.exp(base - jnp.concatenate(full, axis=1)) * step
        cum_rows, step_rows = stash_rows()
        stash_ref[cum_rows] = jnp.concatenate(cum, axis=1)
        stash_ref[SEG_LANE : SEG_LANE + 1] = seg_row
        stash_ref[step_rows] = step
        tails = jnp.where(seg_row == last, tail, 0.0)
        rows[...] = jnp.zeros_like(rows)
        rows[0:32] = jnp.broadcast_to(jnp.exp(base), (32, LANES))
        keep = jnp.transpose(rows[...])[0:1]
        per = LANES // width
        odd = lax.rem(lax.axis_index("seq"), 2) == 1
        lane = lane_iota(state)
        copies[5].wait()
        halves = []
        for j in range(2):
            own, through = [], []
            for i in range(half_w // LANES):
                at = j * half_h + i * per
                written = [(vecs * tails[at + k : at + k + 1]).astype(BF16) for k in range(per)]
                both = dot(jnp.concatenate(written, axis=0), x_ref[:, j * half_w + i * LANES : j * half_w + (i + 1) * LANES])
                tile = both[0:state]
                for k in range(1, per):
                    tile = jnp.where(lane < k * width, tile, both[k * state : (k + 1) * state])
                own.append(tile)
                through.append(spread(keep, at, width))
            halves.append((jnp.concatenate(own, axis=1), jnp.concatenate(through, axis=1), last))
        mine, other = ordered(odd, *halves)
        pack(keep_ref, mine)
        pack(other_ref, other)

    vm = pl.BlockSpec(memory_space=pltpu.VMEM)
    out_shape = shaped(
        ((state + EXTRA, half_w), BF16), ((state + EXTRA, half_w), BF16), ((stash_rows()[1].stop, toks), F32),
    )
    return pl.pallas_call(
        body,
        in_specs=[pl.BlockSpec(memory_space=pltpu.HBM)] * len(arrays),
        out_specs=[vm] * len(out_shape),
        out_shape=out_shape,
        scratch_shapes=[
            *[pltpu.VMEM(a.shape, a.dtype) for a in arrays],
            pltpu.VMEM((LANES, LANES), F32), pltpu.VMEM((32, toks), F32),
            pltpu.SemaphoreType.DMA((len(arrays),)),
        ],
        compiler_params=pltpu.CompilerParams(vmem_limit_bytes=VMEM_ALL),
        cost_estimate=pl.CostEstimate(flops=4_000_000_000, bytes_accessed=1000, transcendentals=0),
    )(*arrays)


def gather_level(upper, entry, other):
    state, through, last_id = entry
    link = through * ((last_id < 0) | (other[2] == last_id)).astype(F32)
    state = state + jnp.where(upper, link, 0.0) * other[0]
    last_id = jnp.where(upper & (last_id < 0), other[2], last_id)
    return state, through * jnp.where(upper, other[1], 1.0), last_id


def pair_step(keep, mate, side, cross, after):
    size, lanes = mate.shape[0] - EXTRA, mate.shape[1]

    def body(
        keep_ref, mate_ref, side_ref, cross_ref, send_ref, entry_ref, first_ref, total_ref, rows_ref
    ):
        odd = position()[0] == 1
        upper = (position()[6] & 2) != 0
        mine, mate = unpack(keep_ref), unpack(mate_ref)
        total = merged(odd, mine, mate)
        other = merged(odd, unpack(side_ref), unpack(cross_ref))
        nothing = (0.0, jnp.ones_like(total[1]), jnp.full_like(total[2], -1.0))
        entry = gather_level(upper, nothing, other)
        total = merged(upper, total, other)
        pack(send_ref, total)
        entry_ref[...], total_ref[...] = entry[0], total[0]
        first_ref[...] = jnp.where(odd, mate[0], mine[0])
        rows = tuple(jnp.where(odd, m, o) for o, m in zip(mine[1:], mate[1:]))
        put_rows(rows_ref, entry[1:] + rows + total[1:])

    state = ((size, lanes), F32)
    return call(
        body, (keep, mate, side, cross),
        shaped((mate.shape, BF16), state, state, state, ((8, lanes), F32)), after=after,
    )


def level_step(bit, final, got, entry, first, total, rows, after):
    size, lanes = entry.shape

    def body(
        got_ref, entry_ref, first_ref, total_ref, rows_ref,
        send_ref, one_ref, two_ref, three_ref,
    ):
        upper = (position()[6] & bit) != 0
        other = unpack(got_ref)
        old = (entry_ref[...], rows_ref[0:1], rows_ref[1:2])
        new = gather_level(upper, old, other)
        if final:
            even = position()[0] == 0
            last_first = rows_ref[3:4]
            link = rows_ref[2:3] * (last_first == new[2]).astype(F32)
            reached = first_ref[...] + link * new[0]
            send_ref[...] = jnp.where(even, reached, new[0]).astype(BF16)
            one_ref[...] = jnp.where(even, new[0], reached).astype(BF16)
            prev = jnp.where(even, new[2], last_first)
            two_ref[...] = jnp.broadcast_to(prev[:, 0:LANES], (8, LANES))
            three_ref[...] = jnp.zeros_like(three_ref)
        else:
            held = (total_ref[...], rows_ref[4:5], rows_ref[5:6])
            held = merged(upper, held, other)
            pack(send_ref, held)
            one_ref[...] = new[0]
            two_ref[...] = held[0]
            put_rows(three_ref, new[1:] + (rows_ref[2:3], rows_ref[3:4]) + held[1:])

    if final:
        out = shaped(((size, lanes), BF16), ((size, lanes), BF16), ((8, LANES), F32), ((8, LANES), F32))
    else:
        out = shaped((got.shape, BF16), ((size, lanes), F32), ((size, lanes), F32), ((8, lanes), F32))
    return call(body, (got, entry, first, total, rows), out, after=after)


def local_part(heads, width, x, gate, read, write, stash, skip, after):
    toks = write.shape[0]
    feats = x.shape[1]
    per = LANES // width
    blocks = toks // GROUP
    strip = 64

    def body(
        x_ref, gate_ref, rd_ref, wr_ref, stash_ref, skip_ref,
        a_ref, b_ref, log_cum, scores, mix, pad, tails, rows_ref,
    ):
        cum_ref, step_ref = (stash_ref.at[rows] for rows in stash_rows())
        lane = lane_iota(GROUP)
        mix[...] = jnp.zeros_like(mix)
        pad[...] = jnp.zeros_like(pad)
        rows_ref[...] = jnp.zeros_like(rows_ref)
        rows_ref[0:1, 0:heads] = skip_ref[...]
        skips = rows_ref[0:1]
        seg_row = cum_ref[SEG_LANE : SEG_LANE + 1]
        log_row = cum_ref[...] * LOG2E - jnp.log(step_ref[...]) * LOG2E
        pad[0:32] = cum_ref[...] * LOG2E
        pad[SEG_LANE : SEG_LANE + 1] = seg_row
        log_cum[...] = jnp.transpose(pad[...])
        seg_col = log_cum[:, SEG_LANE : SEG_LANE + 1]
        tail0 = jnp.exp(cum_ref[:, GROUP - 1 : GROUP] - cum_ref[:, 0:GROUP]) * step_ref[:, 0:GROUP]
        same = seg_row[:, 0:GROUP] == seg_row[:, GROUP - 1 : GROUP]
        pad[0:32, 0:GROUP] = jnp.where(same, tail0, 0.0)
        tails[...] = jnp.transpose(pad[:, 0:GROUP])
        masked = []
        for b in range(blocks):
            rows = slice(b * GROUP, (b + 1) * GROUP)
            s = dot(rd_ref[rows], wr_ref[rows], ((1,), (1,)))
            causal = lax.broadcasted_iota(jnp.int32, (GROUP, GROUP), 0) >= lax.broadcasted_iota(
                jnp.int32, (GROUP, GROUP), 1
            )
            scores[b] = jnp.where(causal & (seg_col[rows] == seg_row[:, rows]), s, 0.0)
            linked = seg_col[rows] == seg_col[b * GROUP - 1 : b * GROUP] if b else None
            masked.append(jnp.where(linked, rd_ref[rows].astype(F32), 0.0).astype(BF16) if b else None)
        for i in range(feats // LANES):
            tile = slice(i * LANES, (i + 1) * LANES)
            gains = spread(skips, i * per, width)
            carry = None
            start = jnp.ones((1, LANES), F32)
            for b in range(blocks):
                rows = slice(b * GROUP, (b + 1) * GROUP)
                slot = (i * blocks + b) % mix.shape[0]
                xb = x_ref[rows, tile]
                logs = []
                for k in range(per):
                    head = i * per + k
                    cb = jnp.broadcast_to(log_cum[rows, head : head + 1], (GROUP, LANES))
                    logs.append(cb)
                    ar = log_row[head : head + 1, rows]
                    for low in range(0, GROUP, strip):
                        for left in range(0, min(low + strip, GROUP), LANES):
                            gap = cb[low : low + strip] - ar[:, left : left + LANES]
                            part = jnp.exp2(jnp.minimum(gap, 60.0))
                            part = part * scores[b, low : low + strip, left : left + LANES]
                            at = k * GROUP + low
                            mix[slot, at : at + strip, left : left + LANES] = part.astype(BF16)
                both = dot(mix[slot], xb)
                inner, dec_log = both[0:GROUP], logs[0]
                for k in range(1, per):
                    inner = jnp.where(lane < k * width, inner, both[k * GROUP : (k + 1) * GROUP])
                    dec_log = jnp.where(lane < k * width, dec_log, logs[k])
                dec = jnp.exp2(dec_log)
                xf = xb.astype(F32)
                y = inner + gains * xf
                if b == 1:
                    y = y + (dot(masked[b], carry[0]) + dot(masked[b], carry[1])) * dec
                else:
                    xs = (xf * spread(tails[...], i * per, width)).astype(BF16)
                    s0 = dot(wr_ref[rows], xs, ((0,), (0,)))
                    s0h = s0.astype(BF16)
                    carry = (s0h, (s0 - s0h.astype(F32)).astype(BF16))
                v = gate_ref[rows, tile].astype(F32)
                sg = v / (1.0 + jnp.exp(-v))
                a_ref[rows, tile] = sg * y
                b_ref[rows, tile] = sg * (dec * start)
                start = start * dec[GROUP - 1 : GROUP]

    return call(
        body, (x, gate, read, write, stash, skip),
        shaped(((toks, feats), F32), ((toks, feats), F32), ((toks, LANES), F32)),
        [
            pltpu.VMEM((blocks, GROUP, GROUP), F32), pltpu.VMEM((4, per * GROUP, GROUP), BF16),
            pltpu.VMEM((LANES, toks), F32), pltpu.VMEM((GROUP, LANES), F32), pltpu.VMEM((8, LANES), F32),
        ],
        cost=8_000_000_000, after=after,
    )


def gated_tile(which, prev_ref, rd_ref, cum_ref, a_ref, b_ref, e_ref, gain_ref):
    half_w = e_ref.shape[1]
    here = pl.ds(pl.multiple_of(position()[which] * half_w, LANES), half_w)
    linked = cum_ref[:, SEG_LANE : SEG_LANE + 1] == prev_ref[0:1, 0:1]
    rm = jnp.where(linked, rd_ref[...].astype(F32), 0.0).astype(BF16)
    gated = a_ref[:, here] + b_ref[:, here] * dot(rm, e_ref[...])
    sq = gated * gated
    part = sq[:, 0:LANES]
    for i in range(1, half_w // LANES):
        part = part + sq[:, i * LANES : (i + 1) * LANES]
    squares = jnp.sum(jnp.transpose(part), axis=0, keepdims=True)
    return (gated * gain_ref[:, here]).astype(BF16), squares


def projected(which, quarter, w_ref, g):
    half_w = g.shape[1]
    cols = w_ref.shape[1] // 4
    rows = pl.ds(pl.multiple_of(position()[which] * half_w, LANES), half_w)
    columns = pl.ds(pl.multiple_of(position()[quarter] * cols, LANES), cols)
    return dot(w_ref[rows, columns], g, ((0,), (1,)))


def with_squares(y, squares):
    high = squares.astype(BF16).astype(F32)
    middle = (squares - high).astype(BF16).astype(F32)
    row = lax.broadcasted_iota(jnp.int32, (EXTRA, squares.shape[1]), 0)
    rows = jnp.where(row == 0, high, jnp.where(row == 1, middle, squares - high - middle))
    return jnp.concatenate([y, rows], axis=0).astype(BF16)


def split_squares(ref):
    size = ref.shape[0] - EXTRA
    whole = ref[...].astype(F32)
    return whole[0:size], whole[size : size + 1] + (whole[size + 1 : size + 2] + whole[size + 2 : size + 3])


def gated_first(prev, read, cum, a, b, e, gain, weight):
    toks = a.shape[0]
    half_w = e.shape[1]
    feats = weight.shape[1]

    def body(
        prev_ref, rd_ref, cum_ref, a_ref, b_ref, e_ref, gain_ref, w_ref, g_ref, s_ref, y_ref
    ):
        g, s_ref[...] = gated_tile(0, prev_ref, rd_ref, cum_ref, a_ref, b_ref, e_ref, gain_ref)
        g_ref[...] = g
        for quarter in range(4):
            y_ref[quarter] = projected(0, 2 + quarter, w_ref, g)

    return call(
        body, (prev, read, cum, a, b, e, gain, weight),
        shaped(((toks, half_w), BF16), ((1, toks), F32), ((4, feats // 4, toks), F32)),
        cost=2_000_000_000,
    )


def gated_second(prev, read, cum, a, b, e, gain, partial, s_first, weight):
    toks = a.shape[0]
    half_w = e.shape[1]
    cols = weight.shape[1] // 4

    def body(
        prev_ref, rd_ref, cum_ref, a_ref, b_ref, e_ref, gain_ref, p_ref, sf_ref, w_ref, g_ref, y_ref
    ):
        g, squares = gated_tile(1, prev_ref, rd_ref, cum_ref, a_ref, b_ref, e_ref, gain_ref)
        g_ref[...] = g
        y_ref[...] = with_squares(p_ref[0] + projected(1, 2, w_ref, g), sf_ref[...] + squares)

    return call(
        body, (prev, read, cum, a, b, e, gain, partial, s_first, weight),
        shaped(((toks, half_w), BF16), ((cols + EXTRA, toks), BF16)), cost=1_000_000_000,
    )


def project_rest(quarter, dtype, cost, g, partial, weight, after, add=None):
    toks = g.shape[0]
    block = (weight.shape[1] // 4, toks)

    def body(g_ref, p_ref, w_ref, *refs):
        y = p_ref[quarter] + projected(1, 2 + quarter, w_ref, g_ref[...])
        if add is not None:
            y = y + refs[0][...].astype(F32)
        refs[-1][...] = y.astype(dtype)

    more = () if add is None else (add,)
    return call(
        body, (g, partial, weight, *more), jax.ShapeDtypeStruct(block, dtype), cost=cost, after=after
    )


def add_far(y_far, to_near, got_near):
    def body(y_ref, mine_ref, got_ref, out_ref):
        got, squares = split_squares(got_ref)
        out_ref[...] = with_squares(y_ref[...] + got, split_squares(mine_ref)[1] + squares)

    return call(body, (y_far, to_near, got_near), jax.ShapeDtypeStruct(got_near.shape, BF16))


def finish(features, y_own, to_far, got_far):
    size, toks = y_own.shape
    parts = 4
    step = size // parts

    def body(own_ref, mine_ref, far_ref, out_hbm, out_ref, sems):
        squares = split_squares(mine_ref)[1] + split_squares(far_ref)[1]
        inv = lax.rsqrt(squares / features + EPS)
        copies = []
        for k in range(parts):
            rows = slice(k * step, (k + 1) * step)
            out_ref[rows] = ((own_ref[rows] + far_ref[rows].astype(F32)) * inv).astype(BF16)
            copies.append(pltpu.make_async_copy(out_ref.at[rows], out_hbm.at[rows], sems.at[k]))
            copies[-1].start()
        for copy in copies:
            copy.wait()

    vm = pl.BlockSpec(memory_space=pltpu.VMEM)
    return pl.pallas_call(
        body,
        in_specs=[vm] * 3,
        out_specs=pl.BlockSpec(memory_space=pl.ANY),
        out_shape=jax.ShapeDtypeStruct((size, toks), BF16),
        scratch_shapes=[pltpu.VMEM((size, toks), BF16), pltpu.SemaphoreType.DMA((parts,))],
        compiler_params=pltpu.CompilerParams(vmem_limit_bytes=VMEM),
    )(y_own, to_far, got_far)


def on_device(
    n_seq, n_tp, head_input, gate_input, write_vecs, read_vecs, step_raw, segment_ids,
    decay_log, step_bias, skip_gain, norm_gain, out_weight,
):
    heads = decay_log.shape[0]
    toks, feats = head_input.shape
    width = feats // heads
    def swap(a, bit):
        return lax.ppermute(a, "seq", [(i, i ^ bit) for i in range(n_seq)])

    def across(a, bit):
        return lax.ppermute(a, "tp", [(i, i ^ bit) for i in range(n_tp)])

    send_other, send_keep, stash = prepare(
        heads, width, step_raw, segment_ids.reshape(1, toks), decay_log.reshape(1, heads),
        step_bias.reshape(1, heads), head_input, write_vecs,
    )
    side = swap(send_keep, 2)
    cross = swap(send_other, 3)
    mate = swap(send_other, 1)
    a, b, log_cum = local_part(
        heads, width, head_input, gate_input, read_vecs, write_vecs, stash,
        skip_gain.reshape(1, heads), None,
    )
    sent, entry, first, total, rows = pair_step(send_keep, mate, side, cross, a)
    bit = 4
    while 2 * bit < n_seq:
        sent, entry, total, rows = level_step(bit, False, swap(sent, bit), entry, first, total, rows, None)
        bit *= 2
    sent, e_keep, prev, _ = level_step(bit, True, swap(sent, bit), entry, first, total, rows, None)
    e_other = swap(sent, 1)
    gain = norm_gain.reshape(1, feats)
    shared = (prev, read_vecs, log_cum, a, b)
    g_keep, s_keep, partial = gated_first(*shared, e_keep, gain, out_weight)
    g_other, to_near = gated_second(*shared, e_other, gain, partial, s_keep, out_weight)
    got_near = across(to_near, 1)
    y_near = project_rest(2, BF16, 500_000_000, g_other, partial, out_weight, to_near)
    got_own = across(y_near, 1)
    y_far = project_rest(1, F32, 500_000_000, g_other, partial, out_weight, y_near)
    to_far = add_far(y_far, to_near, got_near)
    got_far = across(to_far, 2)
    y_own = project_rest(3, F32, 10_000_000_000, g_other, partial, out_weight, to_far, got_own)
    return finish(feats * n_tp, y_own, to_far, got_far)


def solution(mesh):
    in_specs = (
        P("seq", "tp"),
        P("seq", "tp"),
        P("seq", None),
        P("seq", None),
        P("tp", "seq"),
        P("seq"),
        P("tp"),
        P("tp"),
        P("tp"),
        P("tp"),
        P("tp", None),
    )
    out_specs = P("tp", "seq")
    return jax.shard_map(
        functools.partial(on_device, mesh.shape["seq"], mesh.shape["tp"]),
        mesh=mesh, in_specs=in_specs, out_specs=out_specs, check_vma=False,
    )
```

```python
import functools

import jax
import jax.numpy as jnp
from jax import lax
from jax.experimental import pallas as pl
from jax.experimental.pallas import tpu as pltpu
from jax.sharding import PartitionSpec as P

GROUP = 256
LANES = 128
EPS = 1e-05
LOG2E = 1.4426950408889634
SEG_LANE = 24
EXTRA = 8
EARLY_ROWS = 384
NEAR_PIECES = 4
EARLY_LANES = 384
VMEM = 16 * 1024 * 1024
VMEM_ALL = 56 * 1024 * 1024
CHEAP = pl.CostEstimate(flops=1000, bytes_accessed=1000, transcendentals=0)
LONG = pl.CostEstimate(flops=4_000_000_000, bytes_accessed=1000, transcendentals=0)
F32 = jnp.float32
BF16 = jnp.bfloat16


def dot(a, b, dims=((1,), (0,))):
    return lax.dot_general(a, b, (dims, ((), ())), preferred_element_type=F32)


def lane_iota(rows):
    return lax.broadcasted_iota(jnp.int32, (rows, LANES), 1)


def spread(cols, first, width):
    rows = cols.shape[0]
    per = LANES // width
    lane = lane_iota(rows)
    out = jnp.broadcast_to(cols[:, first : first + 1], (rows, LANES))
    for k in range(1, per):
        nxt = jnp.broadcast_to(cols[:, first + k : first + k + 1], (rows, LANES))
        out = jnp.where(lane < k * width, out, nxt)
    return out


def position():
    place, rank = lax.axis_index("seq"), lax.axis_index("tp")
    odd = place & 1
    far = rank ^ 2
    return odd, 1 - odd, far ^ 1, far, rank ^ 1, rank, place


def call(body, args, out_shape, scratch=(), after=None, cost=CHEAP):
    vm = pl.BlockSpec(memory_space=pltpu.VMEM)
    specs = [vm] * len(args)
    operands = list(args)
    kernel = body
    if after is not None:
        specs.append(pl.BlockSpec(memory_space=pl.ANY))
        operands.append(after)
        at = len(operands) - 1

        def kernel(*refs):
            body(*refs[:at], *refs[at + 1 :])

    return pl.pallas_call(
        kernel,
        in_specs=specs,
        out_specs=jax.tree.map(lambda _: vm, out_shape),
        out_shape=out_shape,
        scratch_shapes=list(scratch),
        compiler_params=pltpu.CompilerParams(vmem_limit_bytes=VMEM),
        cost_estimate=cost,
    )(*operands)


def shaped(*shapes):
    return [jax.ShapeDtypeStruct(shape, dtype) for shape, dtype in shapes]


def pack(out_ref, total):
    state, through, last = total
    high = through.astype(BF16).astype(F32)
    row = lax.broadcasted_iota(jnp.int32, (EXTRA, state.shape[1]), 0)
    rows = jnp.where(row == 0, high, jnp.where(row == 1, through - high, last))
    out_ref[...] = jnp.concatenate([state, rows], axis=0).astype(BF16)


def unpack(ref):
    size = ref.shape[0] - EXTRA
    whole = ref[...].astype(F32)
    return whole[0:size], whole[size : size + 1] + whole[size + 1 : size + 2], whole[size + 2 : size + 3]


def merged(swapped, one, two):
    later = jnp.where(swapped, one[1], two[1])
    link = later * (one[2] == two[2]).astype(F32)
    state = jnp.where(swapped, 1.0, link) * one[0] + jnp.where(swapped, link, 1.0) * two[0]
    return state, one[1] * two[1], jnp.where(swapped, one[2], two[2])


def ordered(swapped, one, two):
    firsts = tuple(jnp.where(swapped, t, o) for o, t in zip(one, two))
    seconds = tuple(jnp.where(swapped, o, t) for o, t in zip(one, two))
    return firsts, seconds


def stash_rows():
    return slice(0, 32), slice(32, 64)


def put_rows(rows_ref, rows):
    lanes = rows_ref.shape[1]
    for at, row in enumerate(rows):
        rows_ref[at : at + 1] = jnp.broadcast_to(row, (1, lanes))


def prepare(heads, width, raw, seg, decay_log, bias, x, write):
    toks, state = write.shape
    half_w = x.shape[1] // 2
    half_h = heads // 2
    blocks = toks // GROUP
    arrays = (raw, seg, decay_log, bias, write, x)

    def body(*refs):
        hbm, (other_ref, keep_ref, stash_ref) = refs[: len(arrays)], refs[len(arrays) : -9]
        raw_ref, seg_ref, dl_ref, sb_ref, wr_ref, x_ref, rows, pad, sems = refs[-9:]
        copies = [
            pltpu.make_async_copy(src, dst, sems.at[k])
            for k, (src, dst) in enumerate(zip(hbm, (raw_ref, seg_ref, dl_ref, sb_ref, wr_ref, x_ref)))
        ]
        for copy in copies:
            copy.start()
        rows[...] = jnp.zeros_like(rows)
        pad[...] = jnp.zeros_like(pad)
        tri = (
            lax.broadcasted_iota(jnp.int32, (GROUP, GROUP), 0)
            <= lax.broadcasted_iota(jnp.int32, (GROUP, GROUP), 1)
        ).astype(BF16)
        for copy in copies[:5]:
            copy.wait()
        vecs = jnp.transpose(wr_ref[...].astype(F32))
        rows[0:1, 0:heads] = dl_ref[...]
        rows[1:2, 0:heads] = sb_ref[...]
        pad[0:heads] = raw_ref[...].astype(F32)
        params = jnp.transpose(rows[...])[0:32]
        z = pad[0:32] + params[:, 1:2]
        step = jnp.maximum(z, 0.0) + jnp.log1p(jnp.exp(-jnp.abs(z)))
        rate = -jnp.exp(params[:, 0:1]) * step
        cum, full = [], []
        base = jnp.zeros((32, 1), F32)
        for b in range(blocks):
            r = rate[:, b * GROUP : (b + 1) * GROUP]
            r1 = r.astype(BF16)
            d1 = r - r1.astype(F32)
            r2 = d1.astype(BF16)
            r3 = (d1 - r2.astype(F32)).astype(BF16)
            c = dot(r1, tri) + (dot(r2, tri) + dot(r3, tri))
            cum.append(c)
            full.append(c + base)
            base = base + c[:, GROUP - 1 : GROUP]
        seg_row = seg_ref[...].astype(F32)
        last = seg_row[:, toks - 1 : toks]
        tail = jnp.exp(base - jnp.concatenate(full, axis=1)) * step
        cum_rows, step_rows = stash_rows()
        stash_ref[cum_rows] = jnp.concatenate(cum, axis=1)
        stash_ref[SEG_LANE : SEG_LANE + 1] = seg_row
        stash_ref[step_rows] = step
        tails = jnp.where(seg_row == last, tail, 0.0)
        rows[...] = jnp.zeros_like(rows)
        rows[0:32] = jnp.broadcast_to(jnp.exp(base), (32, LANES))
        keep = jnp.transpose(rows[...])[0:1]
        per = LANES // width
        odd = lax.rem(lax.axis_index("seq"), 2) == 1
        lane = lane_iota(state)
        copies[5].wait()
        halves = []
        for j in range(2):
            own, through = [], []
            for i in range(half_w // LANES):
                at = j * half_h + i * per
                written = [(vecs * tails[at + k : at + k + 1]).astype(BF16) for k in range(per)]
                both = dot(jnp.concatenate(written, axis=0), x_ref[:, j * half_w + i * LANES : j * half_w + (i + 1) * LANES])
                tile = both[0:state]
                for k in range(1, per):
                    tile = jnp.where(lane < k * width, tile, both[k * state : (k + 1) * state])
                own.append(tile)
                through.append(spread(keep, at, width))
            halves.append((jnp.concatenate(own, axis=1), jnp.concatenate(through, axis=1), last))
        mine, other = ordered(odd, *halves)
        pack(keep_ref, mine)
        pack(other_ref, other)

    vm = pl.BlockSpec(memory_space=pltpu.VMEM)
    out_shape = shaped(
        ((state + EXTRA, half_w), BF16), ((state + EXTRA, half_w), BF16), ((stash_rows()[1].stop, toks), F32),
    )
    return pl.pallas_call(
        body,
        in_specs=[pl.BlockSpec(memory_space=pltpu.HBM)] * len(arrays),
        out_specs=[vm] * len(out_shape),
        out_shape=out_shape,
        scratch_shapes=[
            *[pltpu.VMEM(a.shape, a.dtype) for a in arrays],
            pltpu.VMEM((LANES, LANES), F32), pltpu.VMEM((32, toks), F32),
            pltpu.SemaphoreType.DMA((len(arrays),)),
        ],
        compiler_params=pltpu.CompilerParams(vmem_limit_bytes=VMEM_ALL),
        cost_estimate=LONG,
    )(*arrays)


def gather_level(upper, entry, other):
    state, through, last_id = entry
    link = through * ((last_id < 0) | (other[2] == last_id)).astype(F32)
    state = state + jnp.where(upper, link, 0.0) * other[0]
    last_id = jnp.where(upper & (last_id < 0), other[2], last_id)
    return state, through * jnp.where(upper, other[1], 1.0), last_id


def pair_step(keep, mate, side, cross, after):
    size, lanes = mate.shape[0] - EXTRA, mate.shape[1]

    def body(
        keep_ref, mate_ref, side_ref, cross_ref, early_ref, late_ref, entry_ref, first_ref, total_ref, rows_ref
    ):
        odd = position()[0] == 1
        upper = (position()[6] & 2) != 0
        mine, mate = unpack(keep_ref), unpack(mate_ref)
        total = merged(odd, mine, mate)
        other = merged(odd, unpack(side_ref), unpack(cross_ref))
        nothing = (0.0, jnp.ones_like(total[1]), jnp.full_like(total[2], -1.0))
        entry = gather_level(upper, nothing, other)
        total = merged(upper, total, other)
        pack_both(early_ref, late_ref, total)
        entry_ref[...], total_ref[...] = entry[0], total[0]
        first_ref[...] = jnp.where(odd, mate[0], mine[0])
        rows = tuple(jnp.where(odd, m, o) for o, m in zip(mine[1:], mate[1:]))
        put_rows(rows_ref, entry[1:] + rows + total[1:])

    state = ((size, lanes), F32)
    return call(
        body, (keep, mate, side, cross),
        lane_parts(mate.shape) + shaped(state, state, state, ((8, lanes), F32)), after=after, cost=LONG,
    )


def pack_both(early_ref, late_ref, total):
    edge = early_ref.shape[1]
    pack(early_ref, tuple(t[:, :edge] for t in total))
    pack(late_ref, tuple(t[:, edge:] for t in total))


def lane_parts(shape):
    rows, lanes = shape
    return shaped(((rows, EARLY_LANES), BF16), ((rows, lanes - EARLY_LANES), BF16))


def level_step(bit, early, late, entry, first, total, rows):
    size, lanes = entry.shape

    def body(
        early_ref, late_ref, entry_ref, first_ref, total_ref, rows_ref,
        early_out, late_out, entry_out, first_out, total_out, rows_out,
    ):
        upper = (position()[6] & bit) != 0
        other = tuple(jnp.concatenate(pair, axis=1) for pair in zip(unpack(early_ref), unpack(late_ref)))
        new = gather_level(upper, (entry_ref[...], rows_ref[0:1], rows_ref[1:2]), other)
        held = merged(upper, (total_ref[...], rows_ref[4:5], rows_ref[5:6]), other)
        pack_both(early_out, late_out, held)
        entry_out[...], first_out[...], total_out[...] = new[0], first_ref[...], held[0]
        put_rows(rows_out, new[1:] + (rows_ref[2:3], rows_ref[3:4]) + held[1:])

    state = ((size, lanes), F32)
    return call(
        body, (early, late, entry, first, total, rows),
        lane_parts((early.shape[0], lanes)) + shaped(state, state, state, ((8, lanes), F32)),
    )


def entry_step(bit, lanes, got, entry, first, rows, after=None):
    size = entry.shape[0]
    width = lanes.stop - lanes.start

    def body(got_ref, entry_ref, first_ref, rows_ref, other_ref, keep_ref, prev_ref):
        upper = (position()[6] & bit) != 0
        even = position()[0] == 0
        old = (entry_ref[:, lanes], rows_ref[0:1, lanes], rows_ref[1:2, lanes])
        new = gather_level(upper, old, unpack(got_ref))
        last_first = rows_ref[3:4, lanes]
        link = rows_ref[2:3, lanes] * (last_first == new[2]).astype(F32)
        reached = first_ref[:, lanes] + link * new[0]
        other_ref[...] = jnp.where(even, reached, new[0]).astype(BF16)
        keep_ref[...] = jnp.where(even, new[0], reached).astype(BF16)
        prev = jnp.where(even, new[2], last_first)
        prev_ref[...] = jnp.broadcast_to(prev[:, 0:LANES], (8, LANES))

    block = ((size, width), BF16)
    return call(body, (got, entry, first, rows), shaped(block, block, ((8, LANES), F32)), after=after)


def local_part(heads, width, x, gate, read, write, stash, skip, after):
    toks = write.shape[0]
    feats = x.shape[1]
    per = LANES // width
    blocks = toks // GROUP
    strip = 64

    def body(
        x_ref, gate_ref, rd_ref, wr_ref, stash_ref, skip_ref,
        a_ref, b_ref, log_cum, scores, mix, pad, tails, rows_ref,
    ):
        cum_ref, step_ref = (stash_ref.at[rows] for rows in stash_rows())
        lane = lane_iota(GROUP)
        mix[...] = jnp.zeros_like(mix)
        pad[...] = jnp.zeros_like(pad)
        rows_ref[...] = jnp.zeros_like(rows_ref)
        rows_ref[0:1, 0:heads] = skip_ref[...]
        skips = rows_ref[0:1]
        seg_row = cum_ref[SEG_LANE : SEG_LANE + 1]
        log_row = cum_ref[...] * LOG2E - jnp.log(step_ref[...]) * LOG2E
        pad[0:32] = cum_ref[...] * LOG2E
        pad[SEG_LANE : SEG_LANE + 1] = seg_row
        log_cum[...] = jnp.transpose(pad[...])
        seg_col = log_cum[:, SEG_LANE : SEG_LANE + 1]
        tail0 = jnp.exp(cum_ref[:, GROUP - 1 : GROUP] - cum_ref[:, 0:GROUP]) * step_ref[:, 0:GROUP]
        same = seg_row[:, 0:GROUP] == seg_row[:, GROUP - 1 : GROUP]
        pad[0:32, 0:GROUP] = jnp.where(same, tail0, 0.0)
        tails[...] = jnp.transpose(pad[:, 0:GROUP])
        masked = []
        for b in range(blocks):
            rows = slice(b * GROUP, (b + 1) * GROUP)
            s = dot(rd_ref[rows], wr_ref[rows], ((1,), (1,)))
            causal = lax.broadcasted_iota(jnp.int32, (GROUP, GROUP), 0) >= lax.broadcasted_iota(
                jnp.int32, (GROUP, GROUP), 1
            )
            scores[b] = jnp.where(causal & (seg_col[rows] == seg_row[:, rows]), s, 0.0)
            linked = seg_col[rows] == seg_col[b * GROUP - 1 : b * GROUP] if b else None
            masked.append(jnp.where(linked, rd_ref[rows].astype(F32), 0.0).astype(BF16) if b else None)
        for i in range(feats // LANES):
            tile = slice(i * LANES, (i + 1) * LANES)
            gains = spread(skips, i * per, width)
            carry = None
            start = jnp.ones((1, LANES), F32)
            for b in range(blocks):
                rows = slice(b * GROUP, (b + 1) * GROUP)
                slot = (i * blocks + b) % mix.shape[0]
                xb = x_ref[rows, tile]
                logs = []
                for k in range(per):
                    head = i * per + k
                    cb = jnp.broadcast_to(log_cum[rows, head : head + 1], (GROUP, LANES))
                    logs.append(cb)
                    ar = log_row[head : head + 1, rows]
                    for low in range(0, GROUP, strip):
                        for left in range(0, min(low + strip, GROUP), LANES):
                            gap = cb[low : low + strip] - ar[:, left : left + LANES]
                            part = jnp.exp2(jnp.minimum(gap, 60.0))
                            part = part * scores[b, low : low + strip, left : left + LANES]
                            at = k * GROUP + low
                            mix[slot, at : at + strip, left : left + LANES] = part.astype(BF16)
                both = dot(mix[slot], xb)
                inner, dec_log = both[0:GROUP], logs[0]
                for k in range(1, per):
                    inner = jnp.where(lane < k * width, inner, both[k * GROUP : (k + 1) * GROUP])
                    dec_log = jnp.where(lane < k * width, dec_log, logs[k])
                dec = jnp.exp2(dec_log)
                xf = xb.astype(F32)
                y = inner + gains * xf
                if b == 1:
                    y = y + (dot(masked[b], carry[0]) + dot(masked[b], carry[1])) * dec
                else:
                    xs = (xf * spread(tails[...], i * per, width)).astype(BF16)
                    s0 = dot(wr_ref[rows], xs, ((0,), (0,)))
                    s0h = s0.astype(BF16)
                    carry = (s0h, (s0 - s0h.astype(F32)).astype(BF16))
                v = gate_ref[rows, tile].astype(F32)
                sg = v / (1.0 + jnp.exp(-v))
                a_ref[rows, tile] = sg * y
                b_ref[rows, tile] = sg * (dec * start)
                start = start * dec[GROUP - 1 : GROUP]

    return call(
        body, (x, gate, read, write, stash, skip),
        shaped(((toks, feats), F32), ((toks, feats), F32), ((toks, LANES), F32)),
        [
            pltpu.VMEM((blocks, GROUP, GROUP), F32), pltpu.VMEM((4, per * GROUP, GROUP), BF16),
            pltpu.VMEM((LANES, toks), F32), pltpu.VMEM((GROUP, LANES), F32), pltpu.VMEM((8, LANES), F32),
        ],
        after=after, cost=LONG,
    )


def gated_part(which, lanes, prev_ref, rd_ref, cum_ref, a_ref, b_ref, states, gain_ref):
    half_w = a_ref.shape[1] // 2
    first = pl.multiple_of(position()[which] * half_w + lanes.start, LANES)
    here = pl.ds(first, lanes.stop - lanes.start)
    linked = cum_ref[:, SEG_LANE : SEG_LANE + 1] == prev_ref[0:1, 0:1]
    rm = jnp.where(linked, rd_ref[...].astype(F32), 0.0).astype(BF16)
    carried = [dot(rm, state[...]) for state in states]
    carried = carried[0] if len(carried) == 1 else jnp.concatenate(carried, axis=1)
    gated = a_ref[:, here] + b_ref[:, here] * carried
    sq = gated * gated
    part = sq[:, 0:LANES]
    for i in range(1, sq.shape[1] // LANES):
        part = part + sq[:, i * LANES : (i + 1) * LANES]
    squares = jnp.sum(jnp.transpose(part), axis=0, keepdims=True)
    return (gated * gain_ref[:, here]).astype(BF16), squares


def projected(which, lanes, quarter, rows, w_ref, g):
    half_w, cols = w_ref.shape[0] // 2, w_ref.shape[1] // 4
    here = pl.multiple_of(position()[which] * half_w + lanes.start, LANES)
    first = pl.multiple_of(position()[2 + quarter] * cols + rows.start, LANES)
    block = w_ref[pl.ds(here, lanes.stop - lanes.start), pl.ds(first, rows.stop - rows.start)]
    return dot(block, g, ((0,), (1,)))


def with_squares(y, squares):
    high = squares.astype(BF16).astype(F32)
    middle = (squares - high).astype(BF16).astype(F32)
    row = lax.broadcasted_iota(jnp.int32, (EXTRA, squares.shape[1]), 0)
    rows = jnp.where(row == 0, high, jnp.where(row == 1, middle, squares - high - middle))
    return jnp.concatenate([y, rows], axis=0).astype(BF16)


def split_squares(ref):
    size = ref.shape[0] - EXTRA
    whole = ref[...].astype(F32)
    return whole[0:size], whole[size : size + 1] + (whole[size + 1 : size + 2] + whole[size + 2 : size + 3])


def gated_sums(which, lanes, prev, read, cum, a, b, states, gain, weight, partial=None, squares=None):
    toks = a.shape[0]
    cols = weight.shape[1] // 4
    earlier = () if partial is None else (partial, squares)

    def body(prev_ref, rd_ref, cum_ref, a_ref, b_ref, gain_ref, w_ref, *refs):
        states = refs[: len(states_in)]
        old, (g_ref, s_ref, y_ref) = refs[len(states_in) : -3], refs[-3:]
        g, s = gated_part(which, lanes, prev_ref, rd_ref, cum_ref, a_ref, b_ref, states, gain_ref)
        g_ref[...] = g
        s_ref[...] = s + old[1][...] if old else s
        for quarter in range(2):
            y = projected(which, lanes, quarter, slice(0, cols), w_ref, g)
            y_ref[quarter] = y + old[0][quarter] if old else y

    states_in = states
    return call(
        body, (prev, read, cum, a, b, gain, weight, *states, *earlier),
        shaped(((toks, lanes.stop - lanes.start), BF16), ((1, toks), F32), ((2, cols, toks), F32)),
    )


def gated_last(lanes, rows, prev, read, cum, a, b, state, gain, weight, partial, squares):
    toks = a.shape[0]

    def body(prev_ref, rd_ref, cum_ref, a_ref, b_ref, e_ref, gain_ref, w_ref, p_ref, s_ref, g_ref, y_ref):
        g, s = gated_part(1, lanes, prev_ref, rd_ref, cum_ref, a_ref, b_ref, (e_ref,), gain_ref)
        g_ref[...] = g
        y = p_ref[0, rows] + projected(1, lanes, 0, rows, w_ref, g)
        y_ref[...] = with_squares(y, s_ref[...] + s)

    return call(
        body, (prev, read, cum, a, b, state, gain, weight, partial, squares),
        shaped(((toks, lanes.stop - lanes.start), BF16), ((rows.stop - rows.start + EXTRA, toks), BF16)),
    )


def project_last(lanes, pieces, g, partial, weight, after):
    def body(g_ref, p_ref, w_ref, *outs):
        for (quarter, rows, dtype), y_ref in zip(pieces, outs):
            y = p_ref[quarter, rows] + projected(1, lanes, quarter, rows, w_ref, g_ref[...])
            y_ref[...] = y.astype(dtype)

    toks = g.shape[0]
    out = shaped(*[((rows.stop - rows.start, toks), dtype) for _, rows, dtype in pieces])
    return call(body, (g, partial, weight), out, after=after)


def project_whole(quarter, groups, gs, weight, pieces, adds=(), after=None):
    cols = weight.shape[1] // 4
    toks = gs[0].shape[0]
    step = cols // pieces

    def body(w_ref, *refs):
        g_refs, add_refs, outs = refs[: len(gs)], refs[len(gs) : len(gs) + len(adds)], refs[len(gs) + len(adds) :]
        y = sum(
            projected(which, lanes, quarter, slice(0, cols), w_ref, g_ref[...])
            for (which, lanes), g_ref in zip(groups, g_refs)
        )
        if add_refs:
            outs[0][...] = y + jnp.concatenate([r[...].astype(F32) for r in add_refs], axis=0)
        else:
            for k, y_ref in enumerate(outs):
                y_ref[...] = y[k * step : (k + 1) * step].astype(BF16)

    out = shaped(((cols, toks), F32)) if adds else shaped(*[((step, toks), BF16)] * pieces)
    return call(body, (weight, *gs, *adds), out, after=after)


def add_first(y_far, to_near, got_near):
    def body(y_ref, mine_ref, got_ref, out_ref):
        got, squares = split_squares(got_ref)
        out_ref[...] = with_squares(y_ref[...] + got, split_squares(mine_ref)[1] + squares)

    return call(body, (y_far, to_near, got_near), jax.ShapeDtypeStruct(got_near.shape, BF16))


def add_second(y_far, got_near, after):
    def body(y_ref, got_ref, out_ref):
        out_ref[...] = (y_ref[...] + got_ref[...].astype(F32)).astype(BF16)

    return call(body, (y_far, got_near), jax.ShapeDtypeStruct(got_near.shape, BF16), after=after)


def finish(rows, y_own, inputs, out=None, features=None):
    size, toks = y_own.shape
    parts = 2
    step = (rows.stop - rows.start) // parts
    first = out is None

    def body(own_ref, far_ref, factor_ref, *refs):
        out_hbm, *more, out_ref, sems = refs if first else refs[1:]
        if first:
            inv = lax.rsqrt((split_squares(factor_ref)[1] + split_squares(far_ref)[1]) / features + EPS)
            more[0][...] = inv
        else:
            inv = factor_ref[...]
        copies = []
        for k in range(parts):
            here = slice(k * step, (k + 1) * step)
            there = slice(rows.start + here.start, rows.start + here.stop)
            out_ref[here] = ((own_ref[there] + far_ref[here].astype(F32)) * inv).astype(BF16)
            copies.append(pltpu.make_async_copy(out_ref.at[here], out_hbm.at[there], sems.at[k]))
            copies[-1].start()
        for copy in copies:
            copy.wait()

    vm, where = pl.BlockSpec(memory_space=pltpu.VMEM), pl.BlockSpec(memory_space=pl.ANY)
    result = jax.ShapeDtypeStruct((size, toks), BF16)
    return pl.pallas_call(
        body,
        in_specs=[vm] * 3 + ([] if first else [where]),
        out_specs=[where, vm] if first else where,
        out_shape=[result, jax.ShapeDtypeStruct((1, toks), F32)] if first else result,
        scratch_shapes=[pltpu.VMEM((rows.stop - rows.start, toks), BF16), pltpu.SemaphoreType.DMA((parts,))],
        input_output_aliases={} if first else {3: 0},
        compiler_params=pltpu.CompilerParams(vmem_limit_bytes=VMEM),
        cost_estimate=CHEAP,
    )(y_own, *inputs, *(() if first else (out,)))


def on_device(
    n_seq, n_tp, head_input, gate_input, write_vecs, read_vecs, step_raw, segment_ids,
    decay_log, step_bias, skip_gain, norm_gain, out_weight,
):
    heads = decay_log.shape[0]
    toks, feats = head_input.shape
    width = feats // heads
    def swap(a, bit):
        return lax.ppermute(a, "seq", [(i, i ^ bit) for i in range(n_seq)])

    def across(a, bit):
        return lax.ppermute(a, "tp", [(i, i ^ bit) for i in range(n_tp)])

    send_other, send_keep, stash = prepare(
        heads, width, step_raw, segment_ids.reshape(1, toks), decay_log.reshape(1, heads),
        step_bias.reshape(1, heads), head_input, write_vecs,
    )
    side = swap(send_keep, 2)
    cross = swap(send_other, 3)
    mate = swap(send_other, 1)
    a, b, log_cum = local_part(
        heads, width, head_input, gate_input, read_vecs, write_vecs, stash,
        skip_gain.reshape(1, heads), None,
    )
    early, late, entry, first, total, rows = pair_step(send_keep, mate, side, cross, a)
    bit = 4
    while 2 * bit < n_seq:
        early, late, entry, first, total, rows = level_step(
            bit, swap(early, bit), swap(late, bit), entry, first, total, rows
        )
        bit *= 2
    half_w = feats // 2
    quarter = out_weight.shape[1] // 4
    one, two, half = slice(0, EARLY_LANES), slice(EARLY_LANES, half_w), slice(0, half_w)
    top, rest, every = slice(0, EARLY_ROWS), slice(EARLY_ROWS, quarter), slice(0, quarter)
    got_early, got_late = swap(early, bit), swap(late, bit)
    send_one, keep_one, prev = entry_step(bit, one, got_early, entry, first, rows)
    other_one = swap(send_one, 1)
    send_two, keep_two, _ = entry_step(bit, two, got_late, entry, first, rows, send_one)
    other_two = swap(send_two, 1)
    gain = norm_gain.reshape(1, feats)
    shared = (prev, read_vecs, log_cum, a, b)
    g_keep, squares, partial = gated_sums(0, half, *shared, (keep_one, keep_two), gain, out_weight)
    g_one, squares, partial = gated_sums(1, one, *shared, (other_one,), gain, out_weight, partial, squares)
    g_two, near_top = gated_last(two, top, *shared, other_two, gain, out_weight, partial, squares)
    got_top = across(near_top, 1)
    near_rest, far_top, far_rest = project_last(
        two, ((0, rest, BF16), (1, top, F32), (1, rest, F32)), g_two, partial, out_weight, near_top
    )
    got_rest = across(near_rest, 1)
    to_far_top = add_first(far_top, near_top, got_top)
    got_far_top = across(to_far_top, 2)
    to_far_rest = add_second(far_rest, got_rest, to_far_top)
    got_far_rest = across(to_far_rest, 2)
    groups, gs = ((0, half), (1, one), (1, two)), (g_keep, g_one, g_two)
    y_near = project_whole(2, groups, gs, out_weight, NEAR_PIECES, after=to_far_rest)
    got_own = tuple(across(piece, 1) for piece in y_near)
    (y_own,) = project_whole(3, groups, gs, out_weight, 1, got_own)
    out, inv = finish(top, y_own, (got_far_top, to_far_top), features=feats * n_tp)
    return finish(rest, y_own, (got_far_rest, inv), out)


def solution(mesh):
    in_specs = (
        P("seq", "tp"),
        P("seq", "tp"),
        P("seq", None),
        P("seq", None),
        P("tp", "seq"),
        P("seq"),
        P("tp"),
        P("tp"),
        P("tp"),
        P("tp"),
        P("tp", None),
    )
    out_specs = P("tp", "seq")
    return jax.shard_map(
        functools.partial(on_device, mesh.shape["seq"], mesh.shape["tp"]),
        mesh=mesh, in_specs=in_specs, out_specs=out_specs, check_vma=False,
    )
```

```python
import functools

import jax
import jax.numpy as jnp
from jax import lax
from jax.experimental import pallas as pl
from jax.experimental.pallas import tpu as pltpu
from jax.sharding import PartitionSpec as P

GROUP = 256
LANES = 128
EPS = 1e-05
LOG2E = 1.4426950408889634
SEG_LANE = 24
EXTRA = 8
EARLY_ROWS = 384
NEAR_PIECES = 4
EARLY_LANES = 384
VMEM = 16 * 1024 * 1024
VMEM_ALL = 56 * 1024 * 1024
CHEAP = pl.CostEstimate(flops=1000, bytes_accessed=1000, transcendentals=0)
LONG = pl.CostEstimate(flops=4_000_000_000, bytes_accessed=1000, transcendentals=0)
F32 = jnp.float32
BF16 = jnp.bfloat16


def dot(a, b, dims=((1,), (0,))):
    return lax.dot_general(a, b, (dims, ((), ())), preferred_element_type=F32)


def lane_iota(rows):
    return lax.broadcasted_iota(jnp.int32, (rows, LANES), 1)


def spread(cols, first, width):
    rows = cols.shape[0]
    per = LANES // width
    lane = lane_iota(rows)
    out = jnp.broadcast_to(cols[:, first : first + 1], (rows, LANES))
    for k in range(1, per):
        nxt = jnp.broadcast_to(cols[:, first + k : first + k + 1], (rows, LANES))
        out = jnp.where(lane < k * width, out, nxt)
    return out


def position():
    place, rank = lax.axis_index("seq"), lax.axis_index("tp")
    odd = place & 1
    far = rank ^ 2
    return odd, 1 - odd, far ^ 1, far, rank ^ 1, rank, place


def call(body, args, out_shape, scratch=(), after=None, cost=CHEAP):
    vm = pl.BlockSpec(memory_space=pltpu.VMEM)
    specs = [vm] * len(args)
    operands = list(args)
    kernel = body
    if after is not None:
        specs.append(pl.BlockSpec(memory_space=pl.ANY))
        operands.append(after)
        at = len(operands) - 1

        def kernel(*refs):
            body(*refs[:at], *refs[at + 1 :])

    return pl.pallas_call(
        kernel,
        in_specs=specs,
        out_specs=jax.tree.map(lambda _: vm, out_shape),
        out_shape=out_shape,
        scratch_shapes=list(scratch),
        compiler_params=pltpu.CompilerParams(vmem_limit_bytes=VMEM),
        cost_estimate=cost,
    )(*operands)


def shaped(*shapes):
    return [jax.ShapeDtypeStruct(shape, dtype) for shape, dtype in shapes]


def pack(out_ref, total):
    state, through, last = total
    high = through.astype(BF16).astype(F32)
    row = lax.broadcasted_iota(jnp.int32, (EXTRA, state.shape[1]), 0)
    rows = jnp.where(row == 0, high, jnp.where(row == 1, through - high, last))
    out_ref[...] = jnp.concatenate([state, rows], axis=0).astype(BF16)


def unpack(ref):
    size = ref.shape[0] - EXTRA
    whole = ref[...].astype(F32)
    return whole[0:size], whole[size : size + 1] + whole[size + 1 : size + 2], whole[size + 2 : size + 3]


def merged(swapped, one, two):
    later = jnp.where(swapped, one[1], two[1])
    link = later * (one[2] == two[2]).astype(F32)
    state = jnp.where(swapped, 1.0, link) * one[0] + jnp.where(swapped, link, 1.0) * two[0]
    return state, one[1] * two[1], jnp.where(swapped, one[2], two[2])


def ordered(swapped, one, two):
    firsts = tuple(jnp.where(swapped, t, o) for o, t in zip(one, two))
    seconds = tuple(jnp.where(swapped, o, t) for o, t in zip(one, two))
    return firsts, seconds


def stash_rows():
    return slice(0, 32), slice(32, 64), slice(64, 96), slice(96, 104)


def put_rows(rows_ref, rows):
    lanes = rows_ref.shape[1]
    for at, row in enumerate(rows):
        rows_ref[at : at + 1] = jnp.broadcast_to(row, (1, lanes))


def half_state(half, width, vecs, tails_ref, through_row, last, x_ref, first_lane, out_ref):
    state = vecs.shape[0]
    half_w = out_ref.shape[1]
    per = LANES // width
    half_h = half_w // width
    lane = lane_iota(state)
    mine = jnp.where(half == 1, pltpu.roll(through_row, LANES - half_h, 1), through_row)
    own, through = [], []
    for i in range(half_w // LANES):
        written = []
        for k in range(per):
            row = tails_ref[pl.ds(half * half_h + i * per + k, 1), :]
            written.append((vecs * row).astype(BF16))
        here = pl.ds(pl.multiple_of(first_lane + i * LANES, LANES), LANES)
        both = dot(jnp.concatenate(written, axis=0), x_ref[:, here])
        tile = both[0:state]
        for k in range(1, per):
            tile = jnp.where(lane < k * width, tile, both[k * state : (k + 1) * state])
        own.append(tile)
        through.append(spread(mine[0:1], i * per, width))
    group = (jnp.concatenate(own, axis=1), jnp.concatenate(through, axis=1), jnp.broadcast_to(last, (1, half_w)))
    pack(out_ref, group)


def prepare(heads, width, raw, seg, decay_log, bias, x, write):
    toks, state = write.shape
    half_w = x.shape[1] // 2
    blocks = toks // GROUP
    arrays = (raw, seg, decay_log, bias, write, x)

    def body(*refs):
        hbm, (other_ref, stash_ref) = refs[: len(arrays)], refs[len(arrays) : -8]
        raw_ref, seg_ref, dl_ref, sb_ref, wr_ref, x_ref, rows, sems = refs[-8:]
        half = position()[1]
        lanes = pl.ds(pl.multiple_of(half * half_w, LANES), half_w)
        sources = (*hbm[:5], hbm[5].at[:, lanes])
        copies = [
            pltpu.make_async_copy(src, dst, sems.at[k])
            for k, (src, dst) in enumerate(zip(sources, (raw_ref, seg_ref, dl_ref, sb_ref, wr_ref, x_ref)))
        ]
        for copy in copies:
            copy.start()
        rows[...] = jnp.zeros_like(rows)
        tri = (
            lax.broadcasted_iota(jnp.int32, (GROUP, GROUP), 0)
            <= lax.broadcasted_iota(jnp.int32, (GROUP, GROUP), 1)
        ).astype(BF16)
        stash_ref[...] = jnp.zeros_like(stash_ref)
        cum_rows, step_rows, tail_rows, sum_rows = stash_rows()
        for copy in copies[:5]:
            copy.wait()
        vecs = jnp.transpose(wr_ref[...].astype(F32))
        rows[0:1, 0:heads] = dl_ref[...]
        rows[1:2, 0:heads] = sb_ref[...]
        stash_ref[0:heads] = raw_ref[...].astype(F32)
        params = jnp.transpose(rows[...])[0:32]
        z = stash_ref[cum_rows] + params[:, 1:2]
        step = jnp.maximum(z, 0.0) + jnp.log1p(jnp.exp(-jnp.abs(z)))
        rate = -jnp.exp(params[:, 0:1]) * step
        cum, full = [], []
        base = jnp.zeros((32, 1), F32)
        for b in range(blocks):
            r = rate[:, b * GROUP : (b + 1) * GROUP]
            r1 = r.astype(BF16)
            d1 = r - r1.astype(F32)
            r2 = d1.astype(BF16)
            r3 = (d1 - r2.astype(F32)).astype(BF16)
            c = dot(r1, tri) + (dot(r2, tri) + dot(r3, tri))
            cum.append(c)
            full.append(c + base)
            base = base + c[:, GROUP - 1 : GROUP]
        seg_row = seg_ref[...].astype(F32)
        last = seg_row[:, toks - 1 : toks]
        tail = jnp.exp(base - jnp.concatenate(full, axis=1)) * step
        stash_ref[cum_rows] = jnp.concatenate(cum, axis=1)
        stash_ref[SEG_LANE : SEG_LANE + 1] = seg_row
        stash_ref[step_rows] = step
        stash_ref[tail_rows] = jnp.where(seg_row == last, tail, 0.0)
        rows[...] = jnp.zeros_like(rows)
        rows[0:32] = jnp.broadcast_to(jnp.exp(base), (32, LANES))
        sums = jnp.transpose(rows[...])[0:8]
        stash_ref[sum_rows, 0:LANES] = sums
        copies[5].wait()
        half_state(half, width, vecs, stash_ref.at[tail_rows], sums, last, x_ref, 0, other_ref)

    vm = pl.BlockSpec(memory_space=pltpu.VMEM)
    out_shape = shaped(((state + EXTRA, half_w), BF16), ((stash_rows()[-1].stop, toks), F32))
    return pl.pallas_call(
        body,
        in_specs=[pl.BlockSpec(memory_space=pltpu.HBM)] * len(arrays),
        out_specs=[vm] * len(out_shape),
        out_shape=out_shape,
        scratch_shapes=[
            *[pltpu.VMEM(a.shape, a.dtype) for a in arrays[:5]], pltpu.VMEM((toks, half_w), BF16),
            pltpu.VMEM((LANES, LANES), F32), pltpu.SemaphoreType.DMA((len(arrays),)),
        ],
        compiler_params=pltpu.CompilerParams(vmem_limit_bytes=VMEM_ALL),
        cost_estimate=LONG,
    )(*arrays)


def kept_state(width, stash, x, write):
    toks, state = write.shape
    half_w = x.shape[1] // 2

    def body(stash_ref, x_ref, wr_ref, keep_ref):
        half = position()[0]
        cum_rows, _, tail_rows, sum_rows = stash_rows()
        vecs = jnp.transpose(wr_ref[...].astype(F32))
        last = stash_ref[SEG_LANE : SEG_LANE + 1, toks - 1 : toks]
        sums = stash_ref[sum_rows, 0:LANES]
        half_state(half, width, vecs, stash_ref.at[tail_rows], sums, last, x_ref, half * half_w, keep_ref)

    return call(body, (stash, x, write), jax.ShapeDtypeStruct((state + EXTRA, half_w), BF16), cost=LONG)


def gather_level(upper, entry, other):
    state, through, last_id = entry
    link = through * ((last_id < 0) | (other[2] == last_id)).astype(F32)
    state = state + jnp.where(upper, link, 0.0) * other[0]
    last_id = jnp.where(upper & (last_id < 0), other[2], last_id)
    return state, through * jnp.where(upper, other[1], 1.0), last_id


def pair_step(keep, mate, after):
    size, width = mate.shape[0] - EXTRA, mate.shape[1]
    pieces = (slice(0, EARLY_LANES), slice(EARLY_LANES, width))

    def body(keep_ref, mate_ref, *refs):
        odd = position()[0] == 1
        mine, mate = unpack(keep_ref), unpack(mate_ref)
        total = merged(odd, mine, mate)
        first = tuple(jnp.where(odd, m, o) for o, m in zip(mine, mate))
        rows = (jnp.ones_like(total[1]), jnp.full_like(total[2], -1.0)) + first[1:] + total[1:]
        for k, lanes in enumerate(pieces):
            send_ref, total_ref, rows_ref, first_ref = refs[4 * k : 4 * k + 4]
            pack(send_ref, tuple(t[:, lanes] for t in total))
            total_ref[...], first_ref[...] = total[0][:, lanes], first[0][:, lanes]
            put_rows(rows_ref, [row[:, lanes] for row in rows])

    out = []
    for lanes in pieces:
        wide = lanes.stop - lanes.start
        out += shaped(((size + EXTRA, wide), BF16), ((size, wide), F32), ((8, wide), F32), ((size, wide), F32))
    out = call(body, (keep, mate), out, after=after, cost=LONG)
    return out[:4], out[4:]


def level_step(bit, more, got, total, rows, entry=None, after=None):
    size, lanes = total.shape
    entries = () if entry is None else (entry,)

    def body(got_ref, total_ref, rows_ref, *refs):
        send_ref, entry_out, rows_out, *totals = refs[len(entries) :]
        upper = (position()[6] & bit) != 0
        other = unpack(got_ref)
        old = refs[0][...] if entries else jnp.zeros_like(total_ref)
        new = gather_level(upper, (old, rows_ref[0:1], rows_ref[1:2]), other)
        held = merged(upper, (total_ref[...], rows_ref[4:5], rows_ref[5:6]), other)
        pack(send_ref, held)
        entry_out[...] = new[0]
        put_rows(rows_out, new[1:] + (rows_ref[2:3], rows_ref[3:4]) + held[1:])
        if more:
            totals[0][...] = held[0]

    state = ((size, lanes), F32)
    return call(
        body, (got, total, rows, *entries),
        shaped((got.shape, BF16), state, ((8, lanes), F32), *((state,) if more else ())), after=after, cost=LONG,
    )


def entry_step(bit, with_id, got, entry, rows, first, after):
    def body(got_ref, entry_ref, rows_ref, first_ref, other_ref, keep_ref, *prev_ref):
        upper = (position()[6] & bit) != 0
        even = position()[0] == 0
        new = gather_level(upper, (entry_ref[...], rows_ref[0:1], rows_ref[1:2]), unpack(got_ref))
        last_first = rows_ref[3:4]
        link = rows_ref[2:3] * (last_first == new[2]).astype(F32)
        reached = first_ref[...] + link * new[0]
        other_ref[...] = jnp.where(even, reached, new[0]).astype(BF16)
        keep_ref[...] = jnp.where(even, new[0], reached).astype(BF16)
        if with_id:
            prev = jnp.where(even, new[2], last_first)
            prev_ref[0][...] = jnp.broadcast_to(prev[:, 0:LANES], (8, LANES))

    block = (entry.shape, BF16)
    prev = (((8, LANES), F32),) if with_id else ()
    return call(body, (got, entry, rows, first), shaped(block, block, *prev), after=after)


def local_part(which, heads, width, x, gate, read, write, stash, skip, after):
    toks = write.shape[0]
    half_w = x.shape[1] // 2
    half_h = heads // 2
    per = LANES // width
    blocks = toks // GROUP
    strip = 64

    def body(
        x_ref, gate_ref, rd_ref, wr_ref, stash_ref, skip_ref,
        a_ref, b_ref, *refs,
    ):
        *seg_out, log_cum, log_row, scores, mix, pad, tails, rows_ref = refs
        half = position()[which]
        second = half == 1
        cum_ref, step_ref = (stash_ref.at[rows] for rows in stash_rows()[:2])
        lane = lane_iota(GROUP)
        mix[...] = jnp.zeros_like(mix)
        pad[...] = jnp.zeros_like(pad)
        rows_ref[...] = jnp.zeros_like(rows_ref)
        rows_ref[0:1, 0:heads] = skip_ref[...]
        skips = jnp.where(second, pltpu.roll(rows_ref[...], LANES - half_h, 1), rows_ref[...])[0:1]
        seg_row = cum_ref[SEG_LANE : SEG_LANE + 1]
        log_row[...] = cum_ref[...] * LOG2E - jnp.log(step_ref[...]) * LOG2E
        pad[0:32] = cum_ref[...] * LOG2E
        pad[SEG_LANE : SEG_LANE + 1] = seg_row
        columns = jnp.transpose(pad[...])
        seg_col = columns[:, SEG_LANE : SEG_LANE + 1]
        log_cum[...] = jnp.where(second, pltpu.roll(columns, LANES - half_h, 1), columns)
        if seg_out:
            seg_out[0][...] = columns
        tail0 = jnp.exp(cum_ref[:, GROUP - 1 : GROUP] - cum_ref[:, 0:GROUP]) * step_ref[:, 0:GROUP]
        same = seg_row[:, 0:GROUP] == seg_row[:, GROUP - 1 : GROUP]
        pad[0:32, 0:GROUP] = jnp.where(same, tail0, 0.0)
        columns = jnp.transpose(pad[:, 0:GROUP])
        tails[...] = jnp.where(second, pltpu.roll(columns, LANES - half_h, 1), columns)
        masked = []
        for b in range(blocks):
            rows = slice(b * GROUP, (b + 1) * GROUP)
            s = dot(rd_ref[rows], wr_ref[rows], ((1,), (1,)))
            causal = lax.broadcasted_iota(jnp.int32, (GROUP, GROUP), 0) >= lax.broadcasted_iota(
                jnp.int32, (GROUP, GROUP), 1
            )
            scores[b] = jnp.where(causal & (seg_col[rows] == seg_row[:, rows]), s, 0.0)
            linked = seg_col[rows] == seg_col[b * GROUP - 1 : b * GROUP] if b else None
            masked.append(jnp.where(linked, rd_ref[rows].astype(F32), 0.0).astype(BF16) if b else None)
        for i in range(half_w // LANES):
            tile = slice(i * LANES, (i + 1) * LANES)
            there = pl.ds(pl.multiple_of(half * half_w + i * LANES, LANES), LANES)
            gains = spread(skips, i * per, width)
            carry = None
            start = jnp.ones((1, LANES), F32)
            for b in range(blocks):
                rows = slice(b * GROUP, (b + 1) * GROUP)
                slot = (i * blocks + b) % mix.shape[0]
                xb = x_ref[rows, there]
                logs = []
                for k in range(per):
                    head = i * per + k
                    cb = jnp.broadcast_to(log_cum[rows, head : head + 1], (GROUP, LANES))
                    logs.append(cb)
                    ar = log_row[pl.ds(half * half_h + head, 1), rows]
                    for low in range(0, GROUP, strip):
                        for left in range(0, min(low + strip, GROUP), LANES):
                            gap = cb[low : low + strip] - ar[:, left : left + LANES]
                            part = jnp.exp2(jnp.minimum(gap, 60.0))
                            part = part * scores[b, low : low + strip, left : left + LANES]
                            at = k * GROUP + low
                            mix[slot, at : at + strip, left : left + LANES] = part.astype(BF16)
                both = dot(mix[slot], xb)
                inner, dec_log = both[0:GROUP], logs[0]
                for k in range(1, per):
                    inner = jnp.where(lane < k * width, inner, both[k * GROUP : (k + 1) * GROUP])
                    dec_log = jnp.where(lane < k * width, dec_log, logs[k])
                dec = jnp.exp2(dec_log)
                xf = xb.astype(F32)
                y = inner + gains * xf
                if b == 1:
                    y = y + (dot(masked[b], carry[0]) + dot(masked[b], carry[1])) * dec
                else:
                    xs = (xf * spread(tails[...], i * per, width)).astype(BF16)
                    s0 = dot(wr_ref[rows], xs, ((0,), (0,)))
                    s0h = s0.astype(BF16)
                    carry = (s0h, (s0 - s0h.astype(F32)).astype(BF16))
                v = gate_ref[rows, there].astype(F32)
                sg = v / (1.0 + jnp.exp(-v))
                a_ref[rows, tile] = sg * y
                b_ref[rows, tile] = sg * (dec * start)
                start = start * dec[GROUP - 1 : GROUP]

    return call(
        body, (x, gate, read, write, stash, skip),
        shaped(((toks, half_w), F32), ((toks, half_w), F32), *((((toks, LANES), F32),) if which == 0 else ())),
        [
            pltpu.VMEM((toks, LANES), F32), pltpu.VMEM((32, toks), F32),
            pltpu.VMEM((blocks, GROUP, GROUP), F32), pltpu.VMEM((4, per * GROUP, GROUP), BF16),
            pltpu.VMEM((LANES, toks), F32), pltpu.VMEM((GROUP, LANES), F32), pltpu.VMEM((8, LANES), F32),
        ],
        after=after, cost=LONG,
    )


def gated_part(which, lanes, prev_ref, rd_ref, cum_ref, a_ref, b_ref, states, gain_ref):
    half_w = a_ref.shape[1]
    first = pl.multiple_of(position()[which] * half_w + lanes.start, LANES)
    here = pl.ds(first, lanes.stop - lanes.start)
    linked = cum_ref[:, SEG_LANE : SEG_LANE + 1] == prev_ref[0:1, 0:1]
    rm = jnp.where(linked, rd_ref[...].astype(F32), 0.0).astype(BF16)
    carried = [dot(rm, state[...]) for state in states]
    carried = carried[0] if len(carried) == 1 else jnp.concatenate(carried, axis=1)
    gated = a_ref[:, lanes] + b_ref[:, lanes] * carried
    sq = gated * gated
    part = sq[:, 0:LANES]
    for i in range(1, sq.shape[1] // LANES):
        part = part + sq[:, i * LANES : (i + 1) * LANES]
    squares = jnp.sum(jnp.transpose(part), axis=0, keepdims=True)
    return (gated * gain_ref[:, here]).astype(BF16), squares


def projected(which, lanes, quarter, rows, w_ref, g):
    half_w, cols = w_ref.shape[0] // 2, w_ref.shape[1] // 4
    here = pl.multiple_of(position()[which] * half_w + lanes.start, LANES)
    first = pl.multiple_of(position()[2 + quarter] * cols + rows.start, LANES)
    block = w_ref[pl.ds(here, lanes.stop - lanes.start), pl.ds(first, rows.stop - rows.start)]
    return dot(block, g, ((0,), (1,)))


def with_squares(y, squares):
    high = squares.astype(BF16).astype(F32)
    middle = (squares - high).astype(BF16).astype(F32)
    row = lax.broadcasted_iota(jnp.int32, (EXTRA, squares.shape[1]), 0)
    rows = jnp.where(row == 0, high, jnp.where(row == 1, middle, squares - high - middle))
    return jnp.concatenate([y, rows], axis=0).astype(BF16)


def split_squares(ref):
    size = ref.shape[0] - EXTRA
    whole = ref[...].astype(F32)
    return whole[0:size], whole[size : size + 1] + (whole[size + 1 : size + 2] + whole[size + 2 : size + 3])


def gated_sums(which, lanes, prev, read, cum, a, b, states, gain, weight, partial=None, squares=None):
    toks = a.shape[0]
    cols = weight.shape[1] // 4
    earlier = () if partial is None else (partial, squares)

    def body(prev_ref, rd_ref, cum_ref, a_ref, b_ref, gain_ref, w_ref, *refs):
        states = refs[: len(states_in)]
        old, (g_ref, s_ref, y_ref) = refs[len(states_in) : -3], refs[-3:]
        g, s = gated_part(which, lanes, prev_ref, rd_ref, cum_ref, a_ref, b_ref, states, gain_ref)
        g_ref[...] = g
        s_ref[...] = s + old[1][...] if old else s
        for quarter in range(2):
            y = projected(which, lanes, quarter, slice(0, cols), w_ref, g)
            y_ref[quarter] = y + old[0][quarter] if old else y

    states_in = states
    return call(
        body, (prev, read, cum, a, b, gain, weight, *states, *earlier),
        shaped(((toks, lanes.stop - lanes.start), BF16), ((1, toks), F32), ((2, cols, toks), F32)),
    )


def gated_last(lanes, rows, prev, read, cum, a, b, state, gain, weight, partial, squares):
    toks = a.shape[0]

    def body(prev_ref, rd_ref, cum_ref, a_ref, b_ref, e_ref, gain_ref, w_ref, p_ref, s_ref, g_ref, y_ref):
        g, s = gated_part(1, lanes, prev_ref, rd_ref, cum_ref, a_ref, b_ref, (e_ref,), gain_ref)
        g_ref[...] = g
        y = p_ref[0, rows] + projected(1, lanes, 0, rows, w_ref, g)
        y_ref[...] = with_squares(y, s_ref[...] + s)

    return call(
        body, (prev, read, cum, a, b, state, gain, weight, partial, squares),
        shaped(((toks, lanes.stop - lanes.start), BF16), ((rows.stop - rows.start + EXTRA, toks), BF16)),
    )


def project_last(lanes, pieces, g, partial, weight, after):
    def body(g_ref, p_ref, w_ref, *outs):
        for (quarter, rows, dtype), y_ref in zip(pieces, outs):
            y = p_ref[quarter, rows] + projected(1, lanes, quarter, rows, w_ref, g_ref[...])
            y_ref[...] = y.astype(dtype)

    toks = g.shape[0]
    out = shaped(*[((rows.stop - rows.start, toks), dtype) for _, rows, dtype in pieces])
    return call(body, (g, partial, weight), out, after=after)


def project_whole(quarter, groups, gs, weight, pieces, adds=(), after=None):
    cols = weight.shape[1] // 4
    toks = gs[0].shape[0]
    step = cols // pieces

    def body(w_ref, *refs):
        g_refs, add_refs, outs = refs[: len(gs)], refs[len(gs) : len(gs) + len(adds)], refs[len(gs) + len(adds) :]
        y = sum(
            projected(which, lanes, quarter, slice(0, cols), w_ref, g_ref[...])
            for (which, lanes), g_ref in zip(groups, g_refs)
        )
        if add_refs:
            outs[0][...] = y + jnp.concatenate([r[...].astype(F32) for r in add_refs], axis=0)
        else:
            for k, y_ref in enumerate(outs):
                y_ref[...] = y[k * step : (k + 1) * step].astype(BF16)

    out = shaped(((cols, toks), F32)) if adds else shaped(*[((step, toks), BF16)] * pieces)
    return call(body, (weight, *gs, *adds), out, after=after)


def add_first(y_far, to_near, got_near):
    def body(y_ref, mine_ref, got_ref, out_ref):
        got, squares = split_squares(got_ref)
        out_ref[...] = with_squares(y_ref[...] + got, split_squares(mine_ref)[1] + squares)

    return call(body, (y_far, to_near, got_near), jax.ShapeDtypeStruct(got_near.shape, BF16))


def add_second(y_far, got_near, after):
    def body(y_ref, got_ref, out_ref):
        out_ref[...] = (y_ref[...] + got_ref[...].astype(F32)).astype(BF16)

    return call(body, (y_far, got_near), jax.ShapeDtypeStruct(got_near.shape, BF16), after=after)


def finish(rows, y_own, inputs, out=None, features=None):
    size, toks = y_own.shape
    parts = 2
    step = (rows.stop - rows.start) // parts
    first = out is None

    def body(own_ref, far_ref, factor_ref, *refs):
        out_hbm, *more, out_ref, sems = refs if first else refs[1:]
        if first:
            inv = lax.rsqrt((split_squares(factor_ref)[1] + split_squares(far_ref)[1]) / features + EPS)
            more[0][...] = inv
        else:
            inv = factor_ref[...]
        copies = []
        for k in range(parts):
            here = slice(k * step, (k + 1) * step)
            there = slice(rows.start + here.start, rows.start + here.stop)
            out_ref[here] = ((own_ref[there] + far_ref[here].astype(F32)) * inv).astype(BF16)
            copies.append(pltpu.make_async_copy(out_ref.at[here], out_hbm.at[there], sems.at[k]))
            copies[-1].start()
        for copy in copies:
            copy.wait()

    vm, where = pl.BlockSpec(memory_space=pltpu.VMEM), pl.BlockSpec(memory_space=pl.ANY)
    result = jax.ShapeDtypeStruct((size, toks), BF16)
    return pl.pallas_call(
        body,
        in_specs=[vm] * 3 + ([] if first else [where]),
        out_specs=[where, vm] if first else where,
        out_shape=[result, jax.ShapeDtypeStruct((1, toks), F32)] if first else result,
        scratch_shapes=[pltpu.VMEM((rows.stop - rows.start, toks), BF16), pltpu.SemaphoreType.DMA((parts,))],
        input_output_aliases={} if first else {3: 0},
        compiler_params=pltpu.CompilerParams(vmem_limit_bytes=VMEM),
        cost_estimate=CHEAP,
    )(y_own, *inputs, *(() if first else (out,)))


def on_device(
    n_seq, n_tp, head_input, gate_input, write_vecs, read_vecs, step_raw, segment_ids,
    decay_log, step_bias, skip_gain, norm_gain, out_weight,
):
    heads = decay_log.shape[0]
    toks, feats = head_input.shape
    width = feats // heads
    def swap(a, bit):
        return lax.ppermute(a, "seq", [(i, i ^ bit) for i in range(n_seq)])

    def across(a, bit):
        return lax.ppermute(a, "tp", [(i, i ^ bit) for i in range(n_tp)])

    other, stash = prepare(
        heads, width, step_raw, segment_ids.reshape(1, toks), decay_log.reshape(1, heads),
        step_bias.reshape(1, heads), head_input, write_vecs,
    )
    mate = swap(other, 1)
    keep = kept_state(width, stash, head_input, write_vecs)
    local = (heads, width, head_input, gate_input, read_vecs, write_vecs, stash, skip_gain.reshape(1, heads))
    a_keep, b_keep, log_cum = local_part(0, *local, keep)
    sent, totals, rows, firsts = zip(*pair_step(keep, mate, a_keep))
    entries = [()] * 2
    bit = 2
    while 2 * bit < n_seq:
        more = 4 * bit < n_seq
        got = [swap(piece, bit) for piece in sent]
        early = level_step(bit, more, got[0], totals[0], rows[0], *entries[0])
        late = level_step(bit, more, got[1], totals[1], rows[1], *entries[1], after=early[0])
        sent, entries, rows, *totals = zip(early, late)
        totals, entries = totals[0] if more else (), [(entry,) for entry in entries]
        bit *= 2
    a_other, b_other, *_ = local_part(1, *local, sent[1])
    half_w = feats // 2
    quarter = out_weight.shape[1] // 4
    one, two = slice(0, EARLY_LANES), slice(EARLY_LANES, half_w)
    top, rest, every = slice(0, EARLY_ROWS), slice(EARLY_ROWS, quarter), slice(0, quarter)
    send_one, keep_one, prev = entry_step(
        bit, True, swap(sent[0], bit), *entries[0], rows[0], firsts[0], a_other
    )
    other_one = swap(send_one, 1)
    send_two, keep_two = entry_step(bit, False, swap(sent[1], bit), *entries[1], rows[1], firsts[1], send_one)
    other_two = swap(send_two, 1)
    gain = norm_gain.reshape(1, feats)
    kept, rest_of = (prev, read_vecs, log_cum, a_keep, b_keep), (prev, read_vecs, log_cum, a_other, b_other)
    g_near, squares, partial = gated_sums(0, one, *kept, (keep_one,), gain, out_weight)
    g_keep, squares, partial = gated_sums(0, two, *kept, (keep_two,), gain, out_weight, partial, squares)
    g_one, squares, partial = gated_sums(1, one, *rest_of, (other_one,), gain, out_weight, partial, squares)
    g_two, near_top = gated_last(two, top, *rest_of, other_two, gain, out_weight, partial, squares)
    got_top = across(near_top, 1)
    near_rest, far_top, far_rest = project_last(
        two, ((0, rest, BF16), (1, top, F32), (1, rest, F32)), g_two, partial, out_weight, near_top
    )
    got_rest = across(near_rest, 1)
    to_far_top = add_first(far_top, near_top, got_top)
    got_far_top = across(to_far_top, 2)
    to_far_rest = add_second(far_rest, got_rest, to_far_top)
    got_far_rest = across(to_far_rest, 2)
    groups, gs = ((0, one), (0, two), (1, one), (1, two)), (g_near, g_keep, g_one, g_two)
    y_near = project_whole(2, groups, gs, out_weight, NEAR_PIECES, after=to_far_rest)
    got_own = tuple(across(piece, 1) for piece in y_near)
    (y_own,) = project_whole(3, groups, gs, out_weight, 1, got_own)
    out, inv = finish(top, y_own, (got_far_top, to_far_top), features=feats * n_tp)
    return finish(rest, y_own, (got_far_rest, inv), out)


def solution(mesh):
    in_specs = (
        P("seq", "tp"),
        P("seq", "tp"),
        P("seq", None),
        P("seq", None),
        P("tp", "seq"),
        P("seq"),
        P("tp"),
        P("tp"),
        P("tp"),
        P("tp"),
        P("tp", None),
    )
    out_specs = P("tp", "seq")
    return jax.shard_map(
        functools.partial(on_device, mesh.shape["seq"], mesh.shape["tp"]),
        mesh=mesh, in_specs=in_specs, out_specs=out_specs, check_vma=False,
    )
```

```python
import functools

import jax
import jax.numpy as jnp
from jax import lax
from jax.experimental import pallas as pl
from jax.experimental.pallas import tpu as pltpu
from jax.sharding import PartitionSpec as P

GROUP = 256
LANES = 128
EPS = 1e-05
LOG2E = 1.4426950408889634
SEG_LANE = 24
EXTRA = 8
EARLY_ROWS = 384
NEAR_PIECES = 4
EARLY_LANES = 384
VMEM = 16 * 1024 * 1024
VMEM_ALL = 56 * 1024 * 1024
CHEAP = pl.CostEstimate(flops=1000, bytes_accessed=1000, transcendentals=0)
LONG = pl.CostEstimate(flops=4_000_000_000, bytes_accessed=1000, transcendentals=0)
F32 = jnp.float32
BF16 = jnp.bfloat16


def dot(a, b, dims=((1,), (0,))):
    return lax.dot_general(a, b, (dims, ((), ())), preferred_element_type=F32)


def lane_iota(rows):
    return lax.broadcasted_iota(jnp.int32, (rows, LANES), 1)


def spread(cols, first, width):
    rows = cols.shape[0]
    per = LANES // width
    lane = lane_iota(rows)
    out = jnp.broadcast_to(cols[:, first : first + 1], (rows, LANES))
    for k in range(1, per):
        nxt = jnp.broadcast_to(cols[:, first + k : first + k + 1], (rows, LANES))
        out = jnp.where(lane < k * width, out, nxt)
    return out


def position():
    place, rank = lax.axis_index("seq"), lax.axis_index("tp")
    odd = place & 1
    far = rank ^ 2
    return odd, 1 - odd, far ^ 1, far, rank ^ 1, rank, place


def call(body, args, out_shape, scratch=(), after=None, cost=CHEAP):
    vm = pl.BlockSpec(memory_space=pltpu.VMEM)
    specs = [vm] * len(args)
    operands = list(args)
    kernel = body
    if after is not None:
        specs.append(pl.BlockSpec(memory_space=pl.ANY))
        operands.append(after)
        at = len(operands) - 1

        def kernel(*refs):
            body(*refs[:at], *refs[at + 1 :])

    return pl.pallas_call(
        kernel,
        in_specs=specs,
        out_specs=jax.tree.map(lambda _: vm, out_shape),
        out_shape=out_shape,
        scratch_shapes=list(scratch),
        compiler_params=pltpu.CompilerParams(vmem_limit_bytes=VMEM),
        cost_estimate=cost,
    )(*operands)


def shaped(*shapes):
    return [jax.ShapeDtypeStruct(shape, dtype) for shape, dtype in shapes]


def pack(out_ref, total):
    state, through, last = total
    high = through.astype(BF16).astype(F32)
    row = lax.broadcasted_iota(jnp.int32, (EXTRA, state.shape[1]), 0)
    rows = jnp.where(row == 0, high, jnp.where(row == 1, through - high, last))
    out_ref[...] = jnp.concatenate([state, rows], axis=0).astype(BF16)


def unpack(ref):
    size = ref.shape[0] - EXTRA
    whole = ref[...].astype(F32)
    return whole[0:size], whole[size : size + 1] + whole[size + 1 : size + 2], whole[size + 2 : size + 3]


def merged(swapped, one, two):
    later = jnp.where(swapped, one[1], two[1])
    link = later * (one[2] == two[2]).astype(F32)
    state = jnp.where(swapped, 1.0, link) * one[0] + jnp.where(swapped, link, 1.0) * two[0]
    return state, one[1] * two[1], jnp.where(swapped, one[2], two[2])


def ordered(swapped, one, two):
    firsts = tuple(jnp.where(swapped, t, o) for o, t in zip(one, two))
    seconds = tuple(jnp.where(swapped, o, t) for o, t in zip(one, two))
    return firsts, seconds


def stash_rows():
    return slice(0, 32), slice(32, 64), slice(64, 96), slice(96, 104)


def put_rows(rows_ref, rows):
    lanes = rows_ref.shape[1]
    for at, row in enumerate(rows):
        rows_ref[at : at + 1] = jnp.broadcast_to(row, (1, lanes))


def some_state(half, half_w, lanes, width, vecs, tails_ref, through_row, last, x_ref, first_lane, out_ref):
    state = vecs.shape[0]
    per = LANES // width
    half_h = half_w // width
    skipped = lanes.start // width
    lane = lane_iota(state)
    mine = jnp.where(half == 1, pltpu.roll(through_row, LANES - half_h, 1), through_row)
    own, through = [], []
    for i in range((lanes.stop - lanes.start) // LANES):
        written = []
        for k in range(per):
            row = tails_ref[pl.ds(half * half_h + skipped + i * per + k, 1), :]
            written.append((vecs * row).astype(BF16))
        here = pl.ds(pl.multiple_of(first_lane + i * LANES, LANES), LANES)
        both = dot(jnp.concatenate(written, axis=0), x_ref[:, here])
        tile = both[0:state]
        for k in range(1, per):
            tile = jnp.where(lane < k * width, tile, both[k * state : (k + 1) * state])
        own.append(tile)
        through.append(spread(mine[0:1], skipped + i * per, width))
    ids = jnp.broadcast_to(last, (1, lanes.stop - lanes.start))
    group = (jnp.concatenate(own, axis=1), jnp.concatenate(through, axis=1), ids)
    pack(out_ref, group)


def prepare(heads, width, raw, seg, decay_log, bias, x, write):
    toks, state = write.shape
    half_w = x.shape[1] // 2
    blocks = toks // GROUP
    arrays = (raw, seg, decay_log, bias, write, x)

    def body(*refs):
        hbm, (other_ref, stash_ref) = refs[: len(arrays)], refs[len(arrays) : -8]
        raw_ref, seg_ref, dl_ref, sb_ref, wr_ref, x_ref, rows, sems = refs[-8:]
        half = position()[1]
        lanes = pl.ds(pl.multiple_of(half * half_w, LANES), EARLY_LANES)
        sources = (*hbm[:5], hbm[5].at[:, lanes])
        copies = [
            pltpu.make_async_copy(src, dst, sems.at[k])
            for k, (src, dst) in enumerate(zip(sources, (raw_ref, seg_ref, dl_ref, sb_ref, wr_ref, x_ref)))
        ]
        for copy in copies:
            copy.start()
        rows[...] = jnp.zeros_like(rows)
        tri = (
            lax.broadcasted_iota(jnp.int32, (GROUP, GROUP), 0)
            <= lax.broadcasted_iota(jnp.int32, (GROUP, GROUP), 1)
        ).astype(BF16)
        stash_ref[...] = jnp.zeros_like(stash_ref)
        cum_rows, step_rows, tail_rows, sum_rows = stash_rows()
        for copy in copies[:5]:
            copy.wait()
        vecs = jnp.transpose(wr_ref[...].astype(F32))
        rows[0:1, 0:heads] = dl_ref[...]
        rows[1:2, 0:heads] = sb_ref[...]
        stash_ref[0:heads] = raw_ref[...].astype(F32)
        params = jnp.transpose(rows[...])[0:32]
        z = stash_ref[cum_rows] + params[:, 1:2]
        step = jnp.maximum(z, 0.0) + jnp.log1p(jnp.exp(-jnp.abs(z)))
        rate = -jnp.exp(params[:, 0:1]) * step
        cum, full = [], []
        base = jnp.zeros((32, 1), F32)
        for b in range(blocks):
            r = rate[:, b * GROUP : (b + 1) * GROUP]
            r1 = r.astype(BF16)
            d1 = r - r1.astype(F32)
            r2 = d1.astype(BF16)
            r3 = (d1 - r2.astype(F32)).astype(BF16)
            c = dot(r1, tri) + (dot(r2, tri) + dot(r3, tri))
            cum.append(c)
            full.append(c + base)
            base = base + c[:, GROUP - 1 : GROUP]
        seg_row = seg_ref[...].astype(F32)
        last = seg_row[:, toks - 1 : toks]
        tail = jnp.exp(base - jnp.concatenate(full, axis=1)) * step
        stash_ref[cum_rows] = jnp.concatenate(cum, axis=1)
        stash_ref[SEG_LANE : SEG_LANE + 1] = seg_row
        stash_ref[step_rows] = step
        stash_ref[tail_rows] = jnp.where(seg_row == last, tail, 0.0)
        rows[...] = jnp.zeros_like(rows)
        rows[0:32] = jnp.broadcast_to(jnp.exp(base), (32, LANES))
        sums = jnp.transpose(rows[...])[0:8]
        stash_ref[sum_rows, 0:LANES] = sums
        copies[5].wait()
        piece = slice(0, EARLY_LANES)
        some_state(half, half_w, piece, width, vecs, stash_ref.at[tail_rows], sums, last, x_ref, 0, other_ref)

    vm = pl.BlockSpec(memory_space=pltpu.VMEM)
    out_shape = shaped(((state + EXTRA, EARLY_LANES), BF16), ((stash_rows()[-1].stop, toks), F32))
    return pl.pallas_call(
        body,
        in_specs=[pl.BlockSpec(memory_space=pltpu.HBM)] * len(arrays),
        out_specs=[vm] * len(out_shape),
        out_shape=out_shape,
        scratch_shapes=[
            *[pltpu.VMEM(a.shape, a.dtype) for a in arrays[:5]], pltpu.VMEM((toks, EARLY_LANES), BF16),
            pltpu.VMEM((LANES, LANES), F32), pltpu.SemaphoreType.DMA((len(arrays),)),
        ],
        compiler_params=pltpu.CompilerParams(vmem_limit_bytes=VMEM_ALL),
        cost_estimate=LONG,
    )(*arrays)


def more_states(width, stash, x, write):
    toks, state = write.shape
    half_w = x.shape[1] // 2
    one, two = slice(0, EARLY_LANES), slice(EARLY_LANES, half_w)
    pieces = ((1, two), (0, one), (0, two))

    def body(stash_ref, x_ref, wr_ref, *outs):
        _, _, tail_rows, sum_rows = stash_rows()
        vecs = jnp.transpose(wr_ref[...].astype(F32))
        last = stash_ref[SEG_LANE : SEG_LANE + 1, toks - 1 : toks]
        sums = stash_ref[sum_rows, 0:LANES]
        tails_ref = stash_ref.at[tail_rows]
        for (which, lanes), out_ref in zip(pieces, outs):
            half = position()[which]
            first = half * half_w + lanes.start
            some_state(half, half_w, lanes, width, vecs, tails_ref, sums, last, x_ref, first, out_ref)

    out = shaped(*[((state + EXTRA, lanes.stop - lanes.start), BF16) for _, lanes in pieces])
    return call(body, (stash, x, write), out, cost=LONG)


def gather_level(upper, entry, other):
    state, through, last_id = entry
    link = through * ((last_id < 0) | (other[2] == last_id)).astype(F32)
    state = state + jnp.where(upper, link, 0.0) * other[0]
    last_id = jnp.where(upper & (last_id < 0), other[2], last_id)
    return state, through * jnp.where(upper, other[1], 1.0), last_id


def pair_step(keep, mate, after=None):
    size, lanes = mate.shape[0] - EXTRA, mate.shape[1]

    def body(keep_ref, mate_ref, send_ref, total_ref, rows_ref, first_ref):
        odd = position()[0] == 1
        mine, mate = unpack(keep_ref), unpack(mate_ref)
        total = merged(odd, mine, mate)
        first = tuple(jnp.where(odd, m, o) for o, m in zip(mine, mate))
        pack(send_ref, total)
        total_ref[...], first_ref[...] = total[0], first[0]
        put_rows(rows_ref, (jnp.ones_like(total[1]), jnp.full_like(total[2], -1.0)) + first[1:] + total[1:])

    state = ((size, lanes), F32)
    return call(
        body, (keep, mate), shaped((mate.shape, BF16), state, ((8, lanes), F32), state), after=after, cost=LONG
    )


def level_step(bit, more, got, total, rows, entry=None, after=None):
    size, lanes = total.shape
    entries = () if entry is None else (entry,)

    def body(got_ref, total_ref, rows_ref, *refs):
        send_ref, entry_out, rows_out, *totals = refs[len(entries) :]
        upper = (position()[6] & bit) != 0
        other = unpack(got_ref)
        old = refs[0][...] if entries else jnp.zeros_like(total_ref)
        new = gather_level(upper, (old, rows_ref[0:1], rows_ref[1:2]), other)
        held = merged(upper, (total_ref[...], rows_ref[4:5], rows_ref[5:6]), other)
        pack(send_ref, held)
        entry_out[...] = new[0]
        put_rows(rows_out, new[1:] + (rows_ref[2:3], rows_ref[3:4]) + held[1:])
        if more:
            totals[0][...] = held[0]

    state = ((size, lanes), F32)
    return call(
        body, (got, total, rows, *entries),
        shaped((got.shape, BF16), state, ((8, lanes), F32), *((state,) if more else ())), after=after, cost=LONG,
    )


def entry_step(bit, with_id, got, entry, rows, first, after):
    def body(got_ref, entry_ref, rows_ref, first_ref, other_ref, keep_ref, *prev_ref):
        upper = (position()[6] & bit) != 0
        even = position()[0] == 0
        new = gather_level(upper, (entry_ref[...], rows_ref[0:1], rows_ref[1:2]), unpack(got_ref))
        last_first = rows_ref[3:4]
        link = rows_ref[2:3] * (last_first == new[2]).astype(F32)
        reached = first_ref[...] + link * new[0]
        other_ref[...] = jnp.where(even, reached, new[0]).astype(BF16)
        keep_ref[...] = jnp.where(even, new[0], reached).astype(BF16)
        if with_id:
            prev = jnp.where(even, new[2], last_first)
            prev_ref[0][...] = jnp.broadcast_to(prev[:, 0:LANES], (8, LANES))

    block = (entry.shape, BF16)
    prev = (((8, LANES), F32),) if with_id else ()
    return call(body, (got, entry, rows, first), shaped(block, block, *prev), after=after)


def local_setup(heads, width, read, write, stash, skip, after):
    toks = write.shape[0]
    half_h = heads // 2
    blocks = toks // GROUP

    def body(
        rd_ref, wr_ref, stash_ref, skip_ref,
        scores, linked_ref, log_cum, log_row, tails, skips, seg_out, pad, rows_ref,
    ):
        cum_ref, step_ref = (stash_ref.at[rows] for rows in stash_rows()[:2])
        second = [position()[which] == 1 for which in range(2)]
        pad[...] = jnp.zeros_like(pad)
        rows_ref[...] = jnp.zeros_like(rows_ref)
        rows_ref[0:1, 0:heads] = skip_ref[...]
        turned = pltpu.roll(rows_ref[...], LANES - half_h, 1)
        for which in range(2):
            skips[which] = jnp.where(second[which], turned, rows_ref[...])
        seg_row = cum_ref[SEG_LANE : SEG_LANE + 1]
        log_row[...] = cum_ref[...] * LOG2E - jnp.log(step_ref[...]) * LOG2E
        pad[0:32] = cum_ref[...] * LOG2E
        pad[SEG_LANE : SEG_LANE + 1] = seg_row
        columns = jnp.transpose(pad[...])
        seg_col = columns[:, SEG_LANE : SEG_LANE + 1]
        turned = pltpu.roll(columns, LANES - half_h, 1)
        for which in range(2):
            log_cum[which] = jnp.where(second[which], turned, columns)
        seg_out[...] = columns
        tail0 = jnp.exp(cum_ref[:, GROUP - 1 : GROUP] - cum_ref[:, 0:GROUP]) * step_ref[:, 0:GROUP]
        same = seg_row[:, 0:GROUP] == seg_row[:, GROUP - 1 : GROUP]
        pad[0:32, 0:GROUP] = jnp.where(same, tail0, 0.0)
        columns = jnp.transpose(pad[:, 0:GROUP])
        turned = pltpu.roll(columns, LANES - half_h, 1)
        for which in range(2):
            tails[which] = jnp.where(second[which], turned, columns)
        causal = lax.broadcasted_iota(jnp.int32, (GROUP, GROUP), 0) >= lax.broadcasted_iota(
            jnp.int32, (GROUP, GROUP), 1
        )
        for b in range(blocks):
            rows = slice(b * GROUP, (b + 1) * GROUP)
            s = dot(rd_ref[rows], wr_ref[rows], ((1,), (1,)))
            scores[b] = jnp.where(causal & (seg_col[rows] == seg_row[:, rows]), s, 0.0)
        linked = seg_col[GROUP:] == seg_col[GROUP - 1 : GROUP]
        linked_ref[...] = jnp.where(linked, rd_ref[GROUP:].astype(F32), 0.0).astype(BF16)

    return call(
        body, (read, write, stash, skip),
        shaped(
            ((blocks, GROUP, GROUP), F32), ((toks - GROUP, read.shape[1]), BF16), ((2, toks, LANES), F32),
            ((32, toks), F32), ((2, GROUP, LANES), F32), ((2, 8, LANES), F32), ((toks, LANES), F32),
        ),
        [pltpu.VMEM((LANES, toks), F32), pltpu.VMEM((8, LANES), F32)],
        cost=LONG, after=after,
    )


def local_part(which, tiles, heads, width, x, gate, write, setup, after):
    toks = write.shape[0]
    half_w = x.shape[1] // 2
    half_h = heads // 2
    per = LANES // width
    blocks = toks // GROUP
    strip = 64

    def body(
        x_ref, gate_ref, wr_ref, scores, linked_ref, log_cum, log_row, tails, skips, a_ref, b_ref, mix
    ):
        half = position()[which]
        lane = lane_iota(GROUP)
        for slot in range(mix.shape[0]):
            for k in range(per):
                mix[slot, k * GROUP : k * GROUP + LANES, LANES:] = jnp.zeros((LANES, GROUP - LANES), BF16)
        for n, i in enumerate(tiles):
            there = pl.ds(pl.multiple_of(half * half_w + i * LANES, LANES), LANES)
            tile = slice(n * LANES, (n + 1) * LANES)
            gains = spread(skips[which, 0:1], i * per, width)
            carry = None
            start = jnp.ones((1, LANES), F32)
            for b in range(blocks):
                rows = slice(b * GROUP, (b + 1) * GROUP)
                slot = (n * blocks + b) % mix.shape[0]
                xb = x_ref[rows, there]
                logs = []
                for k in range(per):
                    head = i * per + k
                    cb = jnp.broadcast_to(log_cum[which, rows, head : head + 1], (GROUP, LANES))
                    logs.append(cb)
                    ar = log_row[pl.ds(half * half_h + head, 1), rows]
                    for low in range(0, GROUP, strip):
                        for left in range(0, min(low + strip, GROUP), LANES):
                            gap = cb[low : low + strip] - ar[:, left : left + LANES]
                            part = jnp.exp2(jnp.minimum(gap, 60.0))
                            part = part * scores[b, low : low + strip, left : left + LANES]
                            at = k * GROUP + low
                            mix[slot, at : at + strip, left : left + LANES] = part.astype(BF16)
                both = dot(mix[slot], xb)
                inner, dec_log = both[0:GROUP], logs[0]
                for k in range(1, per):
                    inner = jnp.where(lane < k * width, inner, both[k * GROUP : (k + 1) * GROUP])
                    dec_log = jnp.where(lane < k * width, dec_log, logs[k])
                dec = jnp.exp2(dec_log)
                xf = xb.astype(F32)
                y = inner + gains * xf
                if b == 1:
                    y = y + (dot(linked_ref[...], carry[0]) + dot(linked_ref[...], carry[1])) * dec
                else:
                    xs = (xf * spread(tails[which], i * per, width)).astype(BF16)
                    s0 = dot(wr_ref[rows], xs, ((0,), (0,)))
                    s0h = s0.astype(BF16)
                    carry = (s0h, (s0 - s0h.astype(F32)).astype(BF16))
                v = gate_ref[rows, there].astype(F32)
                sg = v / (1.0 + jnp.exp(-v))
                a_ref[rows, tile] = sg * y
                b_ref[rows, tile] = sg * (dec * start)
                start = start * dec[GROUP - 1 : GROUP]

    out = ((toks, len(tiles) * LANES), F32)
    return call(
        body, (x, gate, write, *setup), shaped(out, out), [pltpu.VMEM((4, per * GROUP, GROUP), BF16)],
        cost=LONG, after=after,
    )


def side_by_side(refs):
    values = [ref[...] for ref in refs]
    return values[0] if len(values) == 1 else jnp.concatenate(values, axis=1)


def gated_part(which, lanes, prev_ref, rd_ref, cum_ref, a_refs, b_refs, states, gain_ref):
    half_w = gain_ref.shape[1] // 2
    first = pl.multiple_of(position()[which] * half_w + lanes.start, LANES)
    here = pl.ds(first, lanes.stop - lanes.start)
    linked = cum_ref[:, SEG_LANE : SEG_LANE + 1] == prev_ref[0:1, 0:1]
    rm = jnp.where(linked, rd_ref[...].astype(F32), 0.0).astype(BF16)
    carried = [dot(rm, state[...]) for state in states]
    carried = carried[0] if len(carried) == 1 else jnp.concatenate(carried, axis=1)
    gated = side_by_side(a_refs) + side_by_side(b_refs) * carried
    sq = gated * gated
    part = sq[:, 0:LANES]
    for i in range(1, sq.shape[1] // LANES):
        part = part + sq[:, i * LANES : (i + 1) * LANES]
    squares = jnp.sum(jnp.transpose(part), axis=0, keepdims=True)
    return (gated * gain_ref[:, here]).astype(BF16), squares


def projected(which, lanes, quarter, rows, w_ref, g):
    half_w, cols = w_ref.shape[0] // 2, w_ref.shape[1] // 4
    here = pl.multiple_of(position()[which] * half_w + lanes.start, LANES)
    first = pl.multiple_of(position()[2 + quarter] * cols + rows.start, LANES)
    block = w_ref[pl.ds(here, lanes.stop - lanes.start), pl.ds(first, rows.stop - rows.start)]
    return dot(block, g, ((0,), (1,)))


def with_squares(y, squares):
    high = squares.astype(BF16).astype(F32)
    middle = (squares - high).astype(BF16).astype(F32)
    row = lax.broadcasted_iota(jnp.int32, (EXTRA, squares.shape[1]), 0)
    rows = jnp.where(row == 0, high, jnp.where(row == 1, middle, squares - high - middle))
    return jnp.concatenate([y, rows], axis=0).astype(BF16)


def split_squares(ref):
    size = ref.shape[0] - EXTRA
    whole = ref[...].astype(F32)
    return whole[0:size], whole[size : size + 1] + (whole[size + 1 : size + 2] + whole[size + 2 : size + 3])


def gated_sums(which, lanes, prev, read, seg, a, b, states, gain, weight, partial=None, squares=None):
    toks = read.shape[0]
    cols = weight.shape[1] // 4
    earlier = () if partial is None else (partial, squares)
    ends = [0, len(a), len(a) + len(b), len(a) + len(b) + len(states)]

    def body(prev_ref, rd_ref, seg_ref, gain_ref, w_ref, *refs):
        a_refs, b_refs, s_refs = (refs[low:high] for low, high in zip(ends, ends[1:]))
        old, (g_ref, s_ref, y_ref) = refs[ends[-1] : -3], refs[-3:]
        g, s = gated_part(which, lanes, prev_ref, rd_ref, seg_ref, a_refs, b_refs, s_refs, gain_ref)
        g_ref[...] = g
        s_ref[...] = s + old[1][...] if old else s
        y = projected(which, lanes, 0, slice(0, cols), w_ref, g)
        y_ref[...] = y + old[0][...] if old else y

    return call(
        body, (prev, read, seg, gain, weight, *a, *b, *states, *earlier),
        shaped(((toks, lanes.stop - lanes.start), BF16), ((1, toks), F32), ((cols, toks), F32)),
    )


def gated_last(lanes, rows, prev, read, seg, a, b, state, gain, weight, partial, squares):
    toks = read.shape[0]

    def body(prev_ref, rd_ref, seg_ref, a_ref, b_ref, e_ref, gain_ref, w_ref, p_ref, s_ref, g_ref, y_ref):
        g, s = gated_part(1, lanes, prev_ref, rd_ref, seg_ref, (a_ref,), (b_ref,), (e_ref,), gain_ref)
        g_ref[...] = g
        y = p_ref[rows] + projected(1, lanes, 0, rows, w_ref, g)
        y_ref[...] = with_squares(y, s_ref[...] + s)

    return call(
        body, (prev, read, seg, a, b, state, gain, weight, partial, squares),
        shaped(((toks, lanes.stop - lanes.start), BF16), ((rows.stop - rows.start + EXTRA, toks), BF16)),
    )


def project_next(groups, gs, top, rest, partial, weight, after):
    toks = gs[0].shape[0]

    def body(p_ref, w_ref, *refs):
        g_refs, (near_ref, top_ref, rest_ref) = refs[: len(gs)], refs[len(gs) :]
        which, lanes = groups[-1]
        near = p_ref[rest] + projected(which, lanes, 0, rest, w_ref, g_refs[-1][...])
        near_ref[...] = near.astype(BF16)
        for rows, y_ref in ((top, top_ref), (rest, rest_ref)):
            y_ref[...] = sum(
                projected(which, lanes, 1, rows, w_ref, g_ref[...])
                for (which, lanes), g_ref in zip(groups, g_refs)
            )

    size = rest.stop - rest.start
    out = shaped(((size, toks), BF16), ((top.stop, toks), F32), ((size, toks), F32))
    return call(body, (partial, weight, *gs), out, after=after)


def project_whole(quarter, groups, gs, weight, pieces, adds=(), after=None):
    cols = weight.shape[1] // 4
    toks = gs[0].shape[0]
    step = cols // pieces

    def body(w_ref, *refs):
        g_refs, add_refs, outs = refs[: len(gs)], refs[len(gs) : len(gs) + len(adds)], refs[len(gs) + len(adds) :]
        y = sum(
            projected(which, lanes, quarter, slice(0, cols), w_ref, g_ref[...])
            for (which, lanes), g_ref in zip(groups, g_refs)
        )
        if add_refs:
            outs[0][...] = y + jnp.concatenate([r[...].astype(F32) for r in add_refs], axis=0)
        else:
            for k, y_ref in enumerate(outs):
                y_ref[...] = y[k * step : (k + 1) * step].astype(BF16)

    out = shaped(((cols, toks), F32)) if adds else shaped(*[((step, toks), BF16)] * pieces)
    return call(body, (weight, *gs, *adds), out, after=after)


def add_first(y_far, to_near, got_near):
    def body(y_ref, mine_ref, got_ref, out_ref):
        got, squares = split_squares(got_ref)
        out_ref[...] = with_squares(y_ref[...] + got, split_squares(mine_ref)[1] + squares)

    return call(body, (y_far, to_near, got_near), jax.ShapeDtypeStruct(got_near.shape, BF16))


def add_second(y_far, got_near, after):
    def body(y_ref, got_ref, out_ref):
        out_ref[...] = (y_ref[...] + got_ref[...].astype(F32)).astype(BF16)

    return call(body, (y_far, got_near), jax.ShapeDtypeStruct(got_near.shape, BF16), after=after)


def finish(rows, y_own, inputs, out=None, features=None):
    size, toks = y_own.shape
    parts = 2
    step = (rows.stop - rows.start) // parts
    first = out is None

    def body(own_ref, far_ref, factor_ref, *refs):
        out_hbm, *more, out_ref, sems = refs if first else refs[1:]
        if first:
            inv = lax.rsqrt((split_squares(factor_ref)[1] + split_squares(far_ref)[1]) / features + EPS)
            more[0][...] = inv
        else:
            inv = factor_ref[...]
        copies = []
        for k in range(parts):
            here = slice(k * step, (k + 1) * step)
            there = slice(rows.start + here.start, rows.start + here.stop)
            out_ref[here] = ((own_ref[there] + far_ref[here].astype(F32)) * inv).astype(BF16)
            copies.append(pltpu.make_async_copy(out_ref.at[here], out_hbm.at[there], sems.at[k]))
            copies[-1].start()
        for copy in copies:
            copy.wait()

    vm, where = pl.BlockSpec(memory_space=pltpu.VMEM), pl.BlockSpec(memory_space=pl.ANY)
    result = jax.ShapeDtypeStruct((size, toks), BF16)
    return pl.pallas_call(
        body,
        in_specs=[vm] * 3 + ([] if first else [where]),
        out_specs=[where, vm] if first else where,
        out_shape=[result, jax.ShapeDtypeStruct((1, toks), F32)] if first else result,
        scratch_shapes=[pltpu.VMEM((rows.stop - rows.start, toks), BF16), pltpu.SemaphoreType.DMA((parts,))],
        input_output_aliases={} if first else {3: 0},
        compiler_params=pltpu.CompilerParams(vmem_limit_bytes=VMEM),
        cost_estimate=CHEAP,
    )(y_own, *inputs, *(() if first else (out,)))


def on_device(
    n_seq, n_tp, head_input, gate_input, write_vecs, read_vecs, step_raw, segment_ids,
    decay_log, step_bias, skip_gain, norm_gain, out_weight,
):
    heads = decay_log.shape[0]
    toks, feats = head_input.shape
    width = feats // heads
    def swap(a, bit):
        return lax.ppermute(a, "seq", [(i, i ^ bit) for i in range(n_seq)])

    def across(a, bit):
        return lax.ppermute(a, "tp", [(i, i ^ bit) for i in range(n_tp)])

    other_one, stash = prepare(
        heads, width, step_raw, segment_ids.reshape(1, toks), decay_log.reshape(1, heads),
        step_bias.reshape(1, heads), head_input, write_vecs,
    )
    mate_one = swap(other_one, 1)
    other_two, keep_one, keep_two = more_states(width, stash, head_input, write_vecs)
    mate_two = swap(other_two, 1)
    *setup, seg = local_setup(
        heads, width, read_vecs, write_vecs, stash, skip_gain.reshape(1, heads), other_two
    )

    def local(which, tiles, after):
        return local_part(which, tiles, heads, width, head_input, gate_input, write_vecs, setup, after)

    tiles = feats // 2 // LANES
    edge = EARLY_LANES // LANES
    early = pair_step(keep_one, mate_one, seg)
    keep_a = local(0, range(0, tiles - edge), early[0])
    late = pair_step(keep_two, mate_two, keep_a[0])
    keep_b = local(0, range(tiles - edge, tiles), late[0])
    sent, totals, rows, firsts = zip(early, late)
    entries = [()] * 2
    bit, before = 2, keep_b[0]
    while 2 * bit < n_seq:
        more = 4 * bit < n_seq
        got = [swap(piece, bit) for piece in sent]
        early = level_step(bit, more, got[0], totals[0], rows[0], *entries[0], after=before)
        if bit == 2:
            other_a = local(1, range(0, edge), early[0])
        late = level_step(bit, more, got[1], totals[1], rows[1], *entries[1], after=other_a[0] if bit == 2 else early[0])
        sent, entries, rows, *totals = zip(early, late)
        totals, entries = totals[0] if more else (), [(entry,) for entry in entries]
        bit, before = bit * 2, None
    other_b = local(1, range(edge, tiles), sent[1])
    half_w = feats // 2
    quarter = out_weight.shape[1] // 4
    one, two = slice(0, EARLY_LANES), slice(EARLY_LANES, half_w)
    top, rest, every = slice(0, EARLY_ROWS), slice(EARLY_ROWS, quarter), slice(0, quarter)
    send_one, keep_one, prev = entry_step(
        bit, True, swap(sent[0], bit), *entries[0], rows[0], firsts[0], other_b[0]
    )
    other_one = swap(send_one, 1)
    send_two, keep_two = entry_step(bit, False, swap(sent[1], bit), *entries[1], rows[1], firsts[1], send_one)
    other_two = swap(send_two, 1)
    gain = norm_gain.reshape(1, feats)
    shared = (prev, read_vecs, seg)
    whole_half = slice(0, half_w)
    g_keep, squares, partial = gated_sums(
        0, whole_half, *shared, (keep_a[0], keep_b[0]), (keep_a[1], keep_b[1]), (keep_one, keep_two), gain, out_weight
    )
    g_one, squares, partial = gated_sums(
        1, one, *shared, other_a[:1], other_a[1:], (other_one,), gain, out_weight, partial, squares
    )
    g_two, near_top = gated_last(two, top, *shared, *other_b, other_two, gain, out_weight, partial, squares)
    got_top = across(near_top, 1)
    groups, gs = ((0, whole_half), (1, one), (1, two)), (g_keep, g_one, g_two)
    near_rest, far_top, far_rest = project_next(groups, gs, top, rest, partial, out_weight, near_top)
    got_rest = across(near_rest, 1)
    to_far_top = add_first(far_top, near_top, got_top)
    got_far_top = across(to_far_top, 2)
    to_far_rest = add_second(far_rest, got_rest, to_far_top)
    got_far_rest = across(to_far_rest, 2)
    y_near = project_whole(2, groups, gs, out_weight, NEAR_PIECES, after=to_far_rest)
    got_own = tuple(across(piece, 1) for piece in y_near)
    (y_own,) = project_whole(3, groups, gs, out_weight, 1, got_own)
    out, inv = finish(top, y_own, (got_far_top, to_far_top), features=feats * n_tp)
    return finish(rest, y_own, (got_far_rest, inv), out)


def solution(mesh):
    in_specs = (
        P("seq", "tp"),
        P("seq", "tp"),
        P("seq", None),
        P("seq", None),
        P("tp", "seq"),
        P("seq"),
        P("tp"),
        P("tp"),
        P("tp"),
        P("tp"),
        P("tp", None),
    )
    out_specs = P("tp", "seq")
    return jax.shard_map(
        functools.partial(on_device, mesh.shape["seq"], mesh.shape["tp"]),
        mesh=mesh, in_specs=in_specs, out_specs=out_specs, check_vma=False,
    )
```

```python
import functools

import jax
import jax.numpy as jnp
from jax import lax
from jax.experimental import pallas as pl
from jax.experimental.pallas import tpu as pltpu
from jax.sharding import PartitionSpec as P

GROUP = 256
LANES = 128
EPS = 1e-05
LOG2E = 1.4426950408889634
SEG_LANE = 24
EXTRA = 8
EARLY_ROWS = 384
NEAR_PIECES = 4
EARLY_LANES = 384
VMEM = 16 * 1024 * 1024
VMEM_ALL = 56 * 1024 * 1024
CHEAP = pl.CostEstimate(flops=1000, bytes_accessed=1000, transcendentals=0)
LONG = pl.CostEstimate(flops=4_000_000_000, bytes_accessed=1000, transcendentals=0)
F32 = jnp.float32
BF16 = jnp.bfloat16


def dot(a, b, dims=((1,), (0,))):
    return lax.dot_general(a, b, (dims, ((), ())), preferred_element_type=F32)


def lane_iota(rows):
    return lax.broadcasted_iota(jnp.int32, (rows, LANES), 1)


def spread(cols, first, width):
    rows = cols.shape[0]
    per = LANES // width
    lane = lane_iota(rows)
    out = jnp.broadcast_to(cols[:, first : first + 1], (rows, LANES))
    for k in range(1, per):
        nxt = jnp.broadcast_to(cols[:, first + k : first + k + 1], (rows, LANES))
        out = jnp.where(lane < k * width, out, nxt)
    return out


def position():
    place, rank = lax.axis_index("seq"), lax.axis_index("tp")
    odd = place & 1
    far = rank ^ 2
    return odd, 1 - odd, far ^ 1, far, rank ^ 1, rank, place


def call(body, args, out_shape, scratch=(), after=None, cost=CHEAP):
    vm = pl.BlockSpec(memory_space=pltpu.VMEM)
    specs = [vm] * len(args)
    operands = list(args)
    kernel = body
    if after is not None:
        specs.append(pl.BlockSpec(memory_space=pl.ANY))
        operands.append(after)
        at = len(operands) - 1

        def kernel(*refs):
            body(*refs[:at], *refs[at + 1 :])

    return pl.pallas_call(
        kernel,
        in_specs=specs,
        out_specs=jax.tree.map(lambda _: vm, out_shape),
        out_shape=out_shape,
        scratch_shapes=list(scratch),
        compiler_params=pltpu.CompilerParams(vmem_limit_bytes=VMEM),
        cost_estimate=cost,
    )(*operands)


def shaped(*shapes):
    return [jax.ShapeDtypeStruct(shape, dtype) for shape, dtype in shapes]


def pack(out_ref, total):
    state, through, last = total
    high = through.astype(BF16).astype(F32)
    row = lax.broadcasted_iota(jnp.int32, (EXTRA, state.shape[1]), 0)
    rows = jnp.where(row == 0, high, jnp.where(row == 1, through - high, last))
    out_ref[...] = jnp.concatenate([state, rows], axis=0).astype(BF16)


def unpack(ref):
    size = ref.shape[0] - EXTRA
    whole = ref[...].astype(F32)
    return whole[0:size], whole[size : size + 1] + whole[size + 1 : size + 2], whole[size + 2 : size + 3]


def merged(swapped, one, two):
    later = jnp.where(swapped, one[1], two[1])
    link = later * (one[2] == two[2]).astype(F32)
    state = jnp.where(swapped, 1.0, link) * one[0] + jnp.where(swapped, link, 1.0) * two[0]
    return state, one[1] * two[1], jnp.where(swapped, one[2], two[2])


def stash_rows():
    return slice(0, 32), slice(32, 64), slice(64, 96), slice(96, 104)


def put_rows(rows_ref, rows):
    lanes = rows_ref.shape[1]
    for at, row in enumerate(rows):
        rows_ref[at : at + 1] = jnp.broadcast_to(row, (1, lanes))


def some_state(half, half_w, lanes, width, vecs, tails_ref, through_row, last, x_ref, first_lane, out_ref):
    state = vecs.shape[0]
    per = LANES // width
    half_h = half_w // width
    skipped = lanes.start // width
    lane = lane_iota(state)
    mine = jnp.where(half == 1, pltpu.roll(through_row, LANES - half_h, 1), through_row)
    own, through = [], []
    for i in range((lanes.stop - lanes.start) // LANES):
        written = []
        for k in range(per):
            row = tails_ref[pl.ds(half * half_h + skipped + i * per + k, 1), :]
            written.append((vecs * row).astype(BF16))
        here = pl.ds(pl.multiple_of(first_lane + i * LANES, LANES), LANES)
        both = dot(jnp.concatenate(written, axis=0), x_ref[:, here])
        tile = both[0:state]
        for k in range(1, per):
            tile = jnp.where(lane < k * width, tile, both[k * state : (k + 1) * state])
        own.append(tile)
        through.append(spread(mine[0:1], skipped + i * per, width))
    ids = jnp.broadcast_to(last, (1, lanes.stop - lanes.start))
    group = (jnp.concatenate(own, axis=1), jnp.concatenate(through, axis=1), ids)
    pack(out_ref, group)


def prepare(heads, width, raw, seg, decay_log, bias, x, write):
    toks, state = write.shape
    half_w = x.shape[1] // 2
    blocks = toks // GROUP
    arrays = (raw, seg, decay_log, bias, write, x)

    def body(*refs):
        hbm, (other_ref, stash_ref) = refs[: len(arrays)], refs[len(arrays) : -8]
        raw_ref, seg_ref, dl_ref, sb_ref, wr_ref, x_ref, rows, sems = refs[-8:]
        half = position()[1]
        lanes = pl.ds(pl.multiple_of(half * half_w, LANES), EARLY_LANES)
        sources = (*hbm[:5], hbm[5].at[:, lanes])
        copies = [
            pltpu.make_async_copy(src, dst, sems.at[k])
            for k, (src, dst) in enumerate(zip(sources, (raw_ref, seg_ref, dl_ref, sb_ref, wr_ref, x_ref)))
        ]
        for copy in copies:
            copy.start()
        rows[...] = jnp.zeros_like(rows)
        tri = (
            lax.broadcasted_iota(jnp.int32, (GROUP, GROUP), 0)
            <= lax.broadcasted_iota(jnp.int32, (GROUP, GROUP), 1)
        ).astype(BF16)
        stash_ref[...] = jnp.zeros_like(stash_ref)
        cum_rows, step_rows, tail_rows, sum_rows = stash_rows()
        for copy in copies[:5]:
            copy.wait()
        vecs = jnp.transpose(wr_ref[...].astype(F32))
        rows[0:1, 0:heads] = dl_ref[...]
        rows[1:2, 0:heads] = sb_ref[...]
        stash_ref[0:heads] = raw_ref[...].astype(F32)
        params = jnp.transpose(rows[...])[0:32]
        z = stash_ref[cum_rows] + params[:, 1:2]
        step = jnp.maximum(z, 0.0) + jnp.log1p(jnp.exp(-jnp.abs(z)))
        rate = -jnp.exp(params[:, 0:1]) * step
        cum, full = [], []
        base = jnp.zeros((32, 1), F32)
        for b in range(blocks):
            r = rate[:, b * GROUP : (b + 1) * GROUP]
            r1 = r.astype(BF16)
            d1 = r - r1.astype(F32)
            r2 = d1.astype(BF16)
            r3 = (d1 - r2.astype(F32)).astype(BF16)
            c = dot(r1, tri) + (dot(r2, tri) + dot(r3, tri))
            cum.append(c)
            full.append(c + base)
            base = base + c[:, GROUP - 1 : GROUP]
        seg_row = seg_ref[...].astype(F32)
        last = seg_row[:, toks - 1 : toks]
        tail = jnp.exp(base - jnp.concatenate(full, axis=1)) * step
        stash_ref[cum_rows] = jnp.concatenate(cum, axis=1)
        stash_ref[SEG_LANE : SEG_LANE + 1] = seg_row
        stash_ref[step_rows] = step
        stash_ref[tail_rows] = jnp.where(seg_row == last, tail, 0.0)
        rows[...] = jnp.zeros_like(rows)
        rows[0:32] = jnp.broadcast_to(jnp.exp(base), (32, LANES))
        sums = jnp.transpose(rows[...])[0:8]
        stash_ref[sum_rows, 0:LANES] = sums
        copies[5].wait()
        piece = slice(0, EARLY_LANES)
        some_state(half, half_w, piece, width, vecs, stash_ref.at[tail_rows], sums, last, x_ref, 0, other_ref)

    vm = pl.BlockSpec(memory_space=pltpu.VMEM)
    out_shape = shaped(((state + EXTRA, EARLY_LANES), BF16), ((stash_rows()[-1].stop, toks), F32))
    return pl.pallas_call(
        body,
        in_specs=[pl.BlockSpec(memory_space=pltpu.HBM)] * len(arrays),
        out_specs=[vm] * len(out_shape),
        out_shape=out_shape,
        scratch_shapes=[
            *[pltpu.VMEM(a.shape, a.dtype) for a in arrays[:5]], pltpu.VMEM((toks, EARLY_LANES), BF16),
            pltpu.VMEM((LANES, LANES), F32), pltpu.SemaphoreType.DMA((len(arrays),)),
        ],
        compiler_params=pltpu.CompilerParams(vmem_limit_bytes=VMEM_ALL),
        cost_estimate=LONG,
    )(*arrays)


def more_states(width, stash, x, write):
    toks, state = write.shape
    half_w = x.shape[1] // 2
    one, two = slice(0, EARLY_LANES), slice(EARLY_LANES, half_w)
    pieces = ((1, two), (0, one), (0, two))

    def body(stash_ref, x_ref, wr_ref, *outs):
        _, _, tail_rows, sum_rows = stash_rows()
        vecs = jnp.transpose(wr_ref[...].astype(F32))
        last = stash_ref[SEG_LANE : SEG_LANE + 1, toks - 1 : toks]
        sums = stash_ref[sum_rows, 0:LANES]
        tails_ref = stash_ref.at[tail_rows]
        for (which, lanes), out_ref in zip(pieces, outs):
            half = position()[which]
            first = half * half_w + lanes.start
            some_state(half, half_w, lanes, width, vecs, tails_ref, sums, last, x_ref, first, out_ref)

    out = shaped(*[((state + EXTRA, lanes.stop - lanes.start), BF16) for _, lanes in pieces])
    return call(body, (stash, x, write), out)


def gather_level(upper, entry, other):
    state, through, last_id = entry
    link = through * ((last_id < 0) | (other[2] == last_id)).astype(F32)
    state = state + jnp.where(upper, link, 0.0) * other[0]
    last_id = jnp.where(upper & (last_id < 0), other[2], last_id)
    return state, through * jnp.where(upper, other[1], 1.0), last_id


def pair_step(keep, mate, after=None):
    size, lanes = mate.shape[0] - EXTRA, mate.shape[1]

    def body(keep_ref, mate_ref, send_ref, total_ref, rows_ref, first_ref):
        odd = position()[0] == 1
        mine, mate = unpack(keep_ref), unpack(mate_ref)
        total = merged(odd, mine, mate)
        first = tuple(jnp.where(odd, m, o) for o, m in zip(mine, mate))
        pack(send_ref, total)
        total_ref[...], first_ref[...] = total[0], first[0]
        put_rows(rows_ref, (jnp.ones_like(total[1]), jnp.full_like(total[2], -1.0)) + first[1:] + total[1:])

    state = ((size, lanes), F32)
    return call(
        body, (keep, mate), shaped((mate.shape, BF16), state, ((8, lanes), F32), state), after=after, cost=LONG
    )


def level_step(bit, more, got, total, rows, entry=None, after=None):
    size, lanes = total.shape
    entries = () if entry is None else (entry,)

    def body(got_ref, total_ref, rows_ref, *refs):
        send_ref, entry_out, rows_out, *totals = refs[len(entries) :]
        upper = (position()[6] & bit) != 0
        other = unpack(got_ref)
        old = refs[0][...] if entries else jnp.zeros_like(total_ref)
        new = gather_level(upper, (old, rows_ref[0:1], rows_ref[1:2]), other)
        held = merged(upper, (total_ref[...], rows_ref[4:5], rows_ref[5:6]), other)
        pack(send_ref, held)
        entry_out[...] = new[0]
        put_rows(rows_out, new[1:] + (rows_ref[2:3], rows_ref[3:4]) + held[1:])
        if more:
            totals[0][...] = held[0]

    state = ((size, lanes), F32)
    return call(
        body, (got, total, rows, *entries),
        shaped((got.shape, BF16), state, ((8, lanes), F32), *((state,) if more else ())), after=after, cost=LONG,
    )


def entry_step(bit, with_id, got, entry, rows, first, after):
    def body(got_ref, entry_ref, rows_ref, first_ref, other_ref, keep_ref, *prev_ref):
        upper = (position()[6] & bit) != 0
        even = position()[0] == 0
        new = gather_level(upper, (entry_ref[...], rows_ref[0:1], rows_ref[1:2]), unpack(got_ref))
        last_first = rows_ref[3:4]
        link = rows_ref[2:3] * (last_first == new[2]).astype(F32)
        reached = first_ref[...] + link * new[0]
        other_ref[...] = jnp.where(even, reached, new[0]).astype(BF16)
        keep_ref[...] = jnp.where(even, new[0], reached).astype(BF16)
        if with_id:
            prev = jnp.where(even, new[2], last_first)
            prev_ref[0][...] = jnp.broadcast_to(prev[:, 0:LANES], (8, LANES))

    block = (entry.shape, BF16)
    prev = (((8, LANES), F32),) if with_id else ()
    return call(body, (got, entry, rows, first), shaped(block, block, *prev), after=after)


def local_setup(heads, width, read, write, stash, skip, after):
    toks = write.shape[0]
    half_h = heads // 2
    blocks = toks // GROUP

    def body(
        rd_ref, wr_ref, stash_ref, skip_ref,
        scores, linked_ref, log_cum, log_row, tails, skips, seg_out, pad, rows_ref,
    ):
        cum_ref, step_ref = (stash_ref.at[rows] for rows in stash_rows()[:2])
        second = [position()[which] == 1 for which in range(2)]
        pad[...] = jnp.zeros_like(pad)
        rows_ref[...] = jnp.zeros_like(rows_ref)
        rows_ref[0:1, 0:heads] = skip_ref[...]
        turned = pltpu.roll(rows_ref[...], LANES - half_h, 1)
        for which in range(2):
            skips[which] = jnp.where(second[which], turned, rows_ref[...])
        seg_row = cum_ref[SEG_LANE : SEG_LANE + 1]
        log_row[...] = cum_ref[...] * LOG2E - jnp.log(step_ref[...]) * LOG2E
        pad[0:32] = cum_ref[...] * LOG2E
        pad[SEG_LANE : SEG_LANE + 1] = seg_row
        columns = jnp.transpose(pad[...])
        seg_col = columns[:, SEG_LANE : SEG_LANE + 1]
        turned = pltpu.roll(columns, LANES - half_h, 1)
        for which in range(2):
            log_cum[which] = jnp.where(second[which], turned, columns)
        seg_out[...] = columns
        tail0 = jnp.exp(cum_ref[:, GROUP - 1 : GROUP] - cum_ref[:, 0:GROUP]) * step_ref[:, 0:GROUP]
        same = seg_row[:, 0:GROUP] == seg_row[:, GROUP - 1 : GROUP]
        pad[0:32, 0:GROUP] = jnp.where(same, tail0, 0.0)
        columns = jnp.transpose(pad[:, 0:GROUP])
        turned = pltpu.roll(columns, LANES - half_h, 1)
        for which in range(2):
            tails[which] = jnp.where(second[which], turned, columns)
        causal = lax.broadcasted_iota(jnp.int32, (GROUP, GROUP), 0) >= lax.broadcasted_iota(
            jnp.int32, (GROUP, GROUP), 1
        )
        for b in range(blocks):
            rows = slice(b * GROUP, (b + 1) * GROUP)
            s = dot(rd_ref[rows], wr_ref[rows], ((1,), (1,)))
            scores[b] = jnp.where(causal & (seg_col[rows] == seg_row[:, rows]), s, 0.0)
        linked = seg_col[GROUP:] == seg_col[GROUP - 1 : GROUP]
        linked_ref[...] = jnp.where(linked, rd_ref[GROUP:].astype(F32), 0.0).astype(BF16)

    return call(
        body, (read, write, stash, skip),
        shaped(
            ((blocks, GROUP, GROUP), F32), ((toks - GROUP, read.shape[1]), BF16), ((2, toks, LANES), F32),
            ((32, toks), F32), ((2, GROUP, LANES), F32), ((2, 8, LANES), F32), ((toks, LANES), F32),
        ),
        [pltpu.VMEM((LANES, toks), F32), pltpu.VMEM((8, LANES), F32)],
        cost=LONG, after=after,
    )


def local_part(which, tiles, heads, width, x, gate, write, setup, after):
    toks = write.shape[0]
    half_w = x.shape[1] // 2
    half_h = heads // 2
    per = LANES // width
    blocks = toks // GROUP
    strip = 64

    def body(
        x_ref, gate_ref, wr_ref, scores, linked_ref, log_cum, log_row, tails, skips, a_ref, b_ref, mix
    ):
        half = position()[which]
        lane = lane_iota(GROUP)
        for slot in range(mix.shape[0]):
            for k in range(per):
                mix[slot, k * GROUP : k * GROUP + LANES, LANES:] = jnp.zeros((LANES, GROUP - LANES), BF16)
        for n, i in enumerate(tiles):
            there = pl.ds(pl.multiple_of(half * half_w + i * LANES, LANES), LANES)
            tile = slice(n * LANES, (n + 1) * LANES)
            gains = spread(skips[which, 0:1], i * per, width)
            carry = None
            start = jnp.ones((1, LANES), F32)
            for b in range(blocks):
                rows = slice(b * GROUP, (b + 1) * GROUP)
                slot = (n * blocks + b) % mix.shape[0]
                xb = x_ref[rows, there]
                logs = []
                for k in range(per):
                    head = i * per + k
                    cb = jnp.broadcast_to(log_cum[which, rows, head : head + 1], (GROUP, LANES))
                    logs.append(cb)
                    ar = log_row[pl.ds(half * half_h + head, 1), rows]
                    for low in range(0, GROUP, strip):
                        for left in range(0, min(low + strip, GROUP), LANES):
                            gap = cb[low : low + strip] - ar[:, left : left + LANES]
                            part = jnp.exp2(jnp.minimum(gap, 60.0))
                            part = part * scores[b, low : low + strip, left : left + LANES]
                            at = k * GROUP + low
                            mix[slot, at : at + strip, left : left + LANES] = part.astype(BF16)
                both = dot(mix[slot], xb)
                inner, dec_log = both[0:GROUP], logs[0]
                for k in range(1, per):
                    inner = jnp.where(lane < k * width, inner, both[k * GROUP : (k + 1) * GROUP])
                    dec_log = jnp.where(lane < k * width, dec_log, logs[k])
                dec = jnp.exp2(dec_log)
                xf = xb.astype(F32)
                y = inner + gains * xf
                if b == 1:
                    y = y + (dot(linked_ref[...], carry[0]) + dot(linked_ref[...], carry[1])) * dec
                else:
                    xs = (xf * spread(tails[which], i * per, width)).astype(BF16)
                    s0 = dot(wr_ref[rows], xs, ((0,), (0,)))
                    s0h = s0.astype(BF16)
                    carry = (s0h, (s0 - s0h.astype(F32)).astype(BF16))
                v = gate_ref[rows, there].astype(F32)
                sg = v / (1.0 + jnp.exp(-v))
                a_ref[rows, tile] = sg * y
                b_ref[rows, tile] = sg * (dec * start)
                start = start * dec[GROUP - 1 : GROUP]

    out = ((toks, len(tiles) * LANES), F32)
    return call(
        body, (x, gate, write, *setup), shaped(out, out), [pltpu.VMEM((4, per * GROUP, GROUP), BF16)],
        cost=LONG, after=after,
    )


def side_by_side(refs):
    values = [ref[...] for ref in refs]
    return values[0] if len(values) == 1 else jnp.concatenate(values, axis=1)


def gated_part(which, lanes, prev_ref, rd_ref, cum_ref, a_refs, b_refs, states, gain_ref):
    half_w = gain_ref.shape[1] // 2
    first = pl.multiple_of(position()[which] * half_w + lanes.start, LANES)
    here = pl.ds(first, lanes.stop - lanes.start)
    linked = cum_ref[:, SEG_LANE : SEG_LANE + 1] == prev_ref[0:1, 0:1]
    rm = jnp.where(linked, rd_ref[...].astype(F32), 0.0).astype(BF16)
    carried = [dot(rm, state[...]) for state in states]
    carried = carried[0] if len(carried) == 1 else jnp.concatenate(carried, axis=1)
    gated = side_by_side(a_refs) + side_by_side(b_refs) * carried
    sq = gated * gated
    part = sq[:, 0:LANES]
    for i in range(1, sq.shape[1] // LANES):
        part = part + sq[:, i * LANES : (i + 1) * LANES]
    squares = jnp.sum(jnp.transpose(part), axis=0, keepdims=True)
    return (gated * gain_ref[:, here]).astype(BF16), squares


def projected(which, lanes, quarter, rows, w_ref, g):
    half_w, cols = w_ref.shape[0] // 2, w_ref.shape[1] // 4
    here = pl.multiple_of(position()[which] * half_w + lanes.start, LANES)
    first = pl.multiple_of(position()[2 + quarter] * cols + rows.start, LANES)
    block = w_ref[pl.ds(here, lanes.stop - lanes.start), pl.ds(first, rows.stop - rows.start)]
    return dot(block, g, ((0,), (1,)))


def with_squares(y, squares):
    high = squares.astype(BF16).astype(F32)
    middle = (squares - high).astype(BF16).astype(F32)
    row = lax.broadcasted_iota(jnp.int32, (EXTRA, squares.shape[1]), 0)
    rows = jnp.where(row == 0, high, jnp.where(row == 1, middle, squares - high - middle))
    return jnp.concatenate([y, rows], axis=0).astype(BF16)


def split_squares(ref):
    size = ref.shape[0] - EXTRA
    whole = ref[...].astype(F32)
    return whole[0:size], whole[size : size + 1] + (whole[size + 1 : size + 2] + whole[size + 2 : size + 3])


def gated_sums(which, lanes, prev, read, seg, a, b, states, gain, weight, partial=None, squares=None):
    toks = read.shape[0]
    cols = weight.shape[1] // 4
    earlier = () if partial is None else (partial, squares)
    ends = [0, len(a), len(a) + len(b), len(a) + len(b) + len(states)]

    def body(prev_ref, rd_ref, seg_ref, gain_ref, w_ref, *refs):
        a_refs, b_refs, s_refs = (refs[low:high] for low, high in zip(ends, ends[1:]))
        old, (g_ref, s_ref, y_ref) = refs[ends[-1] : -3], refs[-3:]
        g, s = gated_part(which, lanes, prev_ref, rd_ref, seg_ref, a_refs, b_refs, s_refs, gain_ref)
        g_ref[...] = g
        s_ref[...] = s + old[1][...] if old else s
        y = projected(which, lanes, 0, slice(0, cols), w_ref, g)
        y_ref[...] = y + old[0][...] if old else y

    return call(
        body, (prev, read, seg, gain, weight, *a, *b, *states, *earlier),
        shaped(((toks, lanes.stop - lanes.start), BF16), ((1, toks), F32), ((cols, toks), F32)),
    )


def gated_last(lanes, rows, prev, read, seg, a, b, state, gain, weight, partial, squares):
    toks = read.shape[0]

    def body(prev_ref, rd_ref, seg_ref, a_ref, b_ref, e_ref, gain_ref, w_ref, p_ref, s_ref, g_ref, y_ref):
        g, s = gated_part(1, lanes, prev_ref, rd_ref, seg_ref, (a_ref,), (b_ref,), (e_ref,), gain_ref)
        g_ref[...] = g
        y = p_ref[rows] + projected(1, lanes, 0, rows, w_ref, g)
        y_ref[...] = with_squares(y, s_ref[...] + s)

    return call(
        body, (prev, read, seg, a, b, state, gain, weight, partial, squares),
        shaped(((toks, lanes.stop - lanes.start), BF16), ((rows.stop - rows.start + EXTRA, toks), BF16)),
    )


def project_next(groups, gs, top, rest, partial, weight, after):
    toks = gs[0].shape[0]

    def body(p_ref, w_ref, *refs):
        g_refs, (near_ref, top_ref, rest_ref) = refs[: len(gs)], refs[len(gs) :]
        which, lanes = groups[-1]
        near = p_ref[rest] + projected(which, lanes, 0, rest, w_ref, g_refs[-1][...])
        near_ref[...] = near.astype(BF16)
        for rows, y_ref in ((top, top_ref), (rest, rest_ref)):
            y_ref[...] = sum(
                projected(which, lanes, 1, rows, w_ref, g_ref[...])
                for (which, lanes), g_ref in zip(groups, g_refs)
            )

    size = rest.stop - rest.start
    out = shaped(((size, toks), BF16), ((top.stop, toks), F32), ((size, toks), F32))
    return call(body, (partial, weight, *gs), out, after=after)


def project_whole(quarter, groups, gs, weight, pieces, adds=(), after=None):
    cols = weight.shape[1] // 4
    toks = gs[0].shape[0]
    step = cols // pieces

    def body(w_ref, *refs):
        g_refs, add_refs, outs = refs[: len(gs)], refs[len(gs) : len(gs) + len(adds)], refs[len(gs) + len(adds) :]
        y = sum(
            projected(which, lanes, quarter, slice(0, cols), w_ref, g_ref[...])
            for (which, lanes), g_ref in zip(groups, g_refs)
        )
        if add_refs:
            outs[0][...] = y + jnp.concatenate([r[...].astype(F32) for r in add_refs], axis=0)
        else:
            for k, y_ref in enumerate(outs):
                y_ref[...] = y[k * step : (k + 1) * step].astype(BF16)

    out = shaped(((cols, toks), F32)) if adds else shaped(*[((step, toks), BF16)] * pieces)
    return call(body, (weight, *gs, *adds), out, after=after)


def add_first(y_far, to_near, got_near):
    def body(y_ref, mine_ref, got_ref, out_ref):
        got, squares = split_squares(got_ref)
        out_ref[...] = with_squares(y_ref[...] + got, split_squares(mine_ref)[1] + squares)

    return call(body, (y_far, to_near, got_near), jax.ShapeDtypeStruct(got_near.shape, BF16))


def add_second(y_far, got_near, after):
    def body(y_ref, got_ref, out_ref):
        out_ref[...] = (y_ref[...] + got_ref[...].astype(F32)).astype(BF16)

    return call(body, (y_far, got_near), jax.ShapeDtypeStruct(got_near.shape, BF16), after=after)


def finish(rows, y_own, inputs, out=None, features=None):
    size, toks = y_own.shape
    parts = 2
    step = (rows.stop - rows.start) // parts
    first = out is None

    def body(own_ref, far_ref, factor_ref, *refs):
        out_hbm, *more, out_ref, sems = refs if first else refs[1:]
        if first:
            inv = lax.rsqrt((split_squares(factor_ref)[1] + split_squares(far_ref)[1]) / features + EPS)
            more[0][...] = inv
        else:
            inv = factor_ref[...]
        copies = []
        for k in range(parts):
            here = slice(k * step, (k + 1) * step)
            there = slice(rows.start + here.start, rows.start + here.stop)
            out_ref[here] = ((own_ref[there] + far_ref[here].astype(F32)) * inv).astype(BF16)
            copies.append(pltpu.make_async_copy(out_ref.at[here], out_hbm.at[there], sems.at[k]))
            copies[-1].start()
        for copy in copies:
            copy.wait()

    vm, where = pl.BlockSpec(memory_space=pltpu.VMEM), pl.BlockSpec(memory_space=pl.ANY)
    result = jax.ShapeDtypeStruct((size, toks), BF16)
    return pl.pallas_call(
        body,
        in_specs=[vm] * 3 + ([] if first else [where]),
        out_specs=[where, vm] if first else where,
        out_shape=[result, jax.ShapeDtypeStruct((1, toks), F32)] if first else result,
        scratch_shapes=[pltpu.VMEM((rows.stop - rows.start, toks), BF16), pltpu.SemaphoreType.DMA((parts,))],
        input_output_aliases={} if first else {3: 0},
        compiler_params=pltpu.CompilerParams(vmem_limit_bytes=VMEM),
        cost_estimate=CHEAP,
    )(y_own, *inputs, *(() if first else (out,)))


def on_device(
    n_seq, n_tp, head_input, gate_input, write_vecs, read_vecs, step_raw, segment_ids,
    decay_log, step_bias, skip_gain, norm_gain, out_weight,
):
    heads = decay_log.shape[0]
    toks, feats = head_input.shape
    width = feats // heads
    def swap(a, bit):
        return lax.ppermute(a, "seq", [(i, i ^ bit) for i in range(n_seq)])

    def across(a, bit):
        return lax.ppermute(a, "tp", [(i, i ^ bit) for i in range(n_tp)])

    other_one, stash = prepare(
        heads, width, step_raw, segment_ids.reshape(1, toks), decay_log.reshape(1, heads),
        step_bias.reshape(1, heads), head_input, write_vecs,
    )
    mate_one = swap(other_one, 1)
    other_two, keep_one, keep_two = more_states(width, stash, head_input, write_vecs)
    mate_two = swap(other_two, 1)
    *setup, seg = local_setup(
        heads, width, read_vecs, write_vecs, stash, skip_gain.reshape(1, heads), other_two
    )

    def local(which, tiles, after):
        return local_part(which, tiles, heads, width, head_input, gate_input, write_vecs, setup, after)

    tiles = feats // 2 // LANES
    edge = EARLY_LANES // LANES
    early = pair_step(keep_one, mate_one, seg)
    keep_a = local(0, range(0, tiles - edge), early[0])
    late = pair_step(keep_two, mate_two, keep_a[0])
    keep_b = local(0, range(tiles - edge, tiles), late[0])
    sent, totals, rows, firsts = zip(early, late)
    entries = [()] * 2
    bit, before = 2, keep_b[0]
    while 2 * bit < n_seq:
        more = 4 * bit < n_seq
        got = [swap(piece, bit) for piece in sent]
        early = level_step(bit, more, got[0], totals[0], rows[0], *entries[0], after=before)
        if bit == 2:
            other_a = local(1, range(0, edge), early[0])
        late = level_step(bit, more, got[1], totals[1], rows[1], *entries[1], after=other_a[0] if bit == 2 else early[0])
        sent, entries, rows, *totals = zip(early, late)
        totals, entries = totals[0] if more else (), [(entry,) for entry in entries]
        bit, before = bit * 2, None
    other_b = local(1, range(edge, tiles), sent[1])
    half_w = feats // 2
    quarter = out_weight.shape[1] // 4
    one, two = slice(0, EARLY_LANES), slice(EARLY_LANES, half_w)
    top, rest, every = slice(0, EARLY_ROWS), slice(EARLY_ROWS, quarter), slice(0, quarter)
    send_one, keep_one, prev = entry_step(
        bit, True, swap(sent[0], bit), *entries[0], rows[0], firsts[0], other_b[0]
    )
    other_one = swap(send_one, 1)
    send_two, keep_two = entry_step(bit, False, swap(sent[1], bit), *entries[1], rows[1], firsts[1], send_one)
    other_two = swap(send_two, 1)
    gain = norm_gain.reshape(1, feats)
    shared = (prev, read_vecs, seg)
    whole_half = slice(0, half_w)
    g_keep, squares, partial = gated_sums(
        0, whole_half, *shared, (keep_a[0], keep_b[0]), (keep_a[1], keep_b[1]), (keep_one, keep_two), gain, out_weight
    )
    g_one, squares, partial = gated_sums(
        1, one, *shared, other_a[:1], other_a[1:], (other_one,), gain, out_weight, partial, squares
    )
    g_two, near_top = gated_last(two, top, *shared, *other_b, other_two, gain, out_weight, partial, squares)
    got_top = across(near_top, 1)
    groups, gs = ((0, whole_half), (1, one), (1, two)), (g_keep, g_one, g_two)
    near_rest, far_top, far_rest = project_next(groups, gs, top, rest, partial, out_weight, near_top)
    got_rest = across(near_rest, 1)
    to_far_top = add_first(far_top, near_top, got_top)
    got_far_top = across(to_far_top, 2)
    to_far_rest = add_second(far_rest, got_rest, to_far_top)
    got_far_rest = across(to_far_rest, 2)
    y_near = project_whole(2, groups, gs, out_weight, NEAR_PIECES, after=to_far_rest)
    got_own = tuple(across(piece, 1) for piece in y_near)
    (y_own,) = project_whole(3, groups, gs, out_weight, 1, got_own)
    out, inv = finish(top, y_own, (got_far_top, to_far_top), features=feats * n_tp)
    return finish(rest, y_own, (got_far_rest, inv), out)


def solution(mesh):
    in_specs = (
        P("seq", "tp"),
        P("seq", "tp"),
        P("seq", None),
        P("seq", None),
        P("tp", "seq"),
        P("seq"),
        P("tp"),
        P("tp"),
        P("tp"),
        P("tp"),
        P("tp", None),
    )
    out_specs = P("tp", "seq")
    return jax.shard_map(
        functools.partial(on_device, mesh.shape["seq"], mesh.shape["tp"]),
        mesh=mesh, in_specs=in_specs, out_specs=out_specs, check_vma=False,
    )
```

```python
import functools

import jax
import jax.numpy as jnp
from jax import lax
from jax.experimental import pallas as pl
from jax.experimental.pallas import tpu as pltpu
from jax.sharding import PartitionSpec as P

GROUP = 256
LANES = 128
EPS = 1e-05
LOG2E = 1.4426950408889634
SEG_LANE = 24
EXTRA = 8
EARLY_ROWS = 384
NEAR_PIECES = 4
EARLY_LANES = 384
VMEM = 16 * 1024 * 1024
VMEM_ALL = 56 * 1024 * 1024
CHEAP = pl.CostEstimate(flops=1000, bytes_accessed=1000, transcendentals=0)
LONG = pl.CostEstimate(flops=4_000_000_000, bytes_accessed=1000, transcendentals=0)
F32 = jnp.float32
BF16 = jnp.bfloat16


def dot(a, b, dims=((1,), (0,))):
    return lax.dot_general(a, b, (dims, ((), ())), preferred_element_type=F32)


def lane_iota(rows):
    return lax.broadcasted_iota(jnp.int32, (rows, LANES), 1)


def spread(cols, first, width):
    rows = cols.shape[0]
    per = LANES // width
    lane = lane_iota(rows)
    out = jnp.broadcast_to(cols[:, first : first + 1], (rows, LANES))
    for k in range(1, per):
        nxt = jnp.broadcast_to(cols[:, first + k : first + k + 1], (rows, LANES))
        out = jnp.where(lane < k * width, out, nxt)
    return out


def position():
    place, rank = lax.axis_index("seq"), lax.axis_index("tp")
    odd = place & 1
    far = rank ^ 2
    return odd, 1 - odd, far ^ 1, far, rank ^ 1, rank, place


def call(body, args, out_shape, scratch=(), after=None, cost=CHEAP):
    vm = pl.BlockSpec(memory_space=pltpu.VMEM)
    specs = [vm] * len(args)
    operands = list(args)
    kernel = body
    if after is not None:
        specs.append(pl.BlockSpec(memory_space=pl.ANY))
        operands.append(after)
        at = len(operands) - 1

        def kernel(*refs):
            body(*refs[:at], *refs[at + 1 :])

    return pl.pallas_call(
        kernel,
        in_specs=specs,
        out_specs=jax.tree.map(lambda _: vm, out_shape),
        out_shape=out_shape,
        scratch_shapes=list(scratch),
        compiler_params=pltpu.CompilerParams(vmem_limit_bytes=VMEM),
        cost_estimate=cost,
    )(*operands)


def shaped(*shapes):
    return [jax.ShapeDtypeStruct(shape, dtype) for shape, dtype in shapes]


def pack(out_ref, total):
    state, through, last = total
    high = through.astype(BF16).astype(F32)
    row = lax.broadcasted_iota(jnp.int32, (EXTRA, state.shape[1]), 0)
    rows = jnp.where(row == 0, high, jnp.where(row == 1, through - high, last))
    out_ref[...] = jnp.concatenate([state, rows], axis=0).astype(BF16)


def unpack(ref):
    size = ref.shape[0] - EXTRA
    whole = ref[...].astype(F32)
    return whole[0:size], whole[size : size + 1] + whole[size + 1 : size + 2], whole[size + 2 : size + 3]


def merged(swapped, one, two):
    later = jnp.where(swapped, one[1], two[1])
    link = later * (one[2] == two[2]).astype(F32)
    state = jnp.where(swapped, 1.0, link) * one[0] + jnp.where(swapped, link, 1.0) * two[0]
    return state, one[1] * two[1], jnp.where(swapped, one[2], two[2])


def stash_rows():
    return slice(0, 32), slice(32, 64), slice(64, 96), slice(96, 104)


def put_rows(rows_ref, rows):
    lanes = rows_ref.shape[1]
    for at, row in enumerate(rows):
        rows_ref[at : at + 1] = jnp.broadcast_to(row, (1, lanes))


def some_state(half, half_w, lanes, width, vecs, tails_ref, through_row, last, x_ref, first_lane, out_ref):
    state = vecs.shape[0]
    per = LANES // width
    half_h = half_w // width
    skipped = lanes.start // width
    lane = lane_iota(state)
    mine = jnp.where(half == 1, pltpu.roll(through_row, LANES - half_h, 1), through_row)
    own, through = [], []
    for i in range((lanes.stop - lanes.start) // LANES):
        written = []
        for k in range(per):
            row = tails_ref[pl.ds(half * half_h + skipped + i * per + k, 1), :]
            written.append((vecs * row).astype(BF16))
        here = pl.ds(pl.multiple_of(first_lane + i * LANES, LANES), LANES)
        both = dot(jnp.concatenate(written, axis=0), x_ref[:, here])
        tile = both[0:state]
        for k in range(1, per):
            tile = jnp.where(lane < k * width, tile, both[k * state : (k + 1) * state])
        own.append(tile)
        through.append(spread(mine[0:1], skipped + i * per, width))
    ids = jnp.broadcast_to(last, (1, lanes.stop - lanes.start))
    group = (jnp.concatenate(own, axis=1), jnp.concatenate(through, axis=1), ids)
    pack(out_ref, group)


def prepare(heads, width, raw, seg, decay_log, bias, x, write):
    toks, state = write.shape
    half_w = x.shape[1] // 2
    blocks = toks // GROUP
    arrays = (raw, seg, decay_log, bias, write, x)

    def body(*refs):
        hbm, (other_ref, stash_ref) = refs[: len(arrays)], refs[len(arrays) : -8]
        raw_ref, seg_ref, dl_ref, sb_ref, wr_ref, x_ref, rows, sems = refs[-8:]
        half = position()[1]
        lanes = pl.ds(pl.multiple_of(half * half_w, LANES), EARLY_LANES)
        sources = (*hbm[:5], hbm[5].at[:, lanes])
        copies = [
            pltpu.make_async_copy(src, dst, sems.at[k])
            for k, (src, dst) in enumerate(zip(sources, (raw_ref, seg_ref, dl_ref, sb_ref, wr_ref, x_ref)))
        ]
        for copy in copies:
            copy.start()
        rows[...] = jnp.zeros_like(rows)
        tri = (
            lax.broadcasted_iota(jnp.int32, (GROUP, GROUP), 0)
            <= lax.broadcasted_iota(jnp.int32, (GROUP, GROUP), 1)
        ).astype(BF16)
        stash_ref[...] = jnp.zeros_like(stash_ref)
        cum_rows, step_rows, tail_rows, sum_rows = stash_rows()
        for copy in copies[:4]:
            copy.wait()
        rows[0:1, 0:heads] = dl_ref[...]
        rows[1:2, 0:heads] = sb_ref[...]
        stash_ref[0:heads] = raw_ref[...].astype(F32)
        params = jnp.transpose(rows[...])[0:32]
        z = stash_ref[cum_rows] + params[:, 1:2]
        step = jnp.maximum(z, 0.0) + jnp.log1p(jnp.exp(-jnp.abs(z)))
        rate = -jnp.exp(params[:, 0:1]) * step
        cum, full = [], []
        base = jnp.zeros((32, 1), F32)
        for b in range(blocks):
            r = rate[:, b * GROUP : (b + 1) * GROUP]
            r1 = r.astype(BF16)
            d1 = r - r1.astype(F32)
            r2 = d1.astype(BF16)
            r3 = (d1 - r2.astype(F32)).astype(BF16)
            c = dot(r1, tri) + (dot(r2, tri) + dot(r3, tri))
            cum.append(c)
            full.append(c + base)
            base = base + c[:, GROUP - 1 : GROUP]
        seg_row = seg_ref[...].astype(F32)
        last = seg_row[:, toks - 1 : toks]
        tail = jnp.exp(base - jnp.concatenate(full, axis=1)) * step
        stash_ref[cum_rows] = jnp.concatenate(cum, axis=1)
        stash_ref[SEG_LANE : SEG_LANE + 1] = seg_row
        stash_ref[step_rows] = step
        stash_ref[tail_rows] = jnp.where(seg_row == last, tail, 0.0)
        rows[...] = jnp.zeros_like(rows)
        rows[0:32] = jnp.broadcast_to(jnp.exp(base), (32, LANES))
        sums = jnp.transpose(rows[...])[0:8]
        stash_ref[sum_rows, 0:LANES] = sums
        for copy in copies[4:]:
            copy.wait()
        vecs = jnp.transpose(wr_ref[...].astype(F32))
        piece = slice(0, EARLY_LANES)
        some_state(half, half_w, piece, width, vecs, stash_ref.at[tail_rows], sums, last, x_ref, 0, other_ref)

    vm = pl.BlockSpec(memory_space=pltpu.VMEM)
    out_shape = shaped(((state + EXTRA, EARLY_LANES), BF16), ((stash_rows()[-1].stop, toks), F32))
    return pl.pallas_call(
        body,
        in_specs=[pl.BlockSpec(memory_space=pltpu.HBM)] * len(arrays),
        out_specs=[vm] * len(out_shape),
        out_shape=out_shape,
        scratch_shapes=[
            *[pltpu.VMEM(a.shape, a.dtype) for a in arrays[:5]], pltpu.VMEM((toks, EARLY_LANES), BF16),
            pltpu.VMEM((LANES, LANES), F32), pltpu.SemaphoreType.DMA((len(arrays),)),
        ],
        compiler_params=pltpu.CompilerParams(vmem_limit_bytes=VMEM_ALL),
        cost_estimate=LONG,
    )(*arrays)


def more_states(width, stash, x, write):
    toks, state = write.shape
    half_w = x.shape[1] // 2
    one, two = slice(0, EARLY_LANES), slice(EARLY_LANES, half_w)
    pieces = ((1, two), (0, one), (0, two))

    def body(stash_ref, x_ref, wr_ref, *outs):
        _, _, tail_rows, sum_rows = stash_rows()
        vecs = jnp.transpose(wr_ref[...].astype(F32))
        last = stash_ref[SEG_LANE : SEG_LANE + 1, toks - 1 : toks]
        sums = stash_ref[sum_rows, 0:LANES]
        tails_ref = stash_ref.at[tail_rows]
        for (which, lanes), out_ref in zip(pieces, outs):
            half = position()[which]
            first = half * half_w + lanes.start
            some_state(half, half_w, lanes, width, vecs, tails_ref, sums, last, x_ref, first, out_ref)

    out = shaped(*[((state + EXTRA, lanes.stop - lanes.start), BF16) for _, lanes in pieces])
    return call(body, (stash, x, write), out)


def gather_level(upper, entry, other):
    state, through, last_id = entry
    link = through * ((last_id < 0) | (other[2] == last_id)).astype(F32)
    state = state + jnp.where(upper, link, 0.0) * other[0]
    last_id = jnp.where(upper & (last_id < 0), other[2], last_id)
    return state, through * jnp.where(upper, other[1], 1.0), last_id


def pair_step(keep, mate, after=None):
    size, lanes = mate.shape[0] - EXTRA, mate.shape[1]

    def body(keep_ref, mate_ref, send_ref, total_ref, rows_ref, first_ref):
        odd = position()[0] == 1
        mine, mate = unpack(keep_ref), unpack(mate_ref)
        total = merged(odd, mine, mate)
        first = tuple(jnp.where(odd, m, o) for o, m in zip(mine, mate))
        pack(send_ref, total)
        total_ref[...], first_ref[...] = total[0], first[0]
        put_rows(rows_ref, (jnp.ones_like(total[1]), jnp.full_like(total[2], -1.0)) + first[1:] + total[1:])

    state = ((size, lanes), F32)
    return call(
        body, (keep, mate), shaped((mate.shape, BF16), state, ((8, lanes), F32), state), after=after, cost=LONG
    )


def level_step(bit, more, got, total, rows, entry=None, after=None):
    size, lanes = total.shape
    entries = () if entry is None else (entry,)

    def body(got_ref, total_ref, rows_ref, *refs):
        send_ref, entry_out, rows_out, *totals = refs[len(entries) :]
        upper = (position()[6] & bit) != 0
        other = unpack(got_ref)
        old = refs[0][...] if entries else jnp.zeros_like(total_ref)
        new = gather_level(upper, (old, rows_ref[0:1], rows_ref[1:2]), other)
        held = merged(upper, (total_ref[...], rows_ref[4:5], rows_ref[5:6]), other)
        pack(send_ref, held)
        entry_out[...] = new[0]
        put_rows(rows_out, new[1:] + (rows_ref[2:3], rows_ref[3:4]) + held[1:])
        if more:
            totals[0][...] = held[0]

    state = ((size, lanes), F32)
    return call(
        body, (got, total, rows, *entries),
        shaped((got.shape, BF16), state, ((8, lanes), F32), *((state,) if more else ())), after=after, cost=LONG,
    )


def entry_step(bit, with_id, got, entry, rows, first, after):
    def body(got_ref, entry_ref, rows_ref, first_ref, other_ref, keep_ref, *prev_ref):
        upper = (position()[6] & bit) != 0
        even = position()[0] == 0
        new = gather_level(upper, (entry_ref[...], rows_ref[0:1], rows_ref[1:2]), unpack(got_ref))
        last_first = rows_ref[3:4]
        link = rows_ref[2:3] * (last_first == new[2]).astype(F32)
        reached = first_ref[...] + link * new[0]
        other_ref[...] = jnp.where(even, reached, new[0]).astype(BF16)
        keep_ref[...] = jnp.where(even, new[0], reached).astype(BF16)
        if with_id:
            prev = jnp.where(even, new[2], last_first)
            prev_ref[0][...] = jnp.broadcast_to(prev[:, 0:LANES], (8, LANES))

    block = (entry.shape, BF16)
    prev = (((8, LANES), F32),) if with_id else ()
    return call(body, (got, entry, rows, first), shaped(block, block, *prev), after=after)


def local_setup(heads, width, read, write, stash, skip, after):
    toks = write.shape[0]
    half_h = heads // 2
    blocks = toks // GROUP

    def body(
        rd_ref, wr_ref, stash_ref, skip_ref,
        scores, linked_ref, log_cum, log_row, tails, skips, seg_out, pad, rows_ref,
    ):
        cum_ref, step_ref = (stash_ref.at[rows] for rows in stash_rows()[:2])
        second = [position()[which] == 1 for which in range(2)]
        pad[...] = jnp.zeros_like(pad)
        rows_ref[...] = jnp.zeros_like(rows_ref)
        rows_ref[0:1, 0:heads] = skip_ref[...]
        turned = pltpu.roll(rows_ref[...], LANES - half_h, 1)
        for which in range(2):
            skips[which] = jnp.where(second[which], turned, rows_ref[...])
        seg_row = cum_ref[SEG_LANE : SEG_LANE + 1]
        log_row[...] = cum_ref[...] * LOG2E - jnp.log(step_ref[...]) * LOG2E
        pad[0:32] = cum_ref[...] * LOG2E
        pad[SEG_LANE : SEG_LANE + 1] = seg_row
        columns = jnp.transpose(pad[...])
        seg_col = columns[:, SEG_LANE : SEG_LANE + 1]
        turned = pltpu.roll(columns, LANES - half_h, 1)
        for which in range(2):
            log_cum[which] = jnp.where(second[which], turned, columns)
        seg_out[...] = columns
        tail0 = jnp.exp(cum_ref[:, GROUP - 1 : GROUP] - cum_ref[:, 0:GROUP]) * step_ref[:, 0:GROUP]
        same = seg_row[:, 0:GROUP] == seg_row[:, GROUP - 1 : GROUP]
        pad[0:32, 0:GROUP] = jnp.where(same, tail0, 0.0)
        columns = jnp.transpose(pad[:, 0:GROUP])
        turned = pltpu.roll(columns, LANES - half_h, 1)
        for which in range(2):
            tails[which] = jnp.where(second[which], turned, columns)
        causal = lax.broadcasted_iota(jnp.int32, (GROUP, GROUP), 0) >= lax.broadcasted_iota(
            jnp.int32, (GROUP, GROUP), 1
        )
        for b in range(blocks):
            rows = slice(b * GROUP, (b + 1) * GROUP)
            s = dot(rd_ref[rows], wr_ref[rows], ((1,), (1,)))
            scores[b] = jnp.where(causal & (seg_col[rows] == seg_row[:, rows]), s, 0.0)
        linked = seg_col[GROUP:] == seg_col[GROUP - 1 : GROUP]
        linked_ref[...] = jnp.where(linked, rd_ref[GROUP:].astype(F32), 0.0).astype(BF16)

    return call(
        body, (read, write, stash, skip),
        shaped(
            ((blocks, GROUP, GROUP), F32), ((toks - GROUP, read.shape[1]), BF16), ((2, toks, LANES), F32),
            ((32, toks), F32), ((2, GROUP, LANES), F32), ((2, 8, LANES), F32), ((toks, LANES), F32),
        ),
        [pltpu.VMEM((LANES, toks), F32), pltpu.VMEM((8, LANES), F32)],
        cost=LONG, after=after,
    )


def local_part(which, tiles, heads, width, x, gate, write, setup, after):
    toks = write.shape[0]
    half_w = x.shape[1] // 2
    half_h = heads // 2
    per = LANES // width
    blocks = toks // GROUP
    strip = 64

    def body(
        x_ref, gate_ref, wr_ref, scores, linked_ref, log_cum, log_row, tails, skips, a_ref, b_ref, mix
    ):
        half = position()[which]
        lane = lane_iota(GROUP)
        for slot in range(mix.shape[0]):
            for k in range(per):
                mix[slot, k * GROUP : k * GROUP + LANES, LANES:] = jnp.zeros((LANES, GROUP - LANES), BF16)
        for n, i in enumerate(tiles):
            there = pl.ds(pl.multiple_of(half * half_w + i * LANES, LANES), LANES)
            tile = slice(n * LANES, (n + 1) * LANES)
            gains = spread(skips[which, 0:1], i * per, width)
            carry = None
            start = jnp.ones((1, LANES), F32)
            for b in range(blocks):
                rows = slice(b * GROUP, (b + 1) * GROUP)
                slot = (n * blocks + b) % mix.shape[0]
                xb = x_ref[rows, there]
                logs = []
                for k in range(per):
                    head = i * per + k
                    cb = jnp.broadcast_to(log_cum[which, rows, head : head + 1], (GROUP, LANES))
                    logs.append(cb)
                    ar = log_row[pl.ds(half * half_h + head, 1), rows]
                    for low in range(0, GROUP, strip):
                        for left in range(0, min(low + strip, GROUP), LANES):
                            gap = cb[low : low + strip] - ar[:, left : left + LANES]
                            part = jnp.exp2(jnp.minimum(gap, 60.0))
                            part = part * scores[b, low : low + strip, left : left + LANES]
                            at = k * GROUP + low
                            mix[slot, at : at + strip, left : left + LANES] = part.astype(BF16)
                both = dot(mix[slot], xb)
                inner, dec_log = both[0:GROUP], logs[0]
                for k in range(1, per):
                    inner = jnp.where(lane < k * width, inner, both[k * GROUP : (k + 1) * GROUP])
                    dec_log = jnp.where(lane < k * width, dec_log, logs[k])
                dec = jnp.exp2(dec_log)
                xf = xb.astype(F32)
                y = inner + gains * xf
                if b == 1:
                    y = y + (dot(linked_ref[...], carry[0]) + dot(linked_ref[...], carry[1])) * dec
                else:
                    xs = (xf * spread(tails[which], i * per, width)).astype(BF16)
                    s0 = dot(wr_ref[rows], xs, ((0,), (0,)))
                    s0h = s0.astype(BF16)
                    carry = (s0h, (s0 - s0h.astype(F32)).astype(BF16))
                v = gate_ref[rows, there].astype(F32)
                sg = v / (1.0 + jnp.exp(-v))
                a_ref[rows, tile] = sg * y
                b_ref[rows, tile] = sg * (dec * start)
                start = start * dec[GROUP - 1 : GROUP]

    out = ((toks, len(tiles) * LANES), F32)
    return call(
        body, (x, gate, write, *setup), shaped(out, out), [pltpu.VMEM((4, per * GROUP, GROUP), BF16)],
        cost=LONG, after=after,
    )


def side_by_side(refs):
    values = [ref[...] for ref in refs]
    return values[0] if len(values) == 1 else jnp.concatenate(values, axis=1)


def gated_part(which, lanes, rm, a_refs, b_refs, states, gain_ref):
    half_w = gain_ref.shape[1] // 2
    first = pl.multiple_of(position()[which] * half_w + lanes.start, LANES)
    here = pl.ds(first, lanes.stop - lanes.start)
    carried = [dot(rm, state[...]) for state in states]
    carried = carried[0] if len(carried) == 1 else jnp.concatenate(carried, axis=1)
    gated = side_by_side(a_refs) + side_by_side(b_refs) * carried
    sq = gated * gated
    part = sq[:, 0:LANES]
    for i in range(1, sq.shape[1] // LANES):
        part = part + sq[:, i * LANES : (i + 1) * LANES]
    squares = jnp.sum(jnp.transpose(part), axis=0, keepdims=True)
    return (gated * gain_ref[:, here]).astype(BF16), squares


def projected(which, lanes, quarter, rows, w_ref, g):
    half_w, cols = w_ref.shape[0] // 2, w_ref.shape[1] // 4
    here = pl.multiple_of(position()[which] * half_w + lanes.start, LANES)
    first = pl.multiple_of(position()[2 + quarter] * cols + rows.start, LANES)
    block = w_ref[pl.ds(here, lanes.stop - lanes.start), pl.ds(first, rows.stop - rows.start)]
    return dot(block, g, ((0,), (1,)))


def with_squares(y, squares):
    high = squares.astype(BF16).astype(F32)
    middle = (squares - high).astype(BF16).astype(F32)
    row = lax.broadcasted_iota(jnp.int32, (EXTRA, squares.shape[1]), 0)
    rows = jnp.where(row == 0, high, jnp.where(row == 1, middle, squares - high - middle))
    return jnp.concatenate([y, rows], axis=0).astype(BF16)


def split_squares(ref):
    size = ref.shape[0] - EXTRA
    whole = ref[...].astype(F32)
    return whole[0:size], whole[size : size + 1] + (whole[size + 1 : size + 2] + whole[size + 2 : size + 3])


def gated_sums(which, lanes, reads, a, b, states, gain, weight, partial=None, squares=None):
    toks = reads[0].shape[0]
    masks = len(reads) > 1
    cols = weight.shape[1] // 4
    earlier = () if partial is None else (partial, squares)
    ends = [0, len(a), len(a) + len(b), len(a) + len(b) + len(states)]

    def body(gain_ref, w_ref, rd_ref, *refs):
        if masks:
            prev_ref, seg_ref, *refs, rm_ref = refs
            linked = seg_ref[:, SEG_LANE : SEG_LANE + 1] == prev_ref[0:1, 0:1]
            rm = jnp.where(linked, rd_ref[...].astype(F32), 0.0).astype(BF16)
            rm_ref[...] = rm
        else:
            rm = rd_ref[...]
        a_refs, b_refs, s_refs = (refs[low:high] for low, high in zip(ends, ends[1:]))
        old, (g_ref, s_ref, y_ref) = refs[ends[-1] : -3], refs[-3:]
        g, s = gated_part(which, lanes, rm, a_refs, b_refs, s_refs, gain_ref)
        g_ref[...] = g
        s_ref[...] = s + old[1][...] if old else s
        y = projected(which, lanes, 0, slice(0, cols), w_ref, g)
        y_ref[...] = y + old[0][...] if old else y

    return call(
        body, (gain, weight, *reads, *a, *b, *states, *earlier),
        shaped(
            ((toks, lanes.stop - lanes.start), BF16), ((1, toks), F32), ((cols, toks), F32),
            *([(reads[0].shape, BF16)] if masks else []),
        ),
    )


def gated_last(lanes, rows, read, a, b, state, gain, weight, partial, squares):
    toks = read.shape[0]

    def body(rd_ref, a_ref, b_ref, e_ref, gain_ref, w_ref, p_ref, s_ref, g_ref, y_ref):
        g, s = gated_part(1, lanes, rd_ref[...], (a_ref,), (b_ref,), (e_ref,), gain_ref)
        g_ref[...] = g
        y = p_ref[rows] + projected(1, lanes, 0, rows, w_ref, g)
        y_ref[...] = with_squares(y, s_ref[...] + s)

    return call(
        body, (read, a, b, state, gain, weight, partial, squares),
        shaped(((toks, lanes.stop - lanes.start), BF16), ((rows.stop - rows.start + EXTRA, toks), BF16)),
    )


def project_next(groups, gs, top, rest, partial, weight, after):
    toks = gs[0].shape[0]

    def body(p_ref, w_ref, *refs):
        g_refs, (near_ref, top_ref, rest_ref) = refs[: len(gs)], refs[len(gs) :]
        which, lanes = groups[-1]
        near = p_ref[rest] + projected(which, lanes, 0, rest, w_ref, g_refs[-1][...])
        near_ref[...] = near.astype(BF16)
        for rows, y_ref in ((top, top_ref), (rest, rest_ref)):
            y_ref[...] = sum(
                projected(which, lanes, 1, rows, w_ref, g_ref[...])
                for (which, lanes), g_ref in zip(groups, g_refs)
            )

    size = rest.stop - rest.start
    out = shaped(((size, toks), BF16), ((top.stop, toks), F32), ((size, toks), F32))
    return call(body, (partial, weight, *gs), out, after=after)


def project_whole(quarter, groups, gs, weight, pieces, adds=(), after=None):
    cols = weight.shape[1] // 4
    toks = gs[0].shape[0]
    step = cols // pieces

    def body(w_ref, *refs):
        g_refs, add_refs, outs = refs[: len(gs)], refs[len(gs) : len(gs) + len(adds)], refs[len(gs) + len(adds) :]
        y = sum(
            projected(which, lanes, quarter, slice(0, cols), w_ref, g_ref[...])
            for (which, lanes), g_ref in zip(groups, g_refs)
        )
        if add_refs:
            outs[0][...] = y + jnp.concatenate([r[...].astype(F32) for r in add_refs], axis=0)
        else:
            for k, y_ref in enumerate(outs):
                y_ref[...] = y[k * step : (k + 1) * step].astype(BF16)

    out = shaped(((cols, toks), F32)) if adds else shaped(*[((step, toks), BF16)] * pieces)
    return call(body, (weight, *gs, *adds), out, after=after)


def add_first(y_far, to_near, got_near):
    def body(y_ref, mine_ref, got_ref, out_ref):
        got, squares = split_squares(got_ref)
        out_ref[...] = with_squares(y_ref[...] + got, split_squares(mine_ref)[1] + squares)

    return call(body, (y_far, to_near, got_near), jax.ShapeDtypeStruct(got_near.shape, BF16))


def add_second(y_far, got_near, after):
    def body(y_ref, got_ref, out_ref):
        out_ref[...] = (y_ref[...] + got_ref[...].astype(F32)).astype(BF16)

    return call(body, (y_far, got_near), jax.ShapeDtypeStruct(got_near.shape, BF16), after=after)


def finish(rows, y_own, inputs, out=None, features=None):
    size, toks = y_own.shape
    parts = 2
    step = (rows.stop - rows.start) // parts
    first = out is None

    def body(own_ref, far_ref, factor_ref, *refs):
        out_hbm, *more, out_ref, sems = refs if first else refs[1:]
        if first:
            inv = lax.rsqrt((split_squares(factor_ref)[1] + split_squares(far_ref)[1]) / features + EPS)
            more[0][...] = inv
        else:
            inv = factor_ref[...]
        copies = []
        for k in range(parts):
            here = slice(k * step, (k + 1) * step)
            there = slice(rows.start + here.start, rows.start + here.stop)
            out_ref[here] = ((own_ref[there] + far_ref[here].astype(F32)) * inv).astype(BF16)
            copies.append(pltpu.make_async_copy(out_ref.at[here], out_hbm.at[there], sems.at[k]))
            copies[-1].start()
        for copy in copies:
            copy.wait()

    vm, where = pl.BlockSpec(memory_space=pltpu.VMEM), pl.BlockSpec(memory_space=pl.ANY)
    result = jax.ShapeDtypeStruct((size, toks), BF16)
    return pl.pallas_call(
        body,
        in_specs=[vm] * 3 + ([] if first else [where]),
        out_specs=[where, vm] if first else where,
        out_shape=[result, jax.ShapeDtypeStruct((1, toks), F32)] if first else result,
        scratch_shapes=[pltpu.VMEM((rows.stop - rows.start, toks), BF16), pltpu.SemaphoreType.DMA((parts,))],
        input_output_aliases={} if first else {3: 0},
        compiler_params=pltpu.CompilerParams(vmem_limit_bytes=VMEM),
        cost_estimate=CHEAP,
    )(y_own, *inputs, *(() if first else (out,)))


def on_device(
    n_seq, n_tp, head_input, gate_input, write_vecs, read_vecs, step_raw, segment_ids,
    decay_log, step_bias, skip_gain, norm_gain, out_weight,
):
    heads = decay_log.shape[0]
    toks, feats = head_input.shape
    width = feats // heads
    def swap(a, bit):
        return lax.ppermute(a, "seq", [(i, i ^ bit) for i in range(n_seq)])

    def across(a, bit):
        return lax.ppermute(a, "tp", [(i, i ^ bit) for i in range(n_tp)])

    other_one, stash = prepare(
        heads, width, step_raw, segment_ids.reshape(1, toks), decay_log.reshape(1, heads),
        step_bias.reshape(1, heads), head_input, write_vecs,
    )
    mate_one = swap(other_one, 1)
    other_two, keep_one, keep_two = more_states(width, stash, head_input, write_vecs)
    mate_two = swap(other_two, 1)
    *setup, seg = local_setup(
        heads, width, read_vecs, write_vecs, stash, skip_gain.reshape(1, heads), other_two
    )

    def local(which, tiles, after):
        return local_part(which, tiles, heads, width, head_input, gate_input, write_vecs, setup, after)

    tiles = feats // 2 // LANES
    edge = EARLY_LANES // LANES
    early = pair_step(keep_one, mate_one, seg)
    keep_a = local(0, range(0, tiles - edge), early[0])
    late = pair_step(keep_two, mate_two, keep_a[0])
    keep_b = local(0, range(tiles - edge, tiles), late[0])
    sent, totals, rows, firsts = zip(early, late)
    entries = [()] * 2
    bit, before = 2, keep_b[0]
    while 2 * bit < n_seq:
        more = 4 * bit < n_seq
        got = [swap(piece, bit) for piece in sent]
        early = level_step(bit, more, got[0], totals[0], rows[0], *entries[0], after=before)
        if bit == 2:
            other_a = local(1, range(0, edge), early[0])
        late = level_step(bit, more, got[1], totals[1], rows[1], *entries[1], after=other_a[0] if bit == 2 else early[0])
        sent, entries, rows, *totals = zip(early, late)
        totals, entries = totals[0] if more else (), [(entry,) for entry in entries]
        bit, before = bit * 2, None
    other_b = local(1, range(edge, tiles), sent[1])
    half_w = feats // 2
    quarter = out_weight.shape[1] // 4
    one, two = slice(0, EARLY_LANES), slice(EARLY_LANES, half_w)
    top, rest, every = slice(0, EARLY_ROWS), slice(EARLY_ROWS, quarter), slice(0, quarter)
    send_one, keep_one, prev = entry_step(
        bit, True, swap(sent[0], bit), *entries[0], rows[0], firsts[0], other_b[0]
    )
    other_one = swap(send_one, 1)
    send_two, keep_two = entry_step(bit, False, swap(sent[1], bit), *entries[1], rows[1], firsts[1], send_one)
    other_two = swap(send_two, 1)
    gain = norm_gain.reshape(1, feats)
    whole_half = slice(0, half_w)
    g_keep, squares, partial, linked = gated_sums(
        0, whole_half, (read_vecs, prev, seg), (keep_a[0], keep_b[0]), (keep_a[1], keep_b[1]), (keep_one, keep_two), gain, out_weight
    )
    g_one, squares, partial = gated_sums(
        1, one, (linked,), other_a[:1], other_a[1:], (other_one,), gain, out_weight, partial, squares
    )
    g_two, near_top = gated_last(two, top, linked, *other_b, other_two, gain, out_weight, partial, squares)
    got_top = across(near_top, 1)
    groups, gs = ((0, whole_half), (1, one), (1, two)), (g_keep, g_one, g_two)
    near_rest, far_top, far_rest = project_next(groups, gs, top, rest, partial, out_weight, near_top)
    got_rest = across(near_rest, 1)
    to_far_top = add_first(far_top, near_top, got_top)
    got_far_top = across(to_far_top, 2)
    to_far_rest = add_second(far_rest, got_rest, to_far_top)
    got_far_rest = across(to_far_rest, 2)
    y_near = project_whole(2, groups, gs, out_weight, NEAR_PIECES, after=to_far_rest)
    got_own = tuple(across(piece, 1) for piece in y_near)
    (y_own,) = project_whole(3, groups, gs, out_weight, 1, got_own)
    out, inv = finish(top, y_own, (got_far_top, to_far_top), features=feats * n_tp)
    return finish(rest, y_own, (got_far_rest, inv), out)


def solution(mesh):
    in_specs = (
        P("seq", "tp"),
        P("seq", "tp"),
        P("seq", None),
        P("seq", None),
        P("tp", "seq"),
        P("seq"),
        P("tp"),
        P("tp"),
        P("tp"),
        P("tp"),
        P("tp", None),
    )
    out_specs = P("tp", "seq")
    return jax.shard_map(
        functools.partial(on_device, mesh.shape["seq"], mesh.shape["tp"]),
        mesh=mesh, in_specs=in_specs, out_specs=out_specs, check_vma=False,
    )
```

```python
import functools

import jax
import jax.numpy as jnp
from jax import lax
from jax.experimental import pallas as pl
from jax.experimental.pallas import tpu as pltpu
from jax.sharding import PartitionSpec as P

GROUP = 256
LANES = 128
EPS = 1e-05
LOG2E = 1.4426950408889634
SEG_LANE = 24
EXTRA = 8
EARLY_ROWS = 384
NEAR_PIECES = 4
EARLY_LANES = 384
VMEM = 16 * 1024 * 1024
VMEM_ALL = 56 * 1024 * 1024
CHEAP = pl.CostEstimate(flops=1000, bytes_accessed=1000, transcendentals=0)
LONG = pl.CostEstimate(flops=4_000_000_000, bytes_accessed=1000, transcendentals=0)
F32 = jnp.float32
BF16 = jnp.bfloat16


def dot(a, b, dims=((1,), (0,))):
    return lax.dot_general(a, b, (dims, ((), ())), preferred_element_type=F32)


def lane_iota(rows):
    return lax.broadcasted_iota(jnp.int32, (rows, LANES), 1)


def spread(cols, first, width):
    rows = cols.shape[0]
    per = LANES // width
    lane = lane_iota(rows)
    out = jnp.broadcast_to(cols[:, first : first + 1], (rows, LANES))
    for k in range(1, per):
        nxt = jnp.broadcast_to(cols[:, first + k : first + k + 1], (rows, LANES))
        out = jnp.where(lane < k * width, out, nxt)
    return out


def position():
    place, rank = lax.axis_index("seq"), lax.axis_index("tp")
    odd = place & 1
    far = rank ^ 2
    return odd, 1 - odd, far ^ 1, far, rank ^ 1, rank, place


def call(body, args, out_shape, scratch=(), after=None, cost=CHEAP):
    vm = pl.BlockSpec(memory_space=pltpu.VMEM)
    specs = [vm] * len(args)
    operands = list(args)
    kernel = body
    if after is not None:
        specs.append(pl.BlockSpec(memory_space=pl.ANY))
        operands.append(after)
        at = len(operands) - 1

        def kernel(*refs):
            body(*refs[:at], *refs[at + 1 :])

    return pl.pallas_call(
        kernel,
        in_specs=specs,
        out_specs=jax.tree.map(lambda _: vm, out_shape),
        out_shape=out_shape,
        scratch_shapes=list(scratch),
        compiler_params=pltpu.CompilerParams(vmem_limit_bytes=VMEM),
        cost_estimate=cost,
    )(*operands)


def shaped(*shapes):
    return [jax.ShapeDtypeStruct(shape, dtype) for shape, dtype in shapes]


def pack(out_ref, total):
    state, through, last = total
    high = through.astype(BF16).astype(F32)
    row = lax.broadcasted_iota(jnp.int32, (EXTRA, state.shape[1]), 0)
    rows = jnp.where(row == 0, high, jnp.where(row == 1, through - high, last))
    out_ref[...] = jnp.concatenate([state, rows], axis=0).astype(BF16)


def unpack(ref):
    size = ref.shape[0] - EXTRA
    whole = ref[...].astype(F32)
    return whole[0:size], whole[size : size + 1] + whole[size + 1 : size + 2], whole[size + 2 : size + 3]


def merged(swapped, one, two):
    later = jnp.where(swapped, one[1], two[1])
    link = later * (one[2] == two[2]).astype(F32)
    state = jnp.where(swapped, 1.0, link) * one[0] + jnp.where(swapped, link, 1.0) * two[0]
    return state, one[1] * two[1], jnp.where(swapped, one[2], two[2])


def stash_rows():
    return slice(0, 32), slice(32, 64), slice(64, 96), slice(96, 104)


def put_rows(rows_ref, rows):
    lanes = rows_ref.shape[1]
    for at, row in enumerate(rows):
        rows_ref[at : at + 1] = jnp.broadcast_to(row, (1, lanes))


def some_state(half, half_w, lanes, width, vecs, tails_ref, through_row, last, x_ref, first_lane, out_ref):
    state = vecs.shape[0]
    per = LANES // width
    half_h = half_w // width
    skipped = lanes.start // width
    lane = lane_iota(state)
    mine = jnp.where(half == 1, pltpu.roll(through_row, LANES - half_h, 1), through_row)
    own, through = [], []
    for i in range((lanes.stop - lanes.start) // LANES):
        written = []
        for k in range(per):
            row = tails_ref[pl.ds(half * half_h + skipped + i * per + k, 1), :]
            written.append((vecs * row).astype(BF16))
        here = pl.ds(pl.multiple_of(first_lane + i * LANES, LANES), LANES)
        both = dot(jnp.concatenate(written, axis=0), x_ref[:, here])
        tile = both[0:state]
        for k in range(1, per):
            tile = jnp.where(lane < k * width, tile, both[k * state : (k + 1) * state])
        own.append(tile)
        through.append(spread(mine[0:1], skipped + i * per, width))
    ids = jnp.broadcast_to(last, (1, lanes.stop - lanes.start))
    group = (jnp.concatenate(own, axis=1), jnp.concatenate(through, axis=1), ids)
    pack(out_ref, group)


def prepare(heads, width, raw, seg, decay_log, bias, x, write):
    toks, state = write.shape
    half_w = x.shape[1] // 2
    blocks = toks // GROUP
    arrays = (raw, seg, decay_log, bias, write, x)

    def body(*refs):
        hbm, (other_ref, stash_ref) = refs[: len(arrays)], refs[len(arrays) : -8]
        raw_ref, seg_ref, dl_ref, sb_ref, wr_ref, x_ref, rows, sems = refs[-8:]
        half = position()[1]
        lanes = pl.ds(pl.multiple_of(half * half_w, LANES), EARLY_LANES)
        sources = (*hbm[:5], hbm[5].at[:, lanes])
        copies = [
            pltpu.make_async_copy(src, dst, sems.at[k])
            for k, (src, dst) in enumerate(zip(sources, (raw_ref, seg_ref, dl_ref, sb_ref, wr_ref, x_ref)))
        ]
        for copy in copies:
            copy.start()
        rows[...] = jnp.zeros_like(rows)
        tri = (
            lax.broadcasted_iota(jnp.int32, (GROUP, GROUP), 0)
            <= lax.broadcasted_iota(jnp.int32, (GROUP, GROUP), 1)
        ).astype(BF16)
        stash_ref[...] = jnp.zeros_like(stash_ref)
        cum_rows, step_rows, tail_rows, sum_rows = stash_rows()
        for copy in copies[:4]:
            copy.wait()
        rows[0:1, 0:heads] = dl_ref[...]
        rows[1:2, 0:heads] = sb_ref[...]
        stash_ref[0:heads] = raw_ref[...].astype(F32)
        params = jnp.transpose(rows[...])[0:32]
        z = stash_ref[cum_rows] + params[:, 1:2]
        step = jnp.maximum(z, 0.0) + jnp.log1p(jnp.exp(-jnp.abs(z)))
        rate = -jnp.exp(params[:, 0:1]) * step
        cum, full = [], []
        base = jnp.zeros((32, 1), F32)
        for b in range(blocks):
            r = rate[:, b * GROUP : (b + 1) * GROUP]
            r1 = r.astype(BF16)
            d1 = r - r1.astype(F32)
            r2 = d1.astype(BF16)
            r3 = (d1 - r2.astype(F32)).astype(BF16)
            c = dot(r1, tri) + (dot(r2, tri) + dot(r3, tri))
            cum.append(c)
            full.append(c + base)
            base = base + c[:, GROUP - 1 : GROUP]
        seg_row = seg_ref[...].astype(F32)
        last = seg_row[:, toks - 1 : toks]
        tail = jnp.exp(base - jnp.concatenate(full, axis=1)) * step
        stash_ref[cum_rows] = jnp.concatenate(cum, axis=1)
        stash_ref[SEG_LANE : SEG_LANE + 1] = seg_row
        stash_ref[step_rows] = step
        stash_ref[tail_rows] = jnp.where(seg_row == last, tail, 0.0)
        rows[...] = jnp.zeros_like(rows)
        rows[0:32] = jnp.broadcast_to(jnp.exp(base), (32, LANES))
        sums = jnp.transpose(rows[...])[0:8]
        stash_ref[sum_rows, 0:LANES] = sums
        for copy in copies[4:]:
            copy.wait()
        vecs = jnp.transpose(wr_ref[...].astype(F32))
        piece = slice(0, EARLY_LANES)
        some_state(half, half_w, piece, width, vecs, stash_ref.at[tail_rows], sums, last, x_ref, 0, other_ref)

    vm = pl.BlockSpec(memory_space=pltpu.VMEM)
    out_shape = shaped(((state + EXTRA, EARLY_LANES), BF16), ((stash_rows()[-1].stop, toks), F32))
    return pl.pallas_call(
        body,
        in_specs=[pl.BlockSpec(memory_space=pltpu.HBM)] * len(arrays),
        out_specs=[vm] * len(out_shape),
        out_shape=out_shape,
        scratch_shapes=[
            *[pltpu.VMEM(a.shape, a.dtype) for a in arrays[:5]], pltpu.VMEM((toks, EARLY_LANES), BF16),
            pltpu.VMEM((LANES, LANES), F32), pltpu.SemaphoreType.DMA((len(arrays),)),
        ],
        compiler_params=pltpu.CompilerParams(vmem_limit_bytes=VMEM_ALL),
        cost_estimate=LONG,
    )(*arrays)


def more_states(width, stash, x, write):
    toks, state = write.shape
    half_w = x.shape[1] // 2
    one, two = slice(0, EARLY_LANES), slice(EARLY_LANES, half_w)
    pieces = ((1, two), (0, one), (0, two))

    def body(stash_ref, x_ref, wr_ref, *outs):
        _, _, tail_rows, sum_rows = stash_rows()
        vecs = jnp.transpose(wr_ref[...].astype(F32))
        last = stash_ref[SEG_LANE : SEG_LANE + 1, toks - 1 : toks]
        sums = stash_ref[sum_rows, 0:LANES]
        tails_ref = stash_ref.at[tail_rows]
        for (which, lanes), out_ref in zip(pieces, outs):
            half = position()[which]
            first = half * half_w + lanes.start
            some_state(half, half_w, lanes, width, vecs, tails_ref, sums, last, x_ref, first, out_ref)

    out = shaped(*[((state + EXTRA, lanes.stop - lanes.start), BF16) for _, lanes in pieces])
    return call(body, (stash, x, write), out)


def gather_level(upper, entry, other):
    state, through, last_id = entry
    link = through * ((last_id < 0) | (other[2] == last_id)).astype(F32)
    state = state + jnp.where(upper, link, 0.0) * other[0]
    last_id = jnp.where(upper & (last_id < 0), other[2], last_id)
    return state, through * jnp.where(upper, other[1], 1.0), last_id


def pair_step(keep, mate, after=None):
    size, lanes = mate.shape[0] - EXTRA, mate.shape[1]

    def body(keep_ref, mate_ref, send_ref, total_ref, rows_ref, first_ref):
        odd = position()[0] == 1
        mine, mate = unpack(keep_ref), unpack(mate_ref)
        total = merged(odd, mine, mate)
        first = tuple(jnp.where(odd, m, o) for o, m in zip(mine, mate))
        pack(send_ref, total)
        total_ref[...], first_ref[...] = total[0], first[0]
        put_rows(rows_ref, (jnp.ones_like(total[1]), jnp.full_like(total[2], -1.0)) + first[1:] + total[1:])

    state = ((size, lanes), F32)
    return call(
        body, (keep, mate), shaped((mate.shape, BF16), state, ((8, lanes), F32), state), after=after, cost=LONG
    )


def level_step(bit, more, got, total, rows, entry=None, after=None):
    size, lanes = total.shape
    entries = () if entry is None else (entry,)

    def body(got_ref, total_ref, rows_ref, *refs):
        send_ref, entry_out, rows_out, *totals = refs[len(entries) :]
        upper = (position()[6] & bit) != 0
        other = unpack(got_ref)
        old = refs[0][...] if entries else jnp.zeros_like(total_ref)
        new = gather_level(upper, (old, rows_ref[0:1], rows_ref[1:2]), other)
        held = merged(upper, (total_ref[...], rows_ref[4:5], rows_ref[5:6]), other)
        pack(send_ref, held)
        entry_out[...] = new[0]
        put_rows(rows_out, new[1:] + (rows_ref[2:3], rows_ref[3:4]) + held[1:])
        if more:
            totals[0][...] = held[0]

    state = ((size, lanes), F32)
    return call(
        body, (got, total, rows, *entries),
        shaped((got.shape, BF16), state, ((8, lanes), F32), *((state,) if more else ())), after=after, cost=LONG,
    )


def entry_step(bit, with_id, got, entry, rows, first, after):
    def body(got_ref, entry_ref, rows_ref, first_ref, other_ref, keep_ref, *prev_ref):
        upper = (position()[6] & bit) != 0
        even = position()[0] == 0
        new = gather_level(upper, (entry_ref[...], rows_ref[0:1], rows_ref[1:2]), unpack(got_ref))
        last_first = rows_ref[3:4]
        link = rows_ref[2:3] * (last_first == new[2]).astype(F32)
        reached = first_ref[...] + link * new[0]
        other_ref[...] = jnp.where(even, reached, new[0]).astype(BF16)
        keep_ref[...] = jnp.where(even, new[0], reached).astype(BF16)
        if with_id:
            prev = jnp.where(even, new[2], last_first)
            prev_ref[0][...] = jnp.broadcast_to(prev[:, 0:LANES], (8, LANES))

    block = (entry.shape, BF16)
    prev = (((8, LANES), F32),) if with_id else ()
    return call(body, (got, entry, rows, first), shaped(block, block, *prev), after=after)


def local_setup(heads, width, read, write, stash, skip, after):
    toks = write.shape[0]
    half_h = heads // 2
    blocks = toks // GROUP

    def body(
        rd_ref, wr_ref, stash_ref, skip_ref,
        scores, linked_ref, log_cum, log_row, tails, skips, seg_out, pad, rows_ref,
    ):
        cum_ref, step_ref = (stash_ref.at[rows] for rows in stash_rows()[:2])
        second = [position()[which] == 1 for which in range(2)]
        pad[...] = jnp.zeros_like(pad)
        rows_ref[...] = jnp.zeros_like(rows_ref)
        rows_ref[0:1, 0:heads] = skip_ref[...]
        turned = pltpu.roll(rows_ref[...], LANES - half_h, 1)
        for which in range(2):
            skips[which] = jnp.where(second[which], turned, rows_ref[...])
        seg_row = cum_ref[SEG_LANE : SEG_LANE + 1]
        log_row[...] = cum_ref[...] * LOG2E - jnp.log(step_ref[...]) * LOG2E
        pad[0:32] = cum_ref[...] * LOG2E
        pad[SEG_LANE : SEG_LANE + 1] = seg_row
        columns = jnp.transpose(pad[...])
        seg_col = columns[:, SEG_LANE : SEG_LANE + 1]
        turned = pltpu.roll(columns, LANES - half_h, 1)
        for which in range(2):
            log_cum[which] = jnp.where(second[which], turned, columns)
        seg_out[...] = columns
        tail0 = jnp.exp(cum_ref[:, GROUP - 1 : GROUP] - cum_ref[:, 0:GROUP]) * step_ref[:, 0:GROUP]
        same = seg_row[:, 0:GROUP] == seg_row[:, GROUP - 1 : GROUP]
        pad[0:32, 0:GROUP] = jnp.where(same, tail0, 0.0)
        columns = jnp.transpose(pad[:, 0:GROUP])
        turned = pltpu.roll(columns, LANES - half_h, 1)
        for which in range(2):
            tails[which] = jnp.where(second[which], turned, columns)
        causal = lax.broadcasted_iota(jnp.int32, (GROUP, GROUP), 0) >= lax.broadcasted_iota(
            jnp.int32, (GROUP, GROUP), 1
        )
        for b in range(blocks):
            rows = slice(b * GROUP, (b + 1) * GROUP)
            s = dot(rd_ref[rows], wr_ref[rows], ((1,), (1,)))
            scores[b] = jnp.where(causal & (seg_col[rows] == seg_row[:, rows]), s, 0.0)
        linked = seg_col[GROUP:] == seg_col[GROUP - 1 : GROUP]
        linked_ref[...] = jnp.where(linked, rd_ref[GROUP:].astype(F32), 0.0).astype(BF16)

    return call(
        body, (read, write, stash, skip),
        shaped(
            ((blocks, GROUP, GROUP), F32), ((toks - GROUP, read.shape[1]), BF16), ((2, toks, LANES), F32),
            ((32, toks), F32), ((2, GROUP, LANES), F32), ((2, 8, LANES), F32), ((toks, LANES), F32),
        ),
        [pltpu.VMEM((LANES, toks), F32), pltpu.VMEM((8, LANES), F32)],
        cost=LONG, after=after,
    )


def local_part(which, tiles, heads, width, x, gate, write, setup, after):
    toks = write.shape[0]
    half_w = x.shape[1] // 2
    half_h = heads // 2
    per = LANES // width
    blocks = toks // GROUP
    strip = 64

    def body(
        x_ref, gate_ref, wr_ref, scores, linked_ref, log_cum, log_row, tails, skips, a_ref, b_ref, mix
    ):
        half = position()[which]
        lane = lane_iota(GROUP)
        for slot in range(mix.shape[0]):
            for k in range(per):
                mix[slot, k * GROUP : k * GROUP + LANES, LANES:] = jnp.zeros((LANES, GROUP - LANES), BF16)
        for n, i in enumerate(tiles):
            there = pl.ds(pl.multiple_of(half * half_w + i * LANES, LANES), LANES)
            tile = slice(n * LANES, (n + 1) * LANES)
            gains = spread(skips[which, 0:1], i * per, width)
            carry = None
            start = jnp.ones((1, LANES), F32)
            for b in range(blocks):
                rows = slice(b * GROUP, (b + 1) * GROUP)
                slot = (n * blocks + b) % mix.shape[0]
                xb = x_ref[rows, there]
                logs = []
                for k in range(per):
                    head = i * per + k
                    cb = jnp.broadcast_to(log_cum[which, rows, head : head + 1], (GROUP, LANES))
                    logs.append(cb)
                    ar = log_row[pl.ds(half * half_h + head, 1), rows]
                    for low in range(0, GROUP, strip):
                        for left in range(0, min(low + strip, GROUP), LANES):
                            gap = cb[low : low + strip] - ar[:, left : left + LANES]
                            part = jnp.exp2(jnp.minimum(gap, 60.0))
                            part = part * scores[b, low : low + strip, left : left + LANES]
                            at = k * GROUP + low
                            mix[slot, at : at + strip, left : left + LANES] = part.astype(BF16)
                both = dot(mix[slot], xb)
                inner, dec_log = both[0:GROUP], logs[0]
                for k in range(1, per):
                    inner = jnp.where(lane < k * width, inner, both[k * GROUP : (k + 1) * GROUP])
                    dec_log = jnp.where(lane < k * width, dec_log, logs[k])
                dec = jnp.exp2(dec_log)
                xf = xb.astype(F32)
                y = inner + gains * xf
                if b == 1:
                    y = y + (dot(linked_ref[...], carry[0]) + dot(linked_ref[...], carry[1])) * dec
                else:
                    xs = (xf * spread(tails[which], i * per, width)).astype(BF16)
                    s0 = dot(wr_ref[rows], xs, ((0,), (0,)))
                    s0h = s0.astype(BF16)
                    carry = (s0h, (s0 - s0h.astype(F32)).astype(BF16))
                v = gate_ref[rows, there].astype(F32)
                sg = v / (1.0 + jnp.exp(-v))
                a_ref[rows, tile] = sg * y
                b_ref[rows, tile] = sg * (dec * start)
                start = start * dec[GROUP - 1 : GROUP]

    out = ((toks, len(tiles) * LANES), F32)
    return call(
        body, (x, gate, write, *setup), shaped(out, out), [pltpu.VMEM((4, per * GROUP, GROUP), BF16)],
        cost=LONG, after=after,
    )


def side_by_side(refs):
    values = [ref[...] for ref in refs]
    return values[0] if len(values) == 1 else jnp.concatenate(values, axis=1)


def gated_part(which, lanes, rm, a_refs, b_refs, states, gain_ref):
    half_w = gain_ref.shape[1] // 2
    first = pl.multiple_of(position()[which] * half_w + lanes.start, LANES)
    here = pl.ds(first, lanes.stop - lanes.start)
    carried = [dot(rm, state[...]) for state in states]
    carried = carried[0] if len(carried) == 1 else jnp.concatenate(carried, axis=1)
    gated = side_by_side(a_refs) + side_by_side(b_refs) * carried
    sq = gated * gated
    part = sq[:, 0:LANES]
    for i in range(1, sq.shape[1] // LANES):
        part = part + sq[:, i * LANES : (i + 1) * LANES]
    squares = jnp.sum(jnp.transpose(part), axis=0, keepdims=True)
    return (gated * gain_ref[:, here]).astype(BF16), squares


def projected(which, lanes, quarter, rows, w_ref, g):
    half_w, cols = w_ref.shape[0] // 2, w_ref.shape[1] // 4
    here = pl.multiple_of(position()[which] * half_w + lanes.start, LANES)
    first = pl.multiple_of(position()[2 + quarter] * cols + rows.start, LANES)
    block = w_ref[pl.ds(here, lanes.stop - lanes.start), pl.ds(first, rows.stop - rows.start)]
    return dot(block, g, ((0,), (1,)))


def with_squares(y, squares):
    high = squares.astype(BF16).astype(F32)
    middle = (squares - high).astype(BF16).astype(F32)
    row = lax.broadcasted_iota(jnp.int32, (EXTRA, squares.shape[1]), 0)
    rows = jnp.where(row == 0, high, jnp.where(row == 1, middle, squares - high - middle))
    return jnp.concatenate([y, rows], axis=0).astype(BF16)


def split_squares(ref):
    size = ref.shape[0] - EXTRA
    whole = ref[...].astype(F32)
    return whole[0:size], whole[size : size + 1] + (whole[size + 1 : size + 2] + whole[size + 2 : size + 3])


def gated_sums(which, lanes, reads, a, b, states, gain, weight, partial=None, squares=None):
    toks = reads[0].shape[0]
    masks = len(reads) > 1
    cols = weight.shape[1] // 4
    earlier = () if partial is None else (partial, squares)
    ends = [0, len(a), len(a) + len(b), len(a) + len(b) + len(states)]

    def body(gain_ref, w_ref, rd_ref, *refs):
        if masks:
            prev_ref, seg_ref, *refs, rm_ref = refs
            linked = seg_ref[:, SEG_LANE : SEG_LANE + 1] == prev_ref[0:1, 0:1]
            rm = jnp.where(linked, rd_ref[...].astype(F32), 0.0).astype(BF16)
            rm_ref[...] = rm
        else:
            rm = rd_ref[...]
        a_refs, b_refs, s_refs = (refs[low:high] for low, high in zip(ends, ends[1:]))
        old, (g_ref, s_ref, y_ref) = refs[ends[-1] : -3], refs[-3:]
        g, s = gated_part(which, lanes, rm, a_refs, b_refs, s_refs, gain_ref)
        g_ref[...] = g
        s_ref[...] = s + old[1][...] if old else s
        y = projected(which, lanes, 0, slice(0, cols), w_ref, g)
        y_ref[...] = y + old[0][...] if old else y

    return call(
        body, (gain, weight, *reads, *a, *b, *states, *earlier),
        shaped(
            ((toks, lanes.stop - lanes.start), BF16), ((1, toks), F32), ((cols, toks), F32),
            *([(reads[0].shape, BF16)] if masks else []),
        ),
    )


def gated_last(lanes, rows, read, a, b, state, gain, weight, partial, squares):
    toks = read.shape[0]

    def body(rd_ref, a_ref, b_ref, e_ref, gain_ref, w_ref, p_ref, s_ref, g_ref, y_ref):
        g, s = gated_part(1, lanes, rd_ref[...], (a_ref,), (b_ref,), (e_ref,), gain_ref)
        g_ref[...] = g
        y = p_ref[rows] + projected(1, lanes, 0, rows, w_ref, g)
        y_ref[...] = with_squares(y, s_ref[...] + s)

    return call(
        body, (read, a, b, state, gain, weight, partial, squares),
        shaped(((toks, lanes.stop - lanes.start), BF16), ((rows.stop - rows.start + EXTRA, toks), BF16)),
    )


def project_next(groups, gs, top, rest, partial, weight, after):
    toks = gs[0].shape[0]

    def body(p_ref, w_ref, *refs):
        g_refs, (near_ref, top_ref) = refs[: len(gs)], refs[len(gs) :]
        which, lanes = groups[-1]
        near = p_ref[rest] + projected(which, lanes, 0, rest, w_ref, g_refs[-1][...])
        near_ref[...] = near.astype(BF16)
        top_ref[...] = sum(
            projected(which, lanes, 1, top, w_ref, g_ref[...]) for (which, lanes), g_ref in zip(groups, g_refs)
        )

    size = rest.stop - rest.start
    out = shaped(((size, toks), BF16), ((top.stop, toks), F32))
    return call(body, (partial, weight, *gs), out, after=after)


def project_whole(quarter, groups, gs, weight, pieces, adds=(), after=None):
    cols = weight.shape[1] // 4
    toks = gs[0].shape[0]
    step = cols // pieces

    def body(w_ref, *refs):
        g_refs, add_refs, outs = refs[: len(gs)], refs[len(gs) : len(gs) + len(adds)], refs[len(gs) + len(adds) :]
        y = sum(
            projected(which, lanes, quarter, slice(0, cols), w_ref, g_ref[...])
            for (which, lanes), g_ref in zip(groups, g_refs)
        )
        if add_refs:
            outs[0][...] = y + jnp.concatenate([r[...].astype(F32) for r in add_refs], axis=0)
        else:
            for k, y_ref in enumerate(outs):
                y_ref[...] = y[k * step : (k + 1) * step].astype(BF16)

    out = shaped(((cols, toks), F32)) if adds else shaped(*[((step, toks), BF16)] * pieces)
    return call(body, (weight, *gs, *adds), out, after=after)


def add_first(y_far, to_near, got_near):
    def body(y_ref, mine_ref, got_ref, out_ref):
        got, squares = split_squares(got_ref)
        out_ref[...] = with_squares(y_ref[...] + got, split_squares(mine_ref)[1] + squares)

    return call(body, (y_far, to_near, got_near), jax.ShapeDtypeStruct(got_near.shape, BF16))


def add_second(groups, gs, rows, weight, got_near, after):
    def body(w_ref, got_ref, *refs):
        y = sum(
            projected(which, lanes, 1, rows, w_ref, g_ref[...]) for (which, lanes), g_ref in zip(groups, refs)
        )
        refs[-1][...] = (y + got_ref[...].astype(F32)).astype(BF16)

    out = jax.ShapeDtypeStruct(got_near.shape, BF16)
    return call(body, (weight, got_near, *gs), out, after=after)


def finish(rows, y_own, inputs, out=None, features=None):
    size, toks = y_own.shape
    parts = 2
    step = (rows.stop - rows.start) // parts
    first = out is None

    def body(own_ref, far_ref, factor_ref, *refs):
        out_hbm, *more, out_ref, sems = refs if first else refs[1:]
        if first:
            inv = lax.rsqrt((split_squares(factor_ref)[1] + split_squares(far_ref)[1]) / features + EPS)
            more[0][...] = inv
        else:
            inv = factor_ref[...]
        copies = []
        for k in range(parts):
            here = slice(k * step, (k + 1) * step)
            there = slice(rows.start + here.start, rows.start + here.stop)
            out_ref[here] = ((own_ref[there] + far_ref[here].astype(F32)) * inv).astype(BF16)
            copies.append(pltpu.make_async_copy(out_ref.at[here], out_hbm.at[there], sems.at[k]))
            copies[-1].start()
        for copy in copies:
            copy.wait()

    vm, where = pl.BlockSpec(memory_space=pltpu.VMEM), pl.BlockSpec(memory_space=pl.ANY)
    result = jax.ShapeDtypeStruct((size, toks), BF16)
    return pl.pallas_call(
        body,
        in_specs=[vm] * 3 + ([] if first else [where]),
        out_specs=[where, vm] if first else where,
        out_shape=[result, jax.ShapeDtypeStruct((1, toks), F32)] if first else result,
        scratch_shapes=[pltpu.VMEM((rows.stop - rows.start, toks), BF16), pltpu.SemaphoreType.DMA((parts,))],
        input_output_aliases={} if first else {3: 0},
        compiler_params=pltpu.CompilerParams(vmem_limit_bytes=VMEM),
        cost_estimate=CHEAP,
    )(y_own, *inputs, *(() if first else (out,)))


def on_device(
    n_seq, n_tp, head_input, gate_input, write_vecs, read_vecs, step_raw, segment_ids,
    decay_log, step_bias, skip_gain, norm_gain, out_weight,
):
    heads = decay_log.shape[0]
    toks, feats = head_input.shape
    width = feats // heads
    def swap(a, bit):
        return lax.ppermute(a, "seq", [(i, i ^ bit) for i in range(n_seq)])

    def across(a, bit):
        return lax.ppermute(a, "tp", [(i, i ^ bit) for i in range(n_tp)])

    other_one, stash = prepare(
        heads, width, step_raw, segment_ids.reshape(1, toks), decay_log.reshape(1, heads),
        step_bias.reshape(1, heads), head_input, write_vecs,
    )
    mate_one = swap(other_one, 1)
    other_two, keep_one, keep_two = more_states(width, stash, head_input, write_vecs)
    mate_two = swap(other_two, 1)
    *setup, seg = local_setup(
        heads, width, read_vecs, write_vecs, stash, skip_gain.reshape(1, heads), other_two
    )

    def local(which, tiles, after):
        return local_part(which, tiles, heads, width, head_input, gate_input, write_vecs, setup, after)

    tiles = feats // 2 // LANES
    edge = EARLY_LANES // LANES
    early = pair_step(keep_one, mate_one, seg)
    keep_a = local(0, range(0, tiles - edge), early[0])
    late = pair_step(keep_two, mate_two, keep_a[0])
    keep_b = local(0, range(tiles - edge, tiles), late[0])
    sent, totals, rows, firsts = zip(early, late)
    entries = [()] * 2
    bit, before = 2, keep_b[0]
    while 2 * bit < n_seq:
        more = 4 * bit < n_seq
        got = [swap(piece, bit) for piece in sent]
        early = level_step(bit, more, got[0], totals[0], rows[0], *entries[0], after=before)
        if bit == 2:
            other_a = local(1, range(0, edge), early[0])
        late = level_step(bit, more, got[1], totals[1], rows[1], *entries[1], after=other_a[0] if bit == 2 else early[0])
        sent, entries, rows, *totals = zip(early, late)
        totals, entries = totals[0] if more else (), [(entry,) for entry in entries]
        bit, before = bit * 2, None
    other_b = local(1, range(edge, tiles), sent[1])
    half_w = feats // 2
    quarter = out_weight.shape[1] // 4
    one, two = slice(0, EARLY_LANES), slice(EARLY_LANES, half_w)
    top, rest, every = slice(0, EARLY_ROWS), slice(EARLY_ROWS, quarter), slice(0, quarter)
    send_one, keep_one, prev = entry_step(
        bit, True, swap(sent[0], bit), *entries[0], rows[0], firsts[0], other_b[0]
    )
    other_one = swap(send_one, 1)
    send_two, keep_two = entry_step(bit, False, swap(sent[1], bit), *entries[1], rows[1], firsts[1], send_one)
    other_two = swap(send_two, 1)
    gain = norm_gain.reshape(1, feats)
    whole_half = slice(0, half_w)
    g_keep, squares, partial, linked = gated_sums(
        0, whole_half, (read_vecs, prev, seg), (keep_a[0], keep_b[0]), (keep_a[1], keep_b[1]), (keep_one, keep_two), gain, out_weight
    )
    g_one, squares, partial = gated_sums(
        1, one, (linked,), other_a[:1], other_a[1:], (other_one,), gain, out_weight, partial, squares
    )
    g_two, near_top = gated_last(two, top, linked, *other_b, other_two, gain, out_weight, partial, squares)
    got_top = across(near_top, 1)
    groups, gs = ((0, whole_half), (1, one), (1, two)), (g_keep, g_one, g_two)
    near_rest, far_top = project_next(groups, gs, top, rest, partial, out_weight, near_top)
    got_rest = across(near_rest, 1)
    to_far_top = add_first(far_top, near_top, got_top)
    got_far_top = across(to_far_top, 2)
    to_far_rest = add_second(groups, gs, rest, out_weight, got_rest, to_far_top)
    got_far_rest = across(to_far_rest, 2)
    y_near = project_whole(2, groups, gs, out_weight, NEAR_PIECES, after=to_far_rest)
    got_own = tuple(across(piece, 1) for piece in y_near)
    (y_own,) = project_whole(3, groups, gs, out_weight, 1, got_own)
    out, inv = finish(top, y_own, (got_far_top, to_far_top), features=feats * n_tp)
    return finish(rest, y_own, (got_far_rest, inv), out)


def solution(mesh):
    in_specs = (
        P("seq", "tp"),
        P("seq", "tp"),
        P("seq", None),
        P("seq", None),
        P("tp", "seq"),
        P("seq"),
        P("tp"),
        P("tp"),
        P("tp"),
        P("tp"),
        P("tp", None),
    )
    out_specs = P("tp", "seq")
    return jax.shard_map(
        functools.partial(on_device, mesh.shape["seq"], mesh.shape["tp"]),
        mesh=mesh, in_specs=in_specs, out_specs=out_specs, check_vma=False,
    )
```
